32 devices in a mesh: section: 2 (over x), seq: 4 (over z), mp: 4 (over y, core).
Axes of the slice: x: 2, y: 2, z: 4, core: 2. Of those that a mesh axis runs over, the one named last changes fastest.
Arguments:
- inputs: bfloat16 [6, 768, 2048], P(None, 'mp', 'seq'), may hold values from -6 to 6
- cotangent: bfloat16 [6, 768, 2048], P(None, 'mp', 'seq'), may hold values from -6 to 6
- labels: int32 [6, 2048], P(None, 'seq'), may hold values from 0 to 767
- scored: int32 [6, 2048], P(None, 'seq'), may hold values 0 or 1
- expand_weight: bfloat16 [2, 3072, 768], P('section', 'mp'), may hold values from -0.21875 to 0.21875
- expand_bias: float32 [2, 3072], P('section', 'mp'), may hold values from -3 to 3
- reduce_weight: bfloat16 [2, 768, 3072], P('section', None, 'mp'), may hold values from -0.1875 to 0.1875
- reduce_bias: float32 [2, 768], P('section', 'mp'), may hold values from -2 to 2
- first_gain: float32 [2, 768], P('section', 'mp'), may hold values from 0.5 to 1.5
- first_shift: float32 [2, 768], P('section', 'mp'), may hold values from -2 to 2
- second_gain: float32 [2, 768], P('section', 'mp'), may hold values from 0.5 to 1.5
- second_shift: float32 [2, 768], P('section', 'mp'), may hold values from -2 to 2
Outputs:
- outputs: float32 [2, 6, 768, 2048], P('section', None, 'mp', 'seq')
- input_grads: float32 [2, 6, 768, 2048], P('section', None, 'mp', 'seq')
- expand_weight_grad: float32 [2, 3072, 768], P('section', 'mp')
- expand_bias_grad: float32 [2, 3072], P('section', 'mp')
- reduce_weight_grad: float32 [2, 768, 3072], P('section', None, 'mp')
- reduce_bias_grad: float32 [2, 768], P('section', 'mp')
- first_gain_grad: float32 [2, 768], P('section', 'mp')
- first_shift_grad: float32 [2, 768], P('section', 'mp')
- second_gain_grad: float32 [2, 768], P('section', 'mp')
- second_shift_grad: float32 [2, 768], P('section', 'mp')
- accuracy: float32 [], replicated
The draws below stay inside these ranges and needn't reach their ends.
All inputs are finite; a program needn't handle non-finite values. No bound on the sum of `scored` on one device may be relied on, other than what follows from the above.
Results may differ from the reference program's by a relative error of at most 0.02.
Values may be sent and summed in bfloat16 or wider, within the bound.
No kernel may reach another device: no remote copies, remote signals or barrier semaphores. Data moves between devices by JAX's collectives and lax.ppermute only.
A program may use at most 256 MiB of HBM per device.

```python
import math
import jax
import jax.numpy as jnp
from jax import lax

D = 768
FF = 3072
MICRO = 6
LENGTH = 2048
LAYERS = 2


def touch_ends(drawn, key, smallest, top_value):
    dims = drawn.shape
    index_at = [jax.random.randint(jax.random.fold_in(key, axis), (), 0, dims[axis]) for axis in range(len(dims))]
    drawn = drawn.at[tuple(index_at)].set(smallest)
    longest = dims.index(max(dims))
    index_at[longest] = (index_at[longest] + 1) % dims[longest]
    return drawn.at[tuple(index_at)].set(top_value)


def levels(key, shape, cuts, smallest, top_value):
    factor_of = 1.0
    for dim, shards_of in cuts:
        draws = jax.random.uniform(jax.random.fold_in(jax.random.fold_in(key, 6), dim), (shards_of,), jnp.float32, smallest / len(cuts), top_value / len(cuts))
        factor_of = factor_of * jnp.repeat(jnp.exp(draws), shape[dim] // shards_of).reshape((-1,) + (1,) * (len(shape) - 1 - dim))
    return factor_of


def gaussian(own_key, dims, scale, reach, pieces=(), held_as=jnp.bfloat16):
    result = jax.random.normal(own_key, dims, jnp.float32) * scale
    if len(pieces) > 0:
        result = levels(own_key, dims, pieces, -0.22, 0.18) * result
    return jnp.clip(result, min=-reach, max=reach).astype(held_as)


def setup_inputs(seed: int = 0) -> dict:
    seeds = jax.random.split(jax.random.key(seed), 13)
    inputs = gaussian(seeds[0], (MICRO, D, LENGTH), 1.0, 6.0, ((1, 4), (2, 4)))
    cotangent = gaussian(seeds[1], (MICRO, D, LENGTH), 1.0, 6.0, ((1, 4), (2, 4)))
    labels = touch_ends(jax.random.randint(seeds[2], (MICRO, LENGTH), 0, D), jax.random.fold_in(seeds[2], 1), 0, D - 1).astype(jnp.int32)
    scored = touch_ends((jax.random.randint(seeds[3], (MICRO, LENGTH), 0, 100) < 15).astype(jnp.int32), jax.random.fold_in(seeds[3], 1), 0, 1)
    expand_weight = gaussian(seeds[4], (LAYERS, FF, D), D ** -0.5, 0.21875, ((0, 2), (1, 4)))
    expand_bias = gaussian(seeds[5], (LAYERS, FF), 0.5, 3.0, ((0, 2), (1, 4)), jnp.float32)
    reduce_weight = gaussian(seeds[6], (LAYERS, D, FF), (FF // 3) ** -0.5, 0.1875, ((0, 2), (2, 4)))
    reduce_bias = gaussian(seeds[7], (LAYERS, D), 0.3, 2.0, ((0, 2), (1, 4)), jnp.float32)
    first_gain = jnp.clip(1.0 + 0.1 * jax.random.normal(seeds[8], (LAYERS, D), jnp.float32), 0.5, 1.5)
    first_shift = gaussian(seeds[9], (LAYERS, D), 0.3, 2.0, ((0, 2), (1, 4)), jnp.float32)
    second_gain = jnp.clip(1.0 + 0.1 * jax.random.normal(seeds[10], (LAYERS, D), jnp.float32), 0.5, 1.5)
    second_shift = gaussian(seeds[11], (LAYERS, D), 0.3, 2.0, ((0, 2), (1, 4)), jnp.float32)
    return dict(inputs=inputs, cotangent=cotangent, labels=labels, scored=scored, expand_weight=expand_weight, expand_bias=expand_bias, reduce_weight=reduce_weight, reduce_bias=reduce_bias, first_gain=first_gain, first_shift=first_shift, second_gain=second_gain, second_shift=second_shift)


@jax.custom_vjp
def low(v):
    return lax.optimization_barrier(v.astype(jnp.bfloat16)).astype(jnp.float32)

@jax.custom_vjp
def low_back(v):
    return v

def low_keep(v):
    return (low(v), None)

def low_pass(kept, grad):
    return (grad,)

def back_keep(v):
    return (v, None)

def back_low(kept, grad):
    return (low(grad),)
low.defvjp(low_keep, low_pass)
low_back.defvjp(back_keep, back_low)
EPSILON = 1e-05

def matmul(left, right):
    return jnp.dot(left, right, precision=lax.Precision.HIGHEST, preferred_element_type=jnp.float32)

def trig_pair(points):
    indices = jnp.arange(points, dtype=jnp.int32)
    phases = indices[:, None] * indices[None, :] % points
    angles = phases.astype(jnp.float32) * (2.0 * math.pi / points)
    return (low(jnp.cos(angles)), low(jnp.sin(angles)))

def normalize(values, scaling, offsets):
    average = lax.optimization_barrier(jnp.mean(values, axis=0, keepdims=True))
    centered = values - average
    spread = lax.optimization_barrier(jnp.mean(centered * centered, axis=0, keepdims=True))
    return centered * lax.rsqrt(spread + EPSILON) * scaling[:, None] + offsets[:, None]

def mixing_layer(source, params, tables):
    expand_mat, expand_vec, reduce_mat, reduce_vec, gain_first, shift_first, gain_second, shift_second = params
    feature_cos, feature_sin, token_cos, token_sin = tables
    factor = 1.0 / math.sqrt(LENGTH * D)
    cos_mixed = low(low_back(matmul(feature_cos, source)))
    sin_mixed = low(low_back(matmul(feature_sin, source)))
    token_mixed = low_back((matmul(cos_mixed, token_cos) - matmul(sin_mixed, token_sin)) * factor)
    normed = normalize(source + token_mixed, gain_first, shift_first)
    hidden_pre = low_back(matmul(expand_mat, low(normed)) + expand_vec[:, None])
    active = low(jax.nn.gelu(hidden_pre, approximate=False))
    branch = low_back(matmul(reduce_mat, active))
    return normalize(normed + branch + reduce_vec[:, None], gain_second, shift_second)

def soft_hits(values, targets, chosen_mask):
    chances = jax.nn.softmax(values, axis=0)
    picked = jnp.take_along_axis(chances, targets[None, :].astype(jnp.int32), axis=0)[0]
    return jnp.sum(picked * chosen_mask.astype(jnp.float32))

def reference(inputs, cotangent, labels, scored, expand_weight, expand_bias, reduce_weight, reduce_bias, first_gain, first_shift, second_gain, second_shift):
    weights = (expand_weight.astype(jnp.float32), expand_bias.astype(jnp.float32), reduce_weight.astype(jnp.float32), reduce_bias.astype(jnp.float32), first_gain.astype(jnp.float32), first_shift.astype(jnp.float32), second_gain.astype(jnp.float32), second_shift.astype(jnp.float32))
    first_params = tuple((member[0] for member in weights))
    second_params = tuple((member[1] for member in weights))
    tables = trig_pair(D) + trig_pair(LENGTH)

    def both_layers(params_first, params_second, source, nudging):
        first = mixing_layer(source, params_first, tables)
        passed = low_back(low(first)) + nudging
        second = mixing_layer(passed, params_second, tables)
        return (first, second)

    def adder(running, update):
        return running + update

    def one_sequence(totals, member):
        source, seed_grad, targets, chosen_mask = member
        source = source.astype(jnp.float32)
        (first, second), pullback = jax.vjp(both_layers, first_params, second_params, source, jnp.zeros_like(source))
        first_grads, second_grads, grad_source, grad_nudge = pullback((jnp.zeros_like(first), seed_grad.astype(jnp.float32)))
        totals = jax.tree.map(adder, totals, (first_grads, second_grads))
        hit_count = soft_hits(first, targets, chosen_mask) + soft_hits(second, targets, chosen_mask)
        return (totals, (first, second, grad_source, grad_nudge, hit_count))
    initial = jax.tree.map(jnp.zeros_like, (first_params, second_params))
    totals, (firsts, seconds, grad_sources, grad_nudges, hit_counts) = lax.scan(one_sequence, initial, (inputs, cotangent, labels, scored))
    first_grads, second_grads = totals
    stacked = [jnp.stack([first_grads[index], second_grads[index]]) for index in range(8)]
    return (jnp.stack([firsts, seconds]), jnp.stack([grad_sources, grad_nudges]), stacked[0], stacked[1], stacked[2], stacked[3], stacked[4], stacked[5], stacked[6], stacked[7], jnp.sum(hit_counts))
```

```python
import math

import jax
import jax.numpy as jnp
import ml_dtypes
import numpy as np
from jax import lax
from jax.experimental import pallas as pl
from jax.experimental.pallas import tpu as pltpu
from jax.sharding import PartitionSpec as P

EPSILON = 1e-05
BF = jnp.bfloat16
F32 = jnp.float32
MIB = 1 << 20


def trig(rows, columns, points):
    phases = (rows.astype(np.int64)[:, None] * columns.astype(np.int64)[None, :]) % points
    angles = phases.astype(np.float64) * (2.0 * math.pi / points)
    return np.cos(angles), np.sin(angles)


def low_table(table):
    return table.astype(np.float32).astype(ml_dtypes.bfloat16)


def feature_tables(width, group):
    pairs = width // group // 2
    ids = np.arange(width // 2)
    cos, sin = trig(ids, np.arange(width), width)
    sin[0] = trig(np.array([width // 2]), np.arange(width), width)[0][0]
    packed = np.stack([cos.reshape(group, pairs, width), sin.reshape(group, pairs, width)], 1)
    unpack = np.zeros((width, width), np.float32)
    for k in range(width // 2):
        place = (k // pairs) * 2 * pairs + k % pairs
        if k == 0:
            unpack[0, place] = 1.0
            unpack[width // 2, place + pairs] = 1.0
        else:
            unpack[k, place] = 1.0
            unpack[k, place + pairs] = -1.0
            unpack[width - k, place] = 1.0
            unpack[width - k, place + pairs] = 1.0
    return low_table(packed.reshape(width, width)), low_table(unpack)


def params(limit=24):
    return pltpu.CompilerParams(vmem_limit_bytes=limit * MIB)


def mm(left, right):
    return jnp.dot(left, right, preferred_element_type=F32)


def mm_nt(left, right):
    return lax.dot_general(left, right, (((1,), (1,)), ((), ())), preferred_element_type=F32)


def token_kernel(count, tokens, d_ref, m_ref, c_ref, s_ref, o_ref, x_ref):
    group, rows = d_ref.shape[0], d_ref.shape[1]

    @pl.when(pl.program_id(0) == 0)
    def _():
        for m in range(count):
            for g in range(group):
                x_ref[m * rows : (m + 1) * rows, g * tokens : (g + 1) * tokens] = d_ref[
                    g, :, m * tokens : (m + 1) * tokens
                ]

    values = x_ref[...]
    mixed = jnp.where(m_ref[...] > 0.0, mm(values, c_ref[...]), mm(values, s_ref[...])).astype(BF)
    for g in range(o_ref.shape[0]):
        for m in range(count):
            o_ref[g, :, m * tokens : (m + 1) * tokens] = mixed[
                m * rows : (m + 1) * rows, g * tokens : (g + 1) * tokens
            ]


def token_transform(data, mask, cos, sin, count):
    group, rows, columns = data.shape
    length = cos.shape[0]
    tokens = columns // count
    dests = max(1, min(group, 512 // tokens))
    block = dests * tokens
    whole = lambda i: (0, 0)
    return pl.pallas_call(
        lambda *refs: token_kernel(count, tokens, *refs),
        grid=(length // block,),
        in_specs=[
            pl.BlockSpec(data.shape, lambda i: (0, 0, 0)),
            pl.BlockSpec(mask.shape, whole),
            pl.BlockSpec((length, block), lambda i: (0, i)),
            pl.BlockSpec((length, block), lambda i: (0, i)),
        ],
        out_specs=pl.BlockSpec((dests, rows, columns), lambda i: (i, 0, 0)),
        out_shape=jax.ShapeDtypeStruct(data.shape, BF),
        scratch_shapes=[pltpu.VMEM((count * rows, length), BF)],
        compiler_params=params(40),
        cost_estimate=pl.CostEstimate(
            flops=4 * count * rows * length * length,
            bytes_accessed=4 * length * length,
            transcendentals=0,
        ),
    )(data, mask, cos, sin)


def gelu_parts(x):
    e = jnp.exp(-0.5 * x * x)
    t = 1.0 / (1.0 + (0.3275911 / math.sqrt(2.0)) * jnp.abs(x))
    poly = t * (
        0.5 * 0.254829592
        + t
        * (
            0.5 * -0.284496736
            + t * (0.5 * 1.421413741 + t * (0.5 * -1.453152027 + t * (0.5 * 1.061405429)))
        )
    )
    tail = poly * e
    return jnp.where(x >= 0.0, 1.0 - tail, tail), e * (1.0 / math.sqrt(2.0 * math.pi))


def blocks(size, step):
    step = step if size % step == 0 else size
    return [(i, step) for i in range(0, size, step)]


def ffn_kernel(a_ref, b_ref, w1_ref, bias_ref, w2_ref, oa_ref, ob_ref, act_ref, slope_ref):
    columns = a_ref.shape[1]
    x = jnp.concatenate([a_ref[...], b_ref[...]], axis=1)
    for start, size in blocks(w1_ref.shape[0], 256):
        hidden = mm(w1_ref[start : start + size], x) + bias_ref[start : start + size]
        cdf, density = gelu_parts(hidden)
        act_ref[start : start + size] = (hidden * cdf).astype(BF)
        slope_ref[start : start + size] = (cdf + hidden * density).astype(BF)
    for start, size in blocks(w2_ref.shape[0], 256):
        part = mm(w2_ref[start : start + size], act_ref[...]).astype(BF)
        oa_ref[start : start + size] = part[:, :columns]
        ob_ref[start : start + size] = part[:, columns:]


def ffn(first, second, w1, bias, w2):
    width, columns = first.shape
    units = w1.shape[0]
    half = jax.ShapeDtypeStruct((width, columns), BF)
    full = jax.ShapeDtypeStruct((units, 2 * columns), BF)
    return pl.pallas_call(
        ffn_kernel,
        out_shape=(half, half, full, full),
        compiler_params=params(32),
        cost_estimate=pl.CostEstimate(
            flops=8 * width * units * columns, bytes_accessed=8 << 20, transcendentals=0
        ),
    )(first, second, w1, bias, w2)


def ffn_back_kernel(a_ref, b_ref, w2t_ref, slope_ref, w1t_ref, oa_ref, ob_ref, gp_ref, gb_ref):
    columns = a_ref.shape[1]
    g = jnp.concatenate([a_ref[...], b_ref[...]], axis=1)
    for start, size in blocks(w2t_ref.shape[0], 256):
        grad = mm(w2t_ref[start : start + size], g) * slope_ref[start : start + size].astype(F32)
        low = grad.astype(BF)
        gp_ref[start : start + size] = low
        gb_ref[start : start + size] = jnp.sum(low.astype(F32), axis=1, keepdims=True)
    for start, size in blocks(w1t_ref.shape[0], 256):
        part = mm(w1t_ref[start : start + size], gp_ref[...]).astype(BF)
        oa_ref[start : start + size] = part[:, :columns]
        ob_ref[start : start + size] = part[:, columns:]


def ffn_back(first, second, w2t, slope, w1t):
    width, columns = first.shape
    units = w2t.shape[0]
    half = jax.ShapeDtypeStruct((width, columns), BF)
    return pl.pallas_call(
        ffn_back_kernel,
        out_shape=(
            half,
            half,
            jax.ShapeDtypeStruct((units, 2 * columns), BF),
            jax.ShapeDtypeStruct((units, 1), F32),
        ),
        compiler_params=params(32),
        cost_estimate=pl.CostEstimate(
            flops=8 * width * units * columns, bytes_accessed=8 << 20, transcendentals=0
        ),
    )(first, second, w2t, slope, w1t)


def weight_kernel(count, *refs):
    x_refs, pre_refs = refs[: 2 * count], refs[2 * count : 3 * count]
    g_refs, act_refs = refs[3 * count : 5 * count], refs[5 * count : 6 * count]
    one_ref, two_ref = refs[-2:]

    def joined(pieces):
        return jnp.concatenate([piece[...] for piece in pieces], axis=1)

    g, act = joined(g_refs), joined(act_refs)
    for start, size in blocks(g.shape[0], 256):
        two_ref[start : start + size] = mm_nt(g[start : start + size], act).astype(BF)
    pre, x = joined(pre_refs), joined(x_refs)
    for start, size in blocks(pre.shape[0], 256):
        one_ref[start : start + size] = mm_nt(pre[start : start + size], x).astype(BF)


def weight_grads(xs, pres, gs, acts):
    units, width = pres[0].shape[0], xs[0].shape[0]
    tokens = sum(p.shape[1] for p in pres)
    return pl.pallas_call(
        lambda *refs: weight_kernel(len(pres), *refs),
        out_shape=(
            jax.ShapeDtypeStruct((units, width), BF),
            jax.ShapeDtypeStruct((width, units), BF),
        ),
        compiler_params=params(40),
        cost_estimate=pl.CostEstimate(
            flops=4 * width * units * tokens, bytes_accessed=8 << 20, transcendentals=0
        ),
    )(*xs, *pres, *gs, *acts)


def pencil_kernel(count, tokens, section_ref, x_ref, o_ref):
    for d in range(o_ref.shape[0]):
        for m in range(count):
            o_ref[d, :, m * tokens : (m + 1) * tokens] = x_ref[
                0, m, :, d * tokens : (d + 1) * tokens
            ]


def pencil_parts(local, section, sections, mps):
    batches, features, token_count = local.shape
    count, tokens = batches // sections, token_count // mps
    local = local.reshape(sections, count, features, token_count)
    out = jax.ShapeDtypeStruct((mps, features, count * tokens), local.dtype)
    return pl.pallas_call(
        lambda *refs: pencil_kernel(count, tokens, *refs),
        grid_spec=pltpu.PrefetchScalarGridSpec(
            num_scalar_prefetch=1,
            grid=(1,),
            in_specs=[
                pl.BlockSpec((1, count, features, token_count), lambda i, s: (s[0], 0, 0, 0))
            ],
            out_specs=pl.BlockSpec(out.shape, lambda i, s: (0, 0, 0)),
        ),
        out_shape=out,
        compiler_params=params(16),
    )(section.reshape(1), local)


def block_kernel(count, tokens, x_ref, o_ref):
    for d in range(x_ref.shape[1]):
        for m in range(count):
            o_ref[0, m, :, d * tokens : (d + 1) * tokens] = x_ref[
                0, d, :, m * tokens : (m + 1) * tokens
            ].astype(F32)


def block_parts(got, sections, count):
    parts, features, columns = got.shape
    mps, tokens = parts // sections, columns // count
    got = got.reshape(sections, mps, features, columns)
    out = jax.ShapeDtypeStruct((sections, count, features, mps * tokens), F32)
    whole = lambda i: (i, 0, 0, 0)
    return pl.pallas_call(
        lambda *refs: block_kernel(count, tokens, *refs),
        grid=(sections,),
        in_specs=[pl.BlockSpec((1, mps, features, columns), whole)],
        out_specs=pl.BlockSpec((1,) + out.shape[1:], whole),
        out_shape=out,
        compiler_params=params(16),
    )(got).reshape(1, sections * count, features, mps * tokens)


def norm_forward(values, scaling, offsets):
    average = jnp.mean(values, axis=0, keepdims=True)
    centered = values - average
    spread = jnp.mean(centered * centered, axis=0, keepdims=True)
    inverse = lax.rsqrt(spread + EPSILON)
    standard = centered * inverse
    return standard * scaling + offsets, standard, inverse


def norm_backward(upstream, standard, inverse, scaling):
    weighted = upstream * scaling
    grad = inverse * (
        weighted
        - jnp.mean(weighted, axis=0, keepdims=True)
        - standard * jnp.mean(weighted * standard, axis=0, keepdims=True)
    )
    return grad, jnp.sum(upstream * standard, axis=1), jnp.sum(upstream, axis=1)


def shards(
    inputs,
    cotangent,
    labels,
    scored,
    expand_weight,
    expand_bias,
    reduce_weight,
    reduce_bias,
    first_gain,
    first_shift,
    second_gain,
    second_shift,
):
    batches, feature_count, token_count = inputs.shape
    sections, seqs, mps = (lax.axis_size(axis) for axis in ("section", "seq", "mp"))
    group = seqs * mps
    width = feature_count * mps
    length = token_count * seqs
    units = expand_weight.shape[1]
    count = batches // sections
    tokens = token_count // mps
    columns = count * tokens
    factor = 1.0 / math.sqrt(length * width)
    section = lax.axis_index("section")
    seq_index = lax.axis_index("seq")
    mp_index = lax.axis_index("mp")
    is_first = section == 0
    ring = (("seq", "mp"),)[0]

    packed_np, unpack_np = feature_tables(width, group)
    packed, unpack = jnp.asarray(packed_np), jnp.asarray(unpack_np)
    ids = np.arange(length)
    cos_np, sin_np = trig(ids, ids, length)
    token_cos, token_sin = jnp.asarray(low_table(cos_np)), jnp.asarray(low_table(sin_np))
    rows = width // group
    row_ids = jnp.arange(count * rows, dtype=jnp.int32) % rows
    device = seq_index * mps + mp_index
    mask = (row_ids < rows // 2) | ((row_ids == rows // 2) & (device == 0))
    mask = mask.astype(F32)[:, None]

    swap = [(i, (i + 1) % sections) for i in range(sections)]
    own_one, own_two = expand_weight[0], reduce_weight[0]
    other_one = lax.ppermute(own_one, "section", swap)
    other_two = lax.ppermute(own_two, "section", swap)
    w1 = [jnp.where(is_first, own_one, other_one), jnp.where(is_first, other_one, own_one)]
    w2 = [jnp.where(is_first, own_two, other_two), jnp.where(is_first, other_two, own_two)]
    core_swap = [(i, i ^ 1) for i in range(mps)]
    sides = mps // 2

    def side_shift(array, by):
        pairs = [(i, (i // 2 + by) % sides * 2 + i % 2) for i in range(mps)]
        return lax.ppermute(array, "mp", pairs)

    small = jnp.concatenate(
        [
            expand_bias[0],
            reduce_bias[0],
            first_gain[0],
            first_shift[0],
            second_gain[0],
            second_shift[0],
        ]
    )
    other = lax.ppermute(small, "section", swap)
    small = jnp.where(is_first, jnp.stack([small, other]), jnp.stack([other, small]))
    biases, vectors = small[:, :units], small[:, units:].reshape(sections, 5, 1, feature_count)
    sibling = lax.ppermute(vectors, "mp", core_swap)
    core = mp_index % 2
    chip = jnp.concatenate(
        [jnp.where(core == 0, vectors, sibling), jnp.where(core == 0, sibling, vectors)], axis=2
    )
    chips = jnp.stack([side_shift(chip, -j) if j else chip for j in range(sides)], axis=2)
    order = [(i - mp_index // 2) % sides for i in range(sides)]
    vectors = jnp.stack(
        [lax.dynamic_index_in_dim(chips, i, 2, keepdims=False) for i in order], axis=2
    ).reshape(sections, 5, width, 1)

    def to_pencils(local):
        own = pencil_parts(local, section, sections, mps)
        return lax.all_to_all(own, "mp", 0, 0, tiled=True).reshape(width, columns)

    def to_blocks(layers):
        sent = jnp.stack(layers).reshape(sections * mps, feature_count, columns)
        got = lax.all_to_all(sent, ("section", "mp"), 0, 0, tiled=True)
        return block_parts(got, sections, count)

    def fourier(low):
        sent = mm(packed, low).astype(BF).reshape(group, rows, columns)
        got = lax.all_to_all(sent, ring, 0, 0, tiled=True)
        mixed = token_transform(got, mask, token_cos, token_sin, count)
        got = lax.all_to_all(mixed, ring, 0, 0, tiled=True).reshape(width, columns)
        return mm(unpack, got) * factor

    def gathered(own):
        firsts = [own] + [side_shift(own, j) for j in range(1, sides)]
        return [(first, lax.ppermute(first, "mp", core_swap)) for first in firsts]

    def reduced(parts):
        total = None
        for j in reversed(range(sides)):
            keep, give = parts[j]
            chip = keep.astype(F32) + lax.ppermute(give, "mp", core_swap).astype(F32)
            if j > 0:
                chip = side_shift(chip.astype(BF), -j).astype(F32)
            total = chip if total is None else total + chip
        return total

    def counts(out, local_labels, local_scored):
        exponent = jnp.exp(out)
        matches = jnp.arange(width, dtype=jnp.int32)[:, None] == local_labels[None, :]
        label_exp = jnp.sum(jnp.where(matches, exponent, 0.0), axis=0)
        return jnp.sum(label_exp / jnp.sum(exponent, axis=0) * local_scored)

    def own_tokens(ints):
        own = lax.dynamic_slice(ints, (section * count, mp_index * tokens), (count, tokens))
        return own.reshape(columns)

    local_labels, local_scored = own_tokens(labels), own_tokens(scored).astype(F32)

    low = to_pencils(inputs)
    saved, outs, hits = [], [], jnp.zeros((), F32)
    for layer in range(2):
        reduce_vec, gain1, shift1, gain2, shift2 = (vectors[layer, i] for i in range(5))
        bias = biases[layer][:, None]
        normed, unit1, inv1 = norm_forward(low.astype(F32) + fourier(low), gain1, shift1)
        xs = gathered(normed.astype(BF))
        runs = [ffn(a, b, w1[layer], bias, w2[layer]) for a, b in xs]
        branch = reduced([run[:2] for run in runs])
        out, unit2, inv2 = norm_forward(normed + branch + reduce_vec, gain2, shift2)
        low = out.astype(BF)
        outs.append(low)
        hits = hits + counts(out, local_labels, local_scored)
        saved.append((unit1, inv1, xs, runs, unit2, inv2))
    outputs = to_blocks(outs)

    up = to_pencils(cotangent)
    grads_in, weights_out, smalls = [None, None], [None, None], []
    for layer in (1, 0):
        _, gain1, _, gain2, _ = (vectors[layer, i] for i in range(5))
        unit1, inv1, xs, runs, unit2, inv2 = saved[layer]
        grad_second, gain2_grad, shift2_grad = norm_backward(up.astype(F32), unit2, inv2, gain2)
        gs = gathered(grad_second.astype(BF))
        w2t, w1t = w2[layer].T, w1[layer].T
        backs = [ffn_back(a, b, w2t, run[3], w1t) for (a, b), run in zip(gs, runs)]
        branch = reduced([back[:2] for back in backs])
        weights_out[layer] = weight_grads(
            [x for pair in xs for x in pair],
            [back[2] for back in backs],
            [g for pair in gs for g in pair],
            [run[2] for run in runs],
        )
        branch, weights_out[layer] = lax.optimization_barrier((branch, weights_out[layer]))
        grad_normed = grad_second + branch
        bias_grad = sum(back[3] for back in backs)[:, 0]
        grad_first, gain1_grad, shift1_grad = norm_backward(grad_normed, unit1, inv1, gain1)
        grad_source = grad_first + fourier(grad_first.astype(BF))
        up = grad_source.astype(BF)
        grads_in[layer] = up
        smalls = [
            (bias_grad, jnp.sum(grad_second, axis=1), gain1_grad, shift1_grad, gain2_grad, shift2_grad)
        ] + smalls
    input_grads = to_blocks(grads_in)

    def scattered(layer):
        return [
            lax.psum_scatter(w, "seq", scatter_dimension=0, tiled=True) for w in weights_out[layer]
        ]

    late, early = scattered(1), scattered(0)
    weight_sums = []
    for first, second in zip(early, late):
        got = lax.ppermute(jnp.where(is_first, second, first), "section", swap)
        total = (jnp.where(is_first, first, second).astype(F32) + got.astype(F32)).astype(BF)
        weight_sums.append(lax.all_gather(total, "seq", axis=0, tiled=True).astype(F32))

    def summed(array, axis):
        size, step = lax.axis_size(axis), 1
        while step < size:
            array = array + lax.ppermute(array, axis, [(i, i ^ step) for i in range(size)])
            step *= 2
        return array

    def padded(flat):
        return jnp.pad(flat, (0, -flat.shape[0] % 1024)).reshape(-1, 128)

    per = 5 * width
    flat = [v for layer in smalls for v in layer[1:]] + [hits[None]]
    flat = summed(padded(jnp.concatenate(flat)), "mp")
    bias_rows = padded(jnp.concatenate([layer[0] for layer in smalls]))
    flat = jnp.concatenate([flat, bias_rows])
    flat = summed(summed(flat, "seq"), "section")
    bias_sum = flat[-bias_rows.shape[0] :].reshape(-1)[: 2 * units].reshape(2, units)
    bias_sum = lax.dynamic_index_in_dim(bias_sum, section, 0, keepdims=False)
    flat = flat[: -bias_rows.shape[0]].reshape(-1)
    accuracy = flat[2 * per]
    features = flat[: 2 * per].reshape(2, 5, mps, feature_count)
    features = lax.dynamic_index_in_dim(features, section, 0, keepdims=False)
    features = lax.dynamic_index_in_dim(features, mp_index, 1, keepdims=False)

    return (
        outputs,
        input_grads,
        weight_sums[0][None],
        bias_sum[None],
        weight_sums[1][None],
        features[0][None],
        features[1][None],
        features[2][None],
        features[3][None],
        features[4][None],
        accuracy,
    )


def solution(mesh):
    placed = (
        P(None, "mp", "seq"),
        P(None, "mp", "seq"),
        P(None, "seq"),
        P(None, "seq"),
        P("section", "mp", None),
        P("section", "mp"),
        P("section", None, "mp"),
        P("section", "mp"),
        P("section", "mp"),
        P("section", "mp"),
        P("section", "mp"),
        P("section", "mp"),
    )
    return jax.shard_map(
        shards,
        mesh=mesh,
        in_specs=placed,
        out_specs=(
            P("section", None, "mp", "seq"),
            P("section", None, "mp", "seq"),
            P("section", "mp", None),
            P("section", "mp"),
            P("section", None, "mp"),
            P("section", "mp"),
            P("section", "mp"),
            P("section", "mp"),
            P("section", "mp"),
            P("section", "mp"),
            P(),
        ),
        check_vma=False,
    )
```

```python
import math

import jax
import jax.numpy as jnp
import ml_dtypes
import numpy as np
from jax import lax
from jax.experimental import pallas as pl
from jax.experimental.pallas import tpu as pltpu
from jax.sharding import Mesh
from jax.sharding import PartitionSpec as P

EPSILON = 1e-05
BF = jnp.bfloat16
F32 = jnp.float32
MIB = 1 << 20
AXES = ("section", "half", "rest", "side", "core")
RING = ("section", "rest", "side", "core")
PLANE = ("half", "side", "core")
SQUARE = ("section", "half", "side", "core")
VMEM = pl.BlockSpec(memory_space=pltpu.VMEM)
HBM = pl.BlockSpec(memory_space=pltpu.HBM)
SMEM = pl.BlockSpec(memory_space=pltpu.SMEM)


def trig(rows, columns, points):
    phases = (rows.astype(np.int64)[:, None] * columns.astype(np.int64)[None, :]) % points
    angles = phases.astype(np.float64) * (2.0 * math.pi / points)
    return np.cos(angles), np.sin(angles)


def low_table(table):
    return table.astype(np.float32).astype(ml_dtypes.bfloat16)


def feature_tables(width, group):
    pairs = width // group // 2
    ids = np.arange(width // 2)
    cos, sin = trig(ids, np.arange(width), width)
    sin[0] = trig(np.array([width // 2]), np.arange(width), width)[0][0]
    packed = np.stack([cos.reshape(group, pairs, width), sin.reshape(group, pairs, width)], 1)
    unpack = np.zeros((width, width), np.float32)
    for k in range(width // 2):
        place = (k // pairs) * 2 * pairs + k % pairs
        if k == 0:
            unpack[0, place] = 1.0
            unpack[width // 2, place + pairs] = 1.0
        else:
            unpack[k, place] = 1.0
            unpack[k, place + pairs] = -1.0
            unpack[width - k, place] = 1.0
            unpack[width - k, place + pairs] = 1.0
    return low_table(packed.reshape(width, width)), low_table(unpack)


def token_tables(sections, rests, mps, part):
    parity, rest, place, i = np.meshgrid(
        np.arange(sections), np.arange(rests), np.arange(mps), np.arange(part), indexing="ij"
    )
    first = rest * sections * mps * part + sections * (place * part + i) + parity
    length = 2 * first.size
    every = np.stack([first, first + length // 2], 3).reshape(-1)
    cos, sin = trig(every, first.reshape(-1), length)
    return low_table(cos), low_table(sin)


def sorting_table(sections, count):
    table = np.zeros((count, count), np.float32)
    order = np.arange(count).reshape(-1, sections).T.reshape(-1)
    table[order, np.arange(count)] = 1.0
    return low_table(table)


def mm(left, right):
    return jnp.dot(left, right, preferred_element_type=F32)


def mm_nt(left, right):
    return lax.dot_general(left, right, (((1,), (1,)), ((), ())), preferred_element_type=F32)


def blocks(size, step):
    step = step if size % step == 0 else size
    return [(i, i + step) for i in range(0, size, step)]


def shape(dims, dtype=BF):
    return jax.ShapeDtypeStruct(tuple(dims), dtype)


def call(kernel, outs, args, specs=None, scratch=(), limit=57, flops=0, **extra):
    return pl.pallas_call(
        kernel,
        out_shape=outs,
        in_specs=specs or [VMEM] * len(args),
        scratch_shapes=list(scratch),
        compiler_params=pltpu.CompilerParams(vmem_limit_bytes=limit * MIB),
        cost_estimate=pl.CostEstimate(flops=flops, bytes_accessed=6 << 20, transcendentals=0),
        **extra,
    )(*args)


def paired(first, second):
    left = lax.broadcasted_iota(jnp.int32, first.shape, 1) < 64
    return (
        jnp.where(left, first, pltpu.roll(second, 64, axis=1)),
        jnp.where(left, pltpu.roll(first, 64, axis=1), second),
    )


def send_pencils(local, section, sections, halves, mps, sorting):
    batches, features, tokens = local.shape
    count, part, rows = batches // halves, tokens // sections // mps, features // 2
    out = shape((halves * mps, count * rows, 2 * part), local.dtype)
    if part != 64 or mps % 2:
        own = local.reshape(halves, count, 2, rows, mps, part, sections)
        own = lax.dynamic_index_in_dim(own, section, 6, keepdims=False)
        return own.transpose(0, 4, 1, 3, 2, 5).reshape(out.shape)
    sorting = sorting.reshape(tokens, sections, tokens // sections).transpose(1, 0, 2)

    def kernel(section_ref, x_ref, sorting_ref, o_ref):
        for seq in range(batches):
            half, m = seq // count, seq % count
            values = mm(x_ref[seq], sorting_ref[0])
            for place in range(0, mps, 2):
                a = place * part
                pair = paired(values[:rows, a : a + 128], values[rows:, a : a + 128])
                for k in range(2):
                    d = half * mps + place + k
                    o_ref[d, m * rows : (m + 1) * rows] = pair[k].astype(BF)

    return pl.pallas_call(
        kernel,
        grid_spec=pltpu.PrefetchScalarGridSpec(
            num_scalar_prefetch=1,
            grid=(1,),
            in_specs=[
                pl.BlockSpec(local.shape, lambda i, s: (0, 0, 0)),
                pl.BlockSpec((1,) + sorting.shape[1:], lambda i, s: (s[0], 0, 0)),
            ],
            out_specs=pl.BlockSpec(out.shape, lambda i, s: (0, 0, 0)),
        ),
        out_shape=out,
        compiler_params=pltpu.CompilerParams(vmem_limit_bytes=57 * MIB),
    )(section.reshape(1), local, sorting)


def take_pencils(got, halves, mps, count, packed=None):
    rows, part = got.shape[1] // count, got.shape[2] // 2
    width, columns = mps * 2 * rows, count * halves * part
    if part != 64:
        got = got.reshape(halves, mps, count, rows, 2, part)
        low = got.transpose(1, 4, 3, 2, 0, 5).reshape(width, columns)
        return low, None if packed is None else mm(packed, low).astype(BF)

    def kernel(*refs):
        x_ref, o_ref = refs[0], refs[1 if packed is None else 2]
        for mp in range(mps):
            for m in range(count):
                pair = paired(
                    *(x_ref[h * mps + mp, m * rows : (m + 1) * rows].astype(F32) for h in range(2))
                )
                for k in range(2):
                    a = (mp * 2 + k) * rows
                    o_ref[a : a + rows, m * 128 : (m + 1) * 128] = pair[k].astype(BF)
        if packed is not None:
            refs[3][...] = mm(refs[1][...], o_ref[...]).astype(BF)

    low = shape((width, columns))
    if packed is None:
        return call(kernel, low, (got,)), None
    return call(kernel, (low, low), (got, packed))


def send_blocks(layers, extra, sections, halves, mps, count, part):
    width, columns = layers[0].shape
    rows = width // mps // 2
    more = extra.shape[1]
    out = shape((sections * halves * mps, count * rows + more, 2 * part))
    if part != 64:
        sent = jnp.stack(layers).reshape(sections, mps, 2, rows, count, halves, part)
        sent = sent.transpose(0, 5, 1, 4, 3, 2, 6).reshape(-1, count * rows, 2 * part)
        return jnp.concatenate([sent, extra], axis=1)

    def kernel(*refs):
        o_ref = refs[-1]
        o_ref[:, count * rows :] = refs[sections][...]
        for layer in range(sections):
            for mp in range(mps):
                for m in range(count):
                    a, b = mp * 2 * rows, m * 128
                    pair = paired(
                        refs[layer][a : a + rows, b : b + 128].astype(F32),
                        refs[layer][a + rows : a + 2 * rows, b : b + 128].astype(F32),
                    )
                    for k in range(2):
                        d = (layer * halves + k) * mps + mp
                        o_ref[d, m * rows : (m + 1) * rows] = pair[k].astype(BF)

    return call(kernel, out, (*layers, extra))


def take_blocks(got, rows, sections, halves, mps, count, unsorting):
    part = got.shape[2] // 2
    out = (1, halves * count, 2 * rows, sections * mps * part)
    if part != 64 or mps % 2:
        got = got[:, : count * rows].reshape(sections, halves, mps, count, rows, 2, part)
        return got.transpose(1, 3, 5, 4, 2, 6, 0).reshape(out).astype(F32)
    got = got.reshape(sections, halves, mps, got.shape[1], 128)

    def kernel(x_ref, table_ref, o_ref, s_ref):
        for x in range(sections):
            for place in range(0, mps, 2):
                a = x * mps * part + place * part
                for m in range(count):
                    pair = paired(
                        *(
                            x_ref[x, 0, place + k, m * rows : (m + 1) * rows].astype(F32)
                            for k in range(2)
                        )
                    )
                    for k in range(2):
                        s_ref[(2 * m + k) * rows : (2 * m + k + 1) * rows, a : a + 128] = pair[
                            k
                        ].astype(BF)
        for m in range(count):
            o_ref[0, m] = mm(s_ref[2 * m * rows : 2 * (m + 1) * rows], table_ref[...])

    return pl.pallas_call(
        kernel,
        grid=(halves,),
        in_specs=[
            pl.BlockSpec((sections, 1, mps, got.shape[3], 128), lambda i: (0, i, 0, 0, 0)),
            pl.BlockSpec(unsorting.shape, lambda i: (0, 0)),
        ],
        out_specs=pl.BlockSpec((1, count) + out[2:], lambda i: (i, 0, 0, 0)),
        out_shape=shape((halves, count) + out[2:], F32),
        scratch_shapes=[pltpu.VMEM((count * 2 * rows, out[3]), BF)],
        compiler_params=pltpu.CompilerParams(vmem_limit_bytes=57 * MIB),
    )(got, unsorting).reshape(out)


def token_transform(data, mask, cos, sin, count):
    group, rows, columns = data.shape
    length, spread = cos.shape
    tokens = columns // count
    part = tokens // 2
    if part != 64:
        x = data.reshape(group, rows, count, tokens).transpose(2, 1, 0, 3)
        x = x.reshape(count * rows, length)
        mixed = [
            jnp.where(mask > 0.0, mm(x[:, a:b], cos[a:b]), mm(x[:, a:b], sin[a:b]))
            for a, b in ((0, spread), (spread, length))
        ]
        both = jnp.stack([mixed[0] + mixed[1], mixed[0] - mixed[1]]).astype(BF)
        both = both.reshape(2, count, rows, group, part).transpose(3, 2, 1, 0, 4)
        return both.reshape(data.shape)
    step = 256

    def kernel(d_ref, m_ref, c_hbm, s_hbm, o_ref, x_ref, c_ref, s_ref, sems):
        copies = []
        for n in range(spread // step):
            window = slice(n * step, (n + 1) * step)
            copies.append(
                [
                    pltpu.make_async_copy(src.at[:, window], dst.at[n], sems.at[n, k])
                    for k, (src, dst) in enumerate(((c_hbm, c_ref), (s_hbm, s_ref)))
                ]
            )
            for copy in copies[-1]:
                copy.start()
        for m in range(count):
            for g in range(group):
                x_ref[m * rows : (m + 1) * rows, g * tokens : (g + 1) * tokens] = d_ref[
                    g, :, m * tokens : (m + 1) * tokens
                ]
        keep = m_ref[...] > 0.0
        for n in range(spread // step):
            for copy in copies[n]:
                copy.wait()
            even, odd = (
                jnp.where(
                    keep,
                    mm(x_ref[:, a : a + spread], c_ref[n, a : a + spread]),
                    mm(x_ref[:, a : a + spread], s_ref[n, a : a + spread]),
                )
                for a in (0, spread)
            )
            total, other = even + odd, even - odd
            for p in range(step // 128):
                pair = paired(total[:, p * 128 : (p + 1) * 128], other[:, p * 128 : (p + 1) * 128])
                for k in range(2):
                    g = n * (step // part) + 2 * p + k
                    low = pair[k].astype(BF)
                    for m in range(count):
                        o_ref[g, :, m * tokens : (m + 1) * tokens] = low[m * rows : (m + 1) * rows]

    return call(
        kernel,
        shape(data.shape),
        (data, mask, cos, sin),
        [VMEM, VMEM, HBM, HBM],
        [pltpu.VMEM((count * rows, length), BF)]
        + [pltpu.VMEM((spread // step, length, step), BF)] * 2
        + [pltpu.SemaphoreType.DMA((spread // step, 2))],
        limit=57,
        flops=4 * count * rows * length * spread,
    )


def standardize(values):
    average = jnp.mean(values, axis=0, keepdims=True)
    centered = values - average
    spread = jnp.mean(centered * centered, axis=0, keepdims=True)
    inverse = lax.rsqrt(spread + EPSILON)
    return centered * inverse, inverse


def norm_back(upstream, standard, inverse, scaling):
    weighted = upstream * scaling
    return inverse * (
        weighted
        - jnp.mean(weighted, axis=0, keepdims=True)
        - standard * jnp.mean(weighted * standard, axis=0, keepdims=True)
    )


def column(table_ref, layer, i):
    k = layer * 5 + i
    return table_ref[:, k : k + 1]


def first_norm(got, low, unpack, factor, table, layer):
    width, columns = low.shape

    def kernel(r_ref, x_ref, unpack_ref, table_ref, unit_ref, inverse_ref, low_ref):
        mixed = mm(unpack_ref[...], r_ref[...])
        gain, shift = column(table_ref, layer, 1), column(table_ref, layer, 2)
        for a, b in blocks(columns, 128):
            unit, inverse = standardize(x_ref[:, a:b].astype(F32) + mixed[:, a:b] * factor)
            unit_ref[:, a:b] = unit.astype(BF)
            inverse_ref[:, a:b] = inverse
            low_ref[:, a:b] = (unit * gain + shift).astype(BF)

    outs = (shape((width, columns)), shape((1, columns), F32), shape((width, columns)))
    return call(kernel, outs, (got, low, unpack, table), flops=2 * width * width * columns)


def second_norm(unit1, parts, table, layer, labels, scored, packed):
    width, columns = unit1.shape
    count = len(parts)

    def kernel(*refs):
        unit1_ref, part_refs = refs[0], refs[1 : 1 + count]
        table_ref, labels_ref, scored_ref = refs[1 + count : 4 + count]
        bias, gain1, shift1, gain2, shift2 = (column(table_ref, layer, i) for i in range(5))
        bias = bias + shift1
        unit_ref, inverse_ref, low_ref, hits_ref = refs[len(refs) - outs_count :][:4]
        for a, b in blocks(columns, 128):
            values = unit1_ref[:, a:b].astype(F32) * gain1 + bias
            for part in part_refs:
                values = values + part[:, a:b].astype(F32)
            unit, inverse = standardize(values)
            unit_ref[:, a:b] = unit.astype(BF)
            inverse_ref[:, a:b] = inverse
            out = unit * gain2 + shift2
            low_ref[:, a:b] = out.astype(BF)
            exponent = jnp.exp(out)
            match = lax.broadcasted_iota(jnp.int32, out.shape, 0) == labels_ref[:, a:b]
            picked = jnp.sum(jnp.where(match, exponent, 0.0), axis=0, keepdims=True)
            total = jnp.sum(exponent, axis=0, keepdims=True)
            hits_ref[:, a:b] = picked / total * scored_ref[:, a:b]
        if packed is not None:
            refs[-1][...] = mm(refs[4 + count][...], low_ref[...]).astype(BF)

    row = shape((1, columns), F32)
    outs = [shape((width, columns)), row, shape((width, columns)), row]
    args = [unit1, *parts, table, labels, scored]
    if packed is not None:
        outs, args = outs + [shape((width, columns))], args + [packed]
    outs_count = len(outs)
    return call(kernel, tuple(outs), tuple(args), flops=2 * width * width * columns)


def row_sums(terms, width):
    total = jnp.zeros((8, width), F32)
    for row, term in terms:
        mark = (lax.broadcasted_iota(jnp.int32, (8, term.shape[1]), 0) == row).astype(BF)
        total = total + mm_nt(mark, term)
    return total


def second_back(up, unit, inverse, table, layer, mix=None):
    width, columns = unit.shape

    def kernel(*refs):
        up_ref, unit_ref, inverse_ref, table_ref = refs[:4]
        if mix is None:
            low_ref, sums_ref, product_ref = refs[4:]
            source_ref = up_ref
        else:
            got_ref, unpack_ref, low_ref, sums_ref, source_ref, product_ref = refs[4:]
            mixed = mm(unpack_ref[...], got_ref[...])
        gain = column(table_ref, layer, 3)
        for a, b in blocks(columns, 128):
            if mix is not None:
                values = up_ref[:, a:b].astype(F32) + mixed[:, a:b] * mix[2]
                source_ref[:, a:b] = values.astype(BF)
            values, unit = source_ref[:, a:b].astype(F32), unit_ref[:, a:b].astype(F32)
            low_ref[:, a:b] = norm_back(values, unit, inverse_ref[:, a:b], gain).astype(BF)
            product_ref[:, a:b] = (values * unit).astype(BF)
        sums_ref[...] = row_sums(
            ((0, low_ref[...]), (3, product_ref[...]), (4, source_ref[...])), width
        )

    outs = (shape(unit.shape), shape((8, width), F32))
    args = (up, unit, inverse, table)
    if mix is not None:
        outs, args = outs + (shape(unit.shape),), args + mix[:2]
    scratch = [pltpu.VMEM(unit.shape, BF)]
    return call(kernel, outs, args, None, scratch, flops=2 * width * width * columns)


def first_back(grad_second, parts, unit, inverse, table, layer, packed):
    width, columns = unit.shape
    count = len(parts)

    def kernel(second_ref, *refs):
        part_refs = refs[:count]
        unit_ref, inverse_ref, table_ref, packed_ref = refs[count : count + 4]
        low_ref, sums_ref, sent_ref, product_ref, normed_ref = refs[count + 4 :]
        gain = column(table_ref, layer, 1)
        for a, b in blocks(columns, 128):
            values, unit = second_ref[:, a:b].astype(F32), unit_ref[:, a:b].astype(F32)
            for part in part_refs:
                values = values + part[:, a:b].astype(F32)
            low_ref[:, a:b] = norm_back(values, unit, inverse_ref[:, a:b], gain).astype(BF)
            product_ref[:, a:b] = (values * unit).astype(BF)
            normed_ref[:, a:b] = values.astype(BF)
        sent_ref[...] = mm(packed_ref[...], low_ref[...]).astype(BF)
        sums_ref[...] = row_sums(((1, product_ref[...]), (2, normed_ref[...])), width)

    outs = (shape(unit.shape), shape((8, width), F32), shape(unit.shape))
    args = (grad_second, *parts, unit, inverse, table, packed)
    scratch = [pltpu.VMEM(unit.shape, BF)] * 2
    return call(kernel, outs, args, None, scratch, flops=2 * width * width * columns)


def last_mix(got, grad, unpack, factor):
    width, columns = grad.shape

    def kernel(got_ref, grad_ref, unpack_ref, o_ref):
        mixed = mm(unpack_ref[...], got_ref[...])
        o_ref[...] = (grad_ref[...].astype(F32) + mixed * factor).astype(BF)

    args = (got, grad, unpack)
    return call(kernel, shape(grad.shape), args, flops=2 * width * width * columns)


def gelu_parts(x):
    cdf = 0.5 + 0.5 * lax.erf(x * (1.0 / math.sqrt(2.0)))
    return cdf, jnp.exp(-0.5 * x * x) * (1.0 / math.sqrt(2.0 * math.pi))


def mm_tn(left, right):
    return lax.dot_general(left, right, (((0,), (0,)), ((), ())), preferred_element_type=F32)


def staged(pairs, sems):
    copies = [
        pltpu.make_async_copy(src, dst, sems.at[i]) for i, (src, dst) in enumerate(pairs)
    ]
    for copy in copies:
        copy.start()
    return copies


def chosen(flag, pairs, sems):
    copies = []
    for i, (sources, target) in enumerate(pairs):
        either = [pltpu.make_async_copy(src, target, sems.at[i]) for src in sources]

        @pl.when(flag == 1)
        def _():
            either[0].start()

        @pl.when(flag != 1)
        def _():
            either[1].start()

        copies.append(either[0])
    return copies


def ffn(flag, first, second, own, other, biases, layer):
    width, columns = first.shape
    units = own[0].shape[0]
    steps = blocks(units, 256)

    def kernel(flag_ref, a_ref, b_ref, own1, own2, other1, other2, bias_ref, *refs):
        oa_ref, ob_ref, act_hbm, slope_hbm, one_ref, two_ref, act_ref, slope_ref, sems, sent = refs
        copies = chosen(
            flag_ref[0],
            [((own1.at[a:b], other1.at[a:b]), one_ref.at[a:b]) for a, b in steps]
            + [((own2, other2), two_ref)],
            sems,
        )
        x = jnp.concatenate([a_ref[...], b_ref[...]], axis=1)
        writes = []
        for i, (a, b) in enumerate(steps):
            copies[i].wait()
            hidden = mm(one_ref[a:b], x) + bias_ref[a:b, layer : layer + 1]
            cdf, density = gelu_parts(hidden)
            act_ref[a:b] = (hidden * cdf).astype(BF)
            slope_ref[a:b] = (cdf + hidden * density).astype(BF)
            for k, (src, dst) in enumerate(((act_ref, act_hbm), (slope_ref, slope_hbm))):
                writes.append(pltpu.make_async_copy(src.at[a:b], dst.at[a:b], sent.at[i, k]))
                writes[-1].start()
        copies[-1].wait()
        for a, b in blocks(width, 256):
            part = mm(two_ref[a:b], act_ref[...])
            oa_ref[a:b] = part[:, :columns].astype(BF)
            ob_ref[a:b] = part[:, columns:].astype(BF)
        for write in writes:
            write.wait()

    half, full = shape((width, columns)), shape((units, 2 * columns))
    return call(
        kernel,
        (half, half, full, full),
        (flag, first, second, *own, *other, biases),
        [SMEM] + [VMEM] * 2 + [HBM] * 4 + [VMEM],
        [
            pltpu.VMEM((units, width), BF),
            pltpu.VMEM((width, units), BF),
            pltpu.VMEM(full.shape, BF),
            pltpu.VMEM(full.shape, BF),
            pltpu.SemaphoreType.DMA((len(steps) + 1,)),
            pltpu.SemaphoreType.DMA((len(steps), 2)),
        ],
        limit=57,
        flops=8 * width * units * columns,
        out_specs=(VMEM, VMEM, HBM, HBM),
    )


def ffn_back(flag, first, second, own, other, slope):
    width, columns = first.shape
    units = own[0].shape[0]
    steps = blocks(units, 256)

    def kernel(flag_ref, a_ref, b_ref, own1, own2, other1, other2, slope_hbm, *refs):
        oa_ref, ob_ref, pre_hbm, sums_ref, one_ref, two_ref, pre_ref, slope_ref, sems, sent = refs
        copies = chosen(
            flag_ref[0],
            [((own2, other2), two_ref)]
            + [((slope_hbm.at[a:b],) * 2, slope_ref.at[a:b]) for a, b in steps]
            + [((own1, other1), one_ref)],
            sems,
        )
        g = jnp.concatenate([a_ref[...], b_ref[...]], axis=1)
        copies[0].wait()
        writes = []
        for i, (a, b) in enumerate(steps):
            grad = mm_tn(two_ref[:, a:b], g)
            copies[1 + i].wait()
            pre_ref[a:b] = (grad * slope_ref[a:b].astype(F32)).astype(BF)
            writes.append(pltpu.make_async_copy(pre_ref.at[a:b], pre_hbm.at[a:b], sent.at[i]))
            writes[-1].start()
        copies[-1].wait()
        for a, b in blocks(width, 256):
            part = mm_tn(one_ref[:, a:b], pre_ref[...])
            oa_ref[a:b] = part[:, :columns].astype(BF)
            ob_ref[a:b] = part[:, columns:].astype(BF)
        sums_ref[...] = row_sums(((0, pre_ref[...]),), units)
        for write in writes:
            write.wait()

    half, full = shape((width, columns)), shape((units, 2 * columns))
    return call(
        kernel,
        (half, half, full, shape((8, units), F32)),
        (flag, first, second, *own, *other, slope),
        [SMEM] + [VMEM] * 2 + [HBM] * 5,
        [
            pltpu.VMEM((units, width), BF),
            pltpu.VMEM((width, units), BF),
            pltpu.VMEM(full.shape, BF),
            pltpu.VMEM(full.shape, BF),
            pltpu.SemaphoreType.DMA((len(steps) + 2,)),
            pltpu.SemaphoreType.DMA((len(steps),)),
        ],
        limit=57,
        flops=8 * width * units * columns,
        out_specs=(VMEM, VMEM, HBM, VMEM),
    )


def weight_grads(flag, xs, pres, gs, acts):
    units, width = pres[0].shape[0], xs[0].shape[0]
    tokens = sum(p.shape[1] for p in pres)
    groups = (gs, acts, pres, xs)
    sizes = [len(group) for group in groups]

    def kernel(flag_ref, *refs):
        inputs, rest = refs[: sum(sizes)], refs[sum(sizes) :]
        keep_hbm, give_hbm, one_ref, two_ref = rest[:4]
        scratch, sems, sent = rest[4:8], rest[8], rest[9]
        pairs, ends, k = [], [], 0
        for size, whole in zip(sizes, scratch):
            at = 0
            for _ in range(size):
                step = inputs[k].shape[1]
                pairs.append((inputs[k], whole.at[:, at : at + step]))
                at, k = at + step, k + 1
            ends.append(k)
        copies = staged(pairs, sems)

        def put(src, first, second, sem):
            either = [pltpu.make_async_copy(src, dst, sem) for dst in (first, second)]

            @pl.when(flag_ref[0] == 1)
            def _():
                either[0].start()

            @pl.when(flag_ref[0] != 1)
            def _():
                either[1].start()

            return either[0]

        for copy in copies[: ends[1]]:
            copy.wait()
        for a, b in blocks(width, 256):
            two_ref[a:b] = mm_nt(scratch[0][a:b], scratch[1][...]).astype(BF)
        writes = [put(two_ref, give_hbm, keep_hbm, sent.at[0])]
        for copy in copies[ends[1] :]:
            copy.wait()
        for a, b in blocks(units, 256):
            one_ref[a:b] = mm_nt(scratch[2][a:b], scratch[3][...]).astype(BF)
        writes.append(put(one_ref, keep_hbm, give_hbm, sent.at[1]))
        for write in writes:
            write.wait()

    if units != width:
        pre, x, g, act = (jnp.concatenate(group, axis=1) for group in (pres, xs, gs, acts))
        one, two = mm_nt(pre, x).astype(BF), mm_nt(g, act).astype(BF).reshape(units, width)
        return jnp.where(flag == 1, one, two), jnp.where(flag == 1, two, one)
    return call(
        kernel,
        (shape((units, width)),) * 2,
        (flag, *gs, *acts, *pres, *xs),
        [SMEM] + [HBM] * sum(sizes),
        [pltpu.VMEM((units, width), BF)] * 2
        + [pltpu.VMEM((rows, tokens), BF) for rows in (width, units, units, width)]
        + [pltpu.SemaphoreType.DMA((sum(sizes),)), pltpu.SemaphoreType.DMA((2,))],
        limit=57,
        flops=4 * width * units * tokens,
        out_specs=(HBM, HBM),
    )


def widened(gathered):
    planes, _, rows, width = gathered.shape

    def kernel(x_hbm, one_hbm, two_hbm, in_ref, out_ref, sems, sent):
        order = [(p, k) for k in range(2) for p in range(planes)]
        copies = [
            pltpu.make_async_copy(x_hbm.at[p, k], in_ref.at[p, k], sems.at[p, k]) for p, k in order
        ]
        for copy in copies:
            copy.start()
        writes = []
        for copy, (p, k) in zip(copies, order):
            copy.wait()
            out_ref[p, k] = in_ref[p, k].astype(F32)
            target = (one_hbm, two_hbm)[k].at[p * rows : (p + 1) * rows]
            writes.append(pltpu.make_async_copy(out_ref.at[p, k], target, sent.at[p, k]))
            writes[-1].start()
        for write in writes:
            write.wait()

    return call(
        kernel,
        (shape((planes * rows, width), F32),) * 2,
        (gathered,),
        [HBM],
        [
            pltpu.VMEM(gathered.shape, BF),
            pltpu.VMEM(gathered.shape, F32),
            pltpu.SemaphoreType.DMA((planes, 2)),
            pltpu.SemaphoreType.DMA((planes, 2)),
        ],
        out_specs=(HBM, HBM),
    )


def shards(
    inputs,
    cotangent,
    labels,
    scored,
    expand_weight,
    expand_bias,
    reduce_weight,
    reduce_bias,
    first_gain,
    first_shift,
    second_gain,
    second_shift,
):
    batches, feature_count, token_count = inputs.shape
    sections, halves, rests, sides, cores = (lax.axis_size(axis) for axis in AXES)
    mps = sides * cores
    group = sections * rests * mps
    width = feature_count * mps
    length = token_count * halves * rests
    units = expand_weight.shape[1]
    count = batches // halves
    part = token_count // sections // mps
    columns = count * halves * part
    rows = width // group
    factor = 1.0 / math.sqrt(length * width)
    section, half, rest, side, core = (lax.axis_index(axis) for axis in AXES)
    mp_index = side * cores + core
    is_first = section == 0

    packed, unpack = (jnp.asarray(t) for t in feature_tables(width, group))
    token_cos, token_sin = (jnp.asarray(t) for t in token_tables(sections, rests, mps, part))
    sorting = sorting_table(sections, token_count)
    unsorting, sorting = jnp.asarray(sorting.T), jnp.asarray(sorting)
    row_ids = jnp.arange(count * rows, dtype=jnp.int32) % rows
    corner = (section == 0) & (rest == 0) & (mp_index == 0)
    mask = (row_ids < rows // 2) | ((row_ids == rows // 2) & corner)
    mask = mask.astype(F32)[:, None]

    def swapped(array, axis, by=1):
        size = lax.axis_size(axis)
        return lax.ppermute(array, axis, [(i, (i + by) % size) for i in range(size)])

    own_one, own_two = expand_weight[0], reduce_weight[0]
    other_one, other_two = swapped(own_one, "section"), swapped(own_two, "section")

    def ordered(own, other):
        return [jnp.where(is_first, own, other), jnp.where(is_first, other, own)]

    small = [expand_bias, reduce_bias, first_gain, first_shift, second_gain, second_shift]
    small = jnp.concatenate([vector[0] for vector in small])
    small = jnp.stack(ordered(small, swapped(small, "section")))
    biases, vectors = small[:, :units].T, small[:, units:].reshape(sections * 5, 1, feature_count)
    vectors = jnp.concatenate(ordered_by(core, vectors, swapped(vectors, "core")), axis=1)
    chips = [swapped(vectors, "side", -j) if j else vectors for j in range(sides)]
    chips = jnp.stack(chips, axis=1)
    order = [(i - side) % sides for i in range(sides)]
    table = jnp.stack(
        [lax.dynamic_index_in_dim(chips, i, 1, keepdims=False) for i in order], axis=1
    ).reshape(sections * 5, width)
    table = jnp.pad(table, ((0, -table.shape[0] % 16), (0, 0))).T

    def to_pencils(local, table=None, *others):
        sent = send_pencils(local, section, sections, halves, mps, sorting)
        got = lax.all_to_all(sent, PLANE, 0, 0, tiled=True)
        if others:
            got, others = lax.optimization_barrier((got, others))
        return *take_pencils(got, halves, mps, count, table), *others

    def to_blocks(layers, extra):
        sent = send_blocks(layers, extra, sections, halves, mps, count, part)
        got = lax.all_to_all(sent, SQUARE, 0, 0, tiled=True)
        most = got.shape[1] - extra.shape[1]
        small = jnp.sum(got[:, most:].astype(F32), axis=0).reshape(-1)
        return got, small, sent

    def from_blocks(got):
        rows = feature_count // 2
        return take_blocks(got, rows, sections, halves, mps, count, unsorting)

    def fourier(sent, *others):
        sent = sent.reshape(group, rows, columns)
        got = lax.all_to_all(sent, RING, 0, 0, tiled=True)
        mixed = token_transform(got, mask, token_cos, token_sin, count)
        if others:
            mixed, others = lax.optimization_barrier((mixed, others))
        mixed = lax.all_to_all(mixed, RING, 0, 0, tiled=True).reshape(width, columns)
        return (mixed, *others) if others else mixed

    def gathered(own):
        return [own] + [swapped(own, "side", j) for j in range(1, sides)]

    def reduced(parts):
        terms = [parts[0][0], swapped(parts[0][1], "core")]
        for j in range(1, sides):
            keep, give = parts[j]
            chip = keep.astype(F32) + swapped(give, "core").astype(F32)
            terms.append(swapped(chip.astype(BF), "side", -j))
        return terms

    def added(first, second):
        return (first.astype(F32) + second.astype(F32)).astype(BF)

    def scattered(array):
        return lax.psum_scatter(array, ("half", "rest"), scatter_dimension=0, tiled=True)

    def in_turn(step, firsts):
        done, pairs = [], []
        for i, first in enumerate(firsts):
            if done:
                first, done[-1] = lax.optimization_barrier((first, done[-1]))
            pairs.append((first, swapped(first, "core")))
            done.append(step(*pairs[-1], i))
        return done, pairs

    marks = 2 * labels + scored
    marks = jnp.stack(ordered_by(half, marks, swapped(marks, "half")))
    marks = lax.dynamic_slice_in_dim(marks, half * count, count, 1)
    marks = marks.reshape(halves, count, mps, part, sections)
    marks = lax.dynamic_index_in_dim(marks, section, 4, keepdims=False)
    marks = lax.dynamic_index_in_dim(marks, mp_index, 2, keepdims=False)
    marks = marks.transpose(1, 0, 2).reshape(1, columns)
    local_labels, local_scored = marks // 2, (marks % 2).astype(F32)

    low, sent, other_one = to_pencils(inputs, packed, other_one)
    flags = [is_first.astype(jnp.int32).reshape(1), (1 - is_first.astype(jnp.int32)).reshape(1)]
    saved, outs, hits = [], [], jnp.zeros((), F32)
    for layer in range(2):
        if layer == 0:
            mixed, other_two, table, biases = fourier(sent, other_two, table, biases)
        else:
            mixed = fourier(sent)
        unit1, inv1, normed = first_norm(mixed, low, unpack, factor, table, layer)
        runs, xs = in_turn(
            lambda a, b, i: ffn(
                flags[layer], a, b, (own_one, own_two), (other_one, other_two), biases, layer
            ),
            gathered(normed),
        )
        terms = reduced([run[:2] for run in runs])
        if layer == 0:
            up, _ = lax.optimization_barrier((cotangent, runs[-1][0]))
            up = to_pencils(up)[0]
            terms, up = lax.optimization_barrier((terms, up))
        result = second_norm(
            unit1,
            terms,
            table,
            layer,
            local_labels,
            local_scored,
            packed if layer == 0 else None,
        )
        unit2, inv2, low, hit = result[:4]
        sent = result[-1]
        outs.append(low)
        hits = hits + jnp.sum(hit)
        saved.append((unit1, inv1, xs, runs, unit2, inv2))
    lanes = 2 * part
    outputs = to_blocks(outs, jnp.zeros((sections * halves * mps, 16, lanes), BF))[0]

    grads_in, weights_out, smalls, bias_rows = [None, None], [None, None], [None, None], [None, None]
    mix = None
    for layer in (1, 0):
        unit1, inv1, xs, runs, unit2, inv2 = saved[layer]
        result = second_back(up, unit2, inv2, table, layer, mix)
        grad_low, sums2 = result[:2]
        if mix is not None:
            grads_in[1] = result[2]
        backs, gs = in_turn(
            lambda a, b, i: ffn_back(
                flags[layer], a, b, (own_one, own_two), (other_one, other_two), runs[i][3]
            ),
            gathered(grad_low),
        )
        if layer == 0:
            late, _ = lax.optimization_barrier((late, backs[-1][0]))
            weights_out[1] = scattered(added(*late))
        terms = reduced([back[:2] for back in backs])
        keep, give = weight_grads(
            flags[0],
            [x for pair in xs for x in pair],
            [back[2] for back in backs],
            [g for pair in gs for g in pair],
            [run[2] for run in runs],
        )
        terms, keep, give = lax.optimization_barrier((terms, keep, give))
        if layer == 1:
            terms, outputs = lax.optimization_barrier((terms, outputs))
        up, sums1, sent = first_back(grad_low, terms, unit1, inv1, table, layer, packed)
        if layer == 1:
            mixed = fourier(sent)
            give, _ = lax.optimization_barrier((give, mixed))
            late = (keep, swapped(give, "section"))
        else:
            taken = swapped(give, "section")
            mixed, weights_out[1] = fourier(sent, weights_out[1])
            taken, _ = lax.optimization_barrier((taken, mixed))
            both = added(keep, taken)
            both, _ = lax.optimization_barrier((both, weights_out[1]))
            weights_out[0] = scattered(both)
        mix = (mixed, unpack, factor)
        smalls[layer] = sums1 + sums2
        bias_rows[layer] = sum(back[3][0] for back in backs)
    grads_in[0] = last_mix(mix[0], up, unpack, factor)

    high = hits.astype(BF)
    middle = (hits - high.astype(F32)).astype(BF)
    lowest = (hits - high.astype(F32) - middle.astype(F32)).astype(BF)
    counted = jnp.stack([high, middle, lowest])
    per = 5 * feature_count
    rows_of = []
    for layer in range(sections):
        vectors_of = smalls[layer][:5].reshape(5, mps, feature_count).transpose(1, 0, 2)
        mine = jnp.arange(mps, dtype=jnp.int32)[:, None] == mp_index
        rows_of.append(
            jnp.concatenate(
                [
                    vectors_of.reshape(mps, per).astype(BF),
                    jnp.where(mine, bias_rows[layer][None], 0.0).astype(BF),
                    jnp.broadcast_to(counted[None], (mps, 3)),
                ],
                axis=1,
            )
        )
    extra = jnp.stack(rows_of)
    extra = jnp.pad(extra, ((0, 0), (0, 0), (0, -extra.shape[2] % (8 * lanes))))
    extra = jnp.broadcast_to(extra[:, None], (sections, halves) + extra.shape[1:])
    got, small, sent = to_blocks(grads_in, extra.reshape(sections * halves * mps, -1, lanes))
    input_grads = from_blocks(got)
    outputs = from_blocks(outputs)
    small, step = small.reshape(-1, lanes), 1
    while step < rests:
        small = small + lax.ppermute(small, "rest", [(i, i ^ step) for i in range(rests)])
        step *= 2
    small = small.reshape(-1)
    features = small[:per].reshape(5, feature_count)
    bias_sum = small[per : per + units]
    accuracy = jnp.sum(small[per + units : per + units + 3])

    early, late = weights_out
    early, late, _ = lax.optimization_barrier((early, late, got))
    mine, other = jnp.where(is_first, early, late), jnp.where(is_first, late, early)
    other = swapped(other, "section")
    pair = jnp.stack(ordered(mine, other))
    pair = lax.all_gather(pair, ("half", "rest"), axis=0, tiled=False)
    one, two = widened(pair.reshape((-1,) + pair.shape[-3:]))
    weight_sums = [one, two.reshape(width, units)]

    return (
        outputs,
        input_grads,
        weight_sums[0][None],
        bias_sum[None],
        weight_sums[1][None],
        features[0][None],
        features[1][None],
        features[2][None],
        features[3][None],
        features[4][None],
        accuracy,
    )


def ordered_by(index, own, other):
    return [jnp.where(index == 0, own, other), jnp.where(index == 0, other, own)]


def solution(mesh):
    sizes = mesh.shape
    dims = (sizes["section"], 2, sizes["seq"] // 2, sizes["mp"] // 2, 2)
    names = ("section", ("half", "rest"), ("side", "core"))
    section, seq, mp = names
    placed = (
        P(None, mp, seq),
        P(None, mp, seq),
        P(None, seq),
        P(None, seq),
        P(section, mp, None),
        P(section, mp),
        P(section, None, mp),
        P(section, mp),
        P(section, mp),
        P(section, mp),
        P(section, mp),
        P(section, mp),
    )
    return jax.shard_map(
        shards,
        mesh=Mesh(mesh.devices.reshape(dims), AXES),
        in_specs=placed,
        out_specs=(
            P(section, None, mp, seq),
            P(section, None, mp, seq),
            P(section, mp, None),
            P(section, mp),
            P(section, None, mp),
            P(section, mp),
            P(section, mp),
            P(section, mp),
            P(section, mp),
            P(section, mp),
            P(),
        ),
        check_vma=False,
    )
```

```python
import math

import jax
import jax.numpy as jnp
import ml_dtypes
import numpy as np
from jax import lax
from jax.experimental import pallas as pl
from jax.experimental.pallas import tpu as pltpu
from jax.sharding import Mesh
from jax.sharding import PartitionSpec as P

EPSILON = 1e-05
BF = jnp.bfloat16
F32 = jnp.float32
MIB = 1 << 20
AXES = ("section", "half", "rest", "side", "core")
RING = ("section", "rest", "side", "core")
PLANE = ("half", "side", "core")
SQUARE = ("section", "half", "side", "core")
VMEM = pl.BlockSpec(memory_space=pltpu.VMEM)
HBM = pl.BlockSpec(memory_space=pltpu.HBM)
SMEM = pl.BlockSpec(memory_space=pltpu.SMEM)


def trig(rows, columns, points):
    phases = (rows.astype(np.int64)[:, None] * columns.astype(np.int64)[None, :]) % points
    angles = phases.astype(np.float64) * (2.0 * math.pi / points)
    return np.cos(angles), np.sin(angles)


def low_table(table):
    return table.astype(np.float32).astype(ml_dtypes.bfloat16)


def feature_tables(width, group):
    pairs = width // group // 2
    ids = np.arange(width // 2)
    cos, sin = trig(ids, np.arange(width), width)
    sin[0] = trig(np.array([width // 2]), np.arange(width), width)[0][0]
    packed = np.stack([cos.reshape(group, pairs, width), sin.reshape(group, pairs, width)], 1)
    unpack = np.zeros((width, width), np.float32)
    for k in range(width // 2):
        place = (k // pairs) * 2 * pairs + k % pairs
        if k == 0:
            unpack[0, place] = 1.0
            unpack[width // 2, place + pairs] = 1.0
        else:
            unpack[k, place] = 1.0
            unpack[k, place + pairs] = -1.0
            unpack[width - k, place] = 1.0
            unpack[width - k, place + pairs] = 1.0
    return low_table(packed.reshape(width, width)), low_table(unpack)


def token_tables(sections, rests, mps, part):
    parity, rest, place, i = np.meshgrid(
        np.arange(sections), np.arange(rests), np.arange(mps), np.arange(part), indexing="ij"
    )
    first = rest * sections * mps * part + sections * (place * part + i) + parity
    length = 2 * first.size
    every = np.stack([first, first + length // 2], 3).reshape(-1)
    cos, sin = trig(every, first.reshape(-1), length)
    return low_table(cos), low_table(sin)


def sorting_table(sections, count):
    table = np.zeros((count, count), np.float32)
    order = np.arange(count).reshape(-1, sections).T.reshape(-1)
    table[order, np.arange(count)] = 1.0
    return low_table(table)


def mm(left, right):
    return jnp.dot(left, right, preferred_element_type=F32)


def mm_nt(left, right):
    return lax.dot_general(left, right, (((1,), (1,)), ((), ())), preferred_element_type=F32)


def blocks(size, step):
    step = step if size % step == 0 else size
    return [(i, i + step) for i in range(0, size, step)]


def shape(dims, dtype=BF):
    return jax.ShapeDtypeStruct(tuple(dims), dtype)


def call(kernel, outs, args, specs=None, scratch=(), limit=52, flops=0, **extra):
    return pl.pallas_call(
        kernel,
        out_shape=outs,
        in_specs=specs or [VMEM] * len(args),
        scratch_shapes=list(scratch),
        compiler_params=pltpu.CompilerParams(vmem_limit_bytes=limit * MIB),
        cost_estimate=pl.CostEstimate(flops=flops, bytes_accessed=6 << 20, transcendentals=0),
        **extra,
    )(*args)


def paired(first, second):
    left = lax.broadcasted_iota(jnp.int32, first.shape, 1) < 64
    return (
        jnp.where(left, first, pltpu.roll(second, 64, axis=1)),
        jnp.where(left, pltpu.roll(first, 64, axis=1), second),
    )


def send_pencils(locals_, section, sections, halves, mps, sorting):
    batches, features, tokens = locals_[0].shape
    count, part, rows = batches // halves, tokens // sections // mps, features // 2
    kinds = len(locals_)
    out = shape((halves * mps, kinds * count * rows, 2 * part))
    if part != 64 or mps % 2:
        own = jnp.stack(locals_).reshape(kinds, halves, count, 2, rows, mps, part, sections)
        own = lax.dynamic_index_in_dim(own, section, 7, keepdims=False)
        return own.transpose(1, 5, 0, 2, 4, 3, 6).reshape(out.shape)
    sorting = sorting.reshape(tokens, sections, tokens // sections).transpose(1, 0, 2)

    def kernel(section_ref, *refs):
        x_refs, sorting_ref, o_ref = refs[:kinds], refs[kinds], refs[kinds + 1]
        for kind in range(kinds):
            for seq in range(batches):
                half, m = seq // count, seq % count
                values = mm(x_refs[kind][seq], sorting_ref[0])
                for place in range(0, mps, 2):
                    a = place * part
                    pair = paired(values[:rows, a : a + 128], values[rows:, a : a + 128])
                    for k in range(2):
                        d, at = half * mps + place + k, (kind * count + m) * rows
                        o_ref[d, at : at + rows] = pair[k].astype(BF)

    return pl.pallas_call(
        kernel,
        grid_spec=pltpu.PrefetchScalarGridSpec(
            num_scalar_prefetch=1,
            grid=(1,),
            in_specs=[pl.BlockSpec(locals_[0].shape, lambda i, s: (0, 0, 0))] * kinds
            + [pl.BlockSpec((1,) + sorting.shape[1:], lambda i, s: (s[0], 0, 0))],
            out_specs=pl.BlockSpec(out.shape, lambda i, s: (0, 0, 0)),
        ),
        out_shape=out,
        compiler_params=pltpu.CompilerParams(vmem_limit_bytes=52 * MIB),
    )(section.reshape(1), *locals_, sorting)


def take_pencils(got, kind, kinds, halves, mps, count, packed=None):
    rows, part = got.shape[1] // count // kinds, got.shape[2] // 2
    width, columns = mps * 2 * rows, count * halves * part
    if part != 64:
        got = got.reshape(halves, mps, kinds, count, rows, 2, part)[:, :, kind]
        low = got.transpose(1, 4, 3, 2, 0, 5).reshape(width, columns)
        return low, None if packed is None else mm(packed, low).astype(BF)

    def kernel(*refs):
        x_ref, o_ref = refs[0], refs[1 if packed is None else 2]
        for mp in range(mps):
            for m in range(count):
                at = (kind * count + m) * rows
                pair = paired(*(x_ref[h * mps + mp, at : at + rows].astype(F32) for h in range(2)))
                for k in range(2):
                    a = (mp * 2 + k) * rows
                    o_ref[a : a + rows, m * 128 : (m + 1) * 128] = pair[k].astype(BF)
        if packed is not None:
            refs[3][...] = mm(refs[1][...], o_ref[...]).astype(BF)

    low = shape((width, columns))
    if packed is None:
        return call(kernel, low, (got,)), None
    return call(kernel, (low, low), (got, packed))


def send_blocks(layers, extra, halves, mps, count, part):
    width, columns = layers[0].shape
    rows, kinds = width // mps // 2, len(layers)
    more = extra.shape[1]
    out = shape((kinds * halves * mps, count * rows + more, 2 * part))
    if part != 64:
        sent = jnp.stack(layers).reshape(kinds, mps, 2, rows, count, halves, part)
        sent = sent.transpose(0, 5, 1, 4, 3, 2, 6).reshape(-1, count * rows, 2 * part)
        return jnp.concatenate([sent, extra], axis=1)

    def kernel(*refs):
        o_ref = refs[-1]
        o_ref[:, count * rows :] = refs[kinds][...]
        for layer in range(kinds):
            for mp in range(mps):
                for m in range(count):
                    a, b = mp * 2 * rows, m * 128
                    pair = paired(
                        refs[layer][a : a + rows, b : b + 128].astype(F32),
                        refs[layer][a + rows : a + 2 * rows, b : b + 128].astype(F32),
                    )
                    for k in range(2):
                        d = (layer * halves + k) * mps + mp
                        o_ref[d, m * rows : (m + 1) * rows] = pair[k].astype(BF)

    return call(kernel, out, (*layers, extra))


def take_blocks(got, places, flipped, rows, halves, mps, count, unsorting):
    part = got[0].shape[-1] // 2
    out = (1, halves * count, 2 * rows, 2 * mps * part)
    got = [array.reshape(-1, halves, mps, array.shape[-2], 2 * part) for array in got]
    if part != 64 or mps % 2:
        both = jnp.stack([array[place, :, :, : count * rows] for array, place in zip(got, places)])
        both = jnp.where(flipped == 1, both[::-1], both)
        both = both.reshape(2, halves, mps, count, rows, 2, part)
        return both.transpose(1, 3, 5, 4, 2, 6, 0).reshape(out).astype(F32)
    tables = unsorting.reshape(2, -1, out[3])
    tables = jnp.stack([unsorting, tables[::-1].reshape(unsorting.shape)])

    def kernel(flag_ref, a_ref, b_ref, table_ref, o_ref, s_ref):
        for x, x_ref in enumerate((a_ref, b_ref)):
            for place in range(0, mps, 2):
                a = x * mps * part + place * part
                for m in range(count):
                    pair = paired(
                        *(
                            x_ref[0, 0, place + k, m * rows : (m + 1) * rows].astype(F32)
                            for k in range(2)
                        )
                    )
                    for k in range(2):
                        s_ref[(2 * m + k) * rows : (2 * m + k + 1) * rows, a : a + 128] = pair[
                            k
                        ].astype(BF)
        for m in range(count):
            o_ref[0, m] = mm(s_ref[2 * m * rows : 2 * (m + 1) * rows], table_ref[0])

    def block(place):
        return pl.BlockSpec((1, 1) + got[0].shape[2:], lambda i, s: (place, i, 0, 0, 0))

    return pl.pallas_call(
        kernel,
        grid_spec=pltpu.PrefetchScalarGridSpec(
            num_scalar_prefetch=1,
            grid=(halves,),
            in_specs=[
                block(places[0]),
                block(places[1]),
                pl.BlockSpec((1,) + unsorting.shape, lambda i, s: (s[0], 0, 0)),
            ],
            out_specs=pl.BlockSpec((1, count) + out[2:], lambda i, s: (i, 0, 0, 0)),
            scratch_shapes=[pltpu.VMEM((count * 2 * rows, out[3]), BF)],
        ),
        out_shape=shape((halves, count) + out[2:], F32),
        compiler_params=pltpu.CompilerParams(vmem_limit_bytes=52 * MIB),
    )(flipped, *got, tables).reshape(out)


def token_transform(data, mask, cos, sin, count):
    group, rows, columns = data.shape
    length, spread = cos.shape
    tokens = columns // count
    part = tokens // 2
    if part != 64:
        x = data.reshape(group, rows, count, tokens).transpose(2, 1, 0, 3)
        x = x.reshape(count * rows, length)
        mixed = [
            jnp.where(mask > 0.0, mm(x[:, a:b], cos[a:b]), mm(x[:, a:b], sin[a:b]))
            for a, b in ((0, spread), (spread, length))
        ]
        both = jnp.stack([mixed[0] + mixed[1], mixed[0] - mixed[1]]).astype(BF)
        both = both.reshape(2, count, rows, group, part).transpose(3, 2, 1, 0, 4)
        return both.reshape(data.shape)
    step = 256

    def kernel(d_ref, m_ref, c_hbm, s_hbm, o_ref, x_ref, c_ref, s_ref, sems):
        copies = []
        for n in range(spread // step):
            window = slice(n * step, (n + 1) * step)
            copies.append(
                [
                    pltpu.make_async_copy(src.at[:, window], dst.at[n], sems.at[n, k])
                    for k, (src, dst) in enumerate(((c_hbm, c_ref), (s_hbm, s_ref)))
                ]
            )
            for copy in copies[-1]:
                copy.start()
        for m in range(count):
            for g in range(group):
                x_ref[m * rows : (m + 1) * rows, g * tokens : (g + 1) * tokens] = d_ref[
                    g, :, m * tokens : (m + 1) * tokens
                ]
        keep = m_ref[...] > 0.0
        for n in range(spread // step):
            for copy in copies[n]:
                copy.wait()
            even, odd = (
                jnp.where(
                    keep,
                    mm(x_ref[:, a : a + spread], c_ref[n, a : a + spread]),
                    mm(x_ref[:, a : a + spread], s_ref[n, a : a + spread]),
                )
                for a in (0, spread)
            )
            total, other = even + odd, even - odd
            for p in range(step // 128):
                pair = paired(total[:, p * 128 : (p + 1) * 128], other[:, p * 128 : (p + 1) * 128])
                for k in range(2):
                    g = n * (step // part) + 2 * p + k
                    low = pair[k].astype(BF)
                    for m in range(count):
                        o_ref[g, :, m * tokens : (m + 1) * tokens] = low[m * rows : (m + 1) * rows]

    return call(
        kernel,
        shape(data.shape),
        (data, mask, cos, sin),
        [VMEM, VMEM, HBM, HBM],
        [pltpu.VMEM((count * rows, length), BF)]
        + [pltpu.VMEM((spread // step, length, step), BF)] * 2
        + [pltpu.SemaphoreType.DMA((spread // step, 2))],
        limit=52,
        flops=4 * count * rows * length * spread,
    )


def standardize(values):
    average = jnp.mean(values, axis=0, keepdims=True)
    centered = values - average
    spread = jnp.mean(centered * centered, axis=0, keepdims=True)
    inverse = lax.rsqrt(spread + EPSILON)
    return centered * inverse, inverse


def norm_back(upstream, standard, inverse, scaling):
    weighted = upstream * scaling
    return inverse * (
        weighted
        - jnp.mean(weighted, axis=0, keepdims=True)
        - standard * jnp.mean(weighted * standard, axis=0, keepdims=True)
    )


def column(table, layer, i):
    k = layer * 5 + i
    return table[:, k : k + 1]


def first_norm(got, low, unpack, factor, table, layer):
    width, columns = low.shape

    def kernel(r_ref, x_ref, unpack_ref, table_ref, unit_ref, inverse_ref, low_ref):
        mixed = mm(unpack_ref[...], r_ref[...])
        table = table_ref[...].T
        gain, shift = column(table, layer, 1), column(table, layer, 2)
        for a, b in blocks(columns, 128):
            unit, inverse = standardize(x_ref[:, a:b].astype(F32) + mixed[:, a:b] * factor)
            unit_ref[:, a:b] = unit.astype(BF)
            inverse_ref[:, a:b] = inverse
            low_ref[:, a:b] = (unit * gain + shift).astype(BF)

    outs = (shape((width, columns)), shape((1, columns), F32), shape((width, columns)))
    return call(kernel, outs, (got, low, unpack, table), flops=2 * width * width * columns)


def second_norm(unit1, parts, table, layer, labels, scored, packed):
    width, columns = unit1.shape
    count = len(parts)

    def kernel(*refs):
        unit1_ref, part_refs = refs[0], refs[1 : 1 + count]
        table_ref, labels_ref, scored_ref = refs[1 + count : 4 + count]
        vectors = table_ref[...].T
        bias, gain1, shift1, gain2, shift2 = (column(vectors, layer, i) for i in range(5))
        bias = bias + shift1
        unit_ref, inverse_ref, low_ref, hits_ref = refs[len(refs) - outs_count :][:4]
        for a, b in blocks(columns, 128):
            values = unit1_ref[:, a:b].astype(F32) * gain1 + bias
            for part in part_refs:
                values = values + part[:, a:b].astype(F32)
            unit, inverse = standardize(values)
            unit_ref[:, a:b] = unit.astype(BF)
            inverse_ref[:, a:b] = inverse
            out = unit * gain2 + shift2
            low_ref[:, a:b] = out.astype(BF)
            exponent = jnp.exp(out)
            match = lax.broadcasted_iota(jnp.int32, out.shape, 0) == labels_ref[:, a:b]
            picked = jnp.sum(jnp.where(match, exponent, 0.0), axis=0, keepdims=True)
            total = jnp.sum(exponent, axis=0, keepdims=True)
            hits_ref[:, a:b] = picked / total * scored_ref[:, a:b]
        if packed is not None:
            refs[-1][...] = mm(refs[4 + count][...], low_ref[...]).astype(BF)

    row = shape((1, columns), F32)
    outs = [shape((width, columns)), row, shape((width, columns)), row]
    args = [unit1, *parts, table, labels, scored]
    if packed is not None:
        outs, args = outs + [shape((width, columns))], args + [packed]
    outs_count = len(outs)
    return call(kernel, tuple(outs), tuple(args), flops=2 * width * width * columns)


def row_sums(terms, width):
    total = jnp.zeros((8, width), F32)
    for row, term in terms:
        mark = (lax.broadcasted_iota(jnp.int32, (8, term.shape[1]), 0) == row).astype(BF)
        total = total + mm_nt(mark, term)
    return total


def second_back(up, unit, inverse, table, layer, mix=None):
    width, columns = unit.shape

    def kernel(*refs):
        up_ref, unit_ref, inverse_ref, table_ref = refs[:4]
        if mix is None:
            low_ref, sums_ref, product_ref = refs[4:]
            source_ref = up_ref
        else:
            got_ref, unpack_ref, low_ref, sums_ref, source_ref, product_ref = refs[4:]
            mixed = mm(unpack_ref[...], got_ref[...])
        gain = column(table_ref[...].T, layer, 3)
        for a, b in blocks(columns, 128):
            if mix is not None:
                values = up_ref[:, a:b].astype(F32) + mixed[:, a:b] * mix[2]
                source_ref[:, a:b] = values.astype(BF)
            values, unit = source_ref[:, a:b].astype(F32), unit_ref[:, a:b].astype(F32)
            low_ref[:, a:b] = norm_back(values, unit, inverse_ref[:, a:b], gain).astype(BF)
            product_ref[:, a:b] = (values * unit).astype(BF)
        sums_ref[...] = row_sums(
            ((0, low_ref[...]), (3, product_ref[...]), (4, source_ref[...])), width
        )

    outs = (shape(unit.shape), shape((8, width), F32))
    args = (up, unit, inverse, table)
    if mix is not None:
        outs, args = outs + (shape(unit.shape),), args + mix[:2]
    scratch = [pltpu.VMEM(unit.shape, BF)]
    return call(kernel, outs, args, None, scratch, flops=2 * width * width * columns)


def first_back(grad_second, parts, unit, inverse, table, layer, packed):
    width, columns = unit.shape
    count = len(parts)

    def kernel(second_ref, *refs):
        part_refs = refs[:count]
        unit_ref, inverse_ref, table_ref, packed_ref = refs[count : count + 4]
        low_ref, sums_ref, sent_ref, product_ref, normed_ref = refs[count + 4 :]
        gain = column(table_ref[...].T, layer, 1)
        for a, b in blocks(columns, 128):
            values, unit = second_ref[:, a:b].astype(F32), unit_ref[:, a:b].astype(F32)
            for part in part_refs:
                values = values + part[:, a:b].astype(F32)
            low_ref[:, a:b] = norm_back(values, unit, inverse_ref[:, a:b], gain).astype(BF)
            product_ref[:, a:b] = (values * unit).astype(BF)
            normed_ref[:, a:b] = values.astype(BF)
        sent_ref[...] = mm(packed_ref[...], low_ref[...]).astype(BF)
        sums_ref[...] = row_sums(((1, product_ref[...]), (2, normed_ref[...])), width)

    outs = (shape(unit.shape), shape((8, width), F32), shape(unit.shape))
    args = (grad_second, *parts, unit, inverse, table, packed)
    scratch = [pltpu.VMEM(unit.shape, BF)] * 2
    return call(kernel, outs, args, None, scratch, flops=2 * width * width * columns)


def last_mix(got, grad, unpack, factor):
    width, columns = grad.shape

    def kernel(got_ref, grad_ref, unpack_ref, o_ref):
        mixed = mm(unpack_ref[...], got_ref[...])
        o_ref[...] = (grad_ref[...].astype(F32) + mixed * factor).astype(BF)

    args = (got, grad, unpack)
    return call(kernel, shape(grad.shape), args, flops=2 * width * width * columns)


def gelu_parts(x):
    cdf = 0.5 + 0.5 * lax.erf(x * (1.0 / math.sqrt(2.0)))
    return cdf, jnp.exp(-0.5 * x * x) * (1.0 / math.sqrt(2.0 * math.pi))


def mm_tn(left, right):
    return lax.dot_general(left, right, (((0,), (0,)), ((), ())), preferred_element_type=F32)


def staged(pairs, sems):
    copies = [
        pltpu.make_async_copy(src, dst, sems.at[i]) for i, (src, dst) in enumerate(pairs)
    ]
    for copy in copies:
        copy.start()
    return copies


def chosen(flag, pairs, sems):
    copies = []
    for i, (sources, target) in enumerate(pairs):
        either = [pltpu.make_async_copy(src, target, sems.at[i]) for src in sources]

        @pl.when(flag == 1)
        def _():
            either[0].start()

        @pl.when(flag != 1)
        def _():
            either[1].start()

        copies.append(either[0])
    return copies


def ffn(flag, first, second, own, other, biases, layer):
    width, columns = first.shape
    units = own[0].shape[0]
    steps = blocks(units, 256)

    def kernel(flag_ref, a_ref, b_ref, own1, own2, other1, other2, bias_ref, *refs):
        oa_ref, ob_ref, act_hbm, slope_hbm, one_ref, two_ref, act_ref, slope_ref, sems, sent = refs
        copies = chosen(
            flag_ref[0],
            [((own1.at[a:b], other1.at[a:b]), one_ref.at[a:b]) for a, b in steps]
            + [((own2, other2), two_ref)],
            sems,
        )
        x = jnp.concatenate([a_ref[...], b_ref[...]], axis=1)
        bias = bias_ref[...].T
        writes = []
        for i, (a, b) in enumerate(steps):
            copies[i].wait()
            hidden = mm(one_ref[a:b], x) + bias[a:b, layer : layer + 1]
            cdf, density = gelu_parts(hidden)
            act_ref[a:b] = (hidden * cdf).astype(BF)
            slope_ref[a:b] = (cdf + hidden * density).astype(BF)
            for k, (src, dst) in enumerate(((act_ref, act_hbm), (slope_ref, slope_hbm))):
                writes.append(pltpu.make_async_copy(src.at[a:b], dst.at[a:b], sent.at[i, k]))
                writes[-1].start()
        copies[-1].wait()
        for a, b in blocks(width, 256):
            part = mm(two_ref[a:b], act_ref[...])
            oa_ref[a:b] = part[:, :columns].astype(BF)
            ob_ref[a:b] = part[:, columns:].astype(BF)
        for write in writes:
            write.wait()

    half, full = shape((width, columns)), shape((units, 2 * columns))
    return call(
        kernel,
        (half, half, full, full),
        (flag, first, second, *own, *other, biases),
        [SMEM] + [VMEM] * 2 + [HBM] * 4 + [VMEM],
        [
            pltpu.VMEM((units, width), BF),
            pltpu.VMEM((width, units), BF),
            pltpu.VMEM(full.shape, BF),
            pltpu.VMEM(full.shape, BF),
            pltpu.SemaphoreType.DMA((len(steps) + 1,)),
            pltpu.SemaphoreType.DMA((len(steps), 2)),
        ],
        limit=52,
        flops=8 * width * units * columns,
        out_specs=(VMEM, VMEM, HBM, HBM),
    )


def ffn_back(flag, first, second, own, other, slope):
    width, columns = first.shape
    units = own[0].shape[0]
    steps = blocks(units, 256)

    def kernel(flag_ref, a_ref, b_ref, own1, own2, other1, other2, slope_hbm, *refs):
        oa_ref, ob_ref, pre_hbm, sums_ref, one_ref, two_ref, pre_ref, slope_ref, sems, sent = refs
        copies = chosen(
            flag_ref[0],
            [((own2, other2), two_ref)]
            + [((slope_hbm.at[a:b],) * 2, slope_ref.at[a:b]) for a, b in steps]
            + [((own1, other1), one_ref)],
            sems,
        )
        g = jnp.concatenate([a_ref[...], b_ref[...]], axis=1)
        copies[0].wait()
        writes = []
        for i, (a, b) in enumerate(steps):
            grad = mm_tn(two_ref[:, a:b], g)
            copies[1 + i].wait()
            pre_ref[a:b] = (grad * slope_ref[a:b].astype(F32)).astype(BF)
            writes.append(pltpu.make_async_copy(pre_ref.at[a:b], pre_hbm.at[a:b], sent.at[i]))
            writes[-1].start()
        copies[-1].wait()
        for a, b in blocks(width, 256):
            part = mm_tn(one_ref[:, a:b], pre_ref[...])
            oa_ref[a:b] = part[:, :columns].astype(BF)
            ob_ref[a:b] = part[:, columns:].astype(BF)
        sums_ref[...] = row_sums(((0, pre_ref[...]),), units)
        for write in writes:
            write.wait()

    half, full = shape((width, columns)), shape((units, 2 * columns))
    return call(
        kernel,
        (half, half, full, shape((8, units), F32)),
        (flag, first, second, *own, *other, slope),
        [SMEM] + [VMEM] * 2 + [HBM] * 5,
        [
            pltpu.VMEM((units, width), BF),
            pltpu.VMEM((width, units), BF),
            pltpu.VMEM(full.shape, BF),
            pltpu.VMEM(full.shape, BF),
            pltpu.SemaphoreType.DMA((len(steps) + 2,)),
            pltpu.SemaphoreType.DMA((len(steps),)),
        ],
        limit=52,
        flops=8 * width * units * columns,
        out_specs=(VMEM, VMEM, HBM, VMEM),
    )


def weight_grads(flag, xs, pres, gs, acts):
    units, width = pres[0].shape[0], xs[0].shape[0]
    tokens = sum(p.shape[1] for p in pres)
    groups = (gs, acts, pres, xs)
    sizes = [len(group) for group in groups]

    def kernel(flag_ref, *refs):
        inputs, rest = refs[: sum(sizes)], refs[sum(sizes) :]
        keep_hbm, give_hbm, one_ref, two_ref = rest[:4]
        scratch, sems, sent = rest[4:8], rest[8], rest[9]
        pairs, ends, k = [], [], 0
        for size, whole in zip(sizes, scratch):
            at = 0
            for _ in range(size):
                step = inputs[k].shape[1]
                pairs.append((inputs[k], whole.at[:, at : at + step]))
                at, k = at + step, k + 1
            ends.append(k)
        copies = staged(pairs, sems)

        def put(src, first, second, sem):
            either = [pltpu.make_async_copy(src, dst, sem) for dst in (first, second)]

            @pl.when(flag_ref[0] == 1)
            def _():
                either[0].start()

            @pl.when(flag_ref[0] != 1)
            def _():
                either[1].start()

            return either[0]

        for copy in copies[: ends[1]]:
            copy.wait()
        for a, b in blocks(width, 256):
            two_ref[a:b] = mm_nt(scratch[0][a:b], scratch[1][...]).astype(BF)
        writes = [put(two_ref, give_hbm, keep_hbm, sent.at[0])]
        for copy in copies[ends[1] :]:
            copy.wait()
        for a, b in blocks(units, 256):
            one_ref[a:b] = mm_nt(scratch[2][a:b], scratch[3][...]).astype(BF)
        writes.append(put(one_ref, keep_hbm, give_hbm, sent.at[1]))
        for write in writes:
            write.wait()

    if units != width:
        pre, x, g, act = (jnp.concatenate(group, axis=1) for group in (pres, xs, gs, acts))
        one, two = mm_nt(pre, x).astype(BF), mm_nt(g, act).astype(BF).reshape(units, width)
        return jnp.where(flag == 1, one, two), jnp.where(flag == 1, two, one)
    return call(
        kernel,
        (shape((units, width)),) * 2,
        (flag, *gs, *acts, *pres, *xs),
        [SMEM] + [HBM] * sum(sizes),
        [pltpu.VMEM((units, width), BF)] * 2
        + [pltpu.VMEM((rows, tokens), BF) for rows in (width, units, units, width)]
        + [pltpu.SemaphoreType.DMA((sum(sizes),)), pltpu.SemaphoreType.DMA((2,))],
        limit=52,
        flops=4 * width * units * tokens,
        out_specs=(HBM, HBM),
    )


def widened(gathered):
    planes, _, rows, width = gathered.shape

    def kernel(x_hbm, one_hbm, two_hbm, in_ref, out_ref, sems, sent):
        order = [(p, k) for k in range(2) for p in range(planes)]
        copies = [
            pltpu.make_async_copy(x_hbm.at[p, k], in_ref.at[p, k], sems.at[p, k]) for p, k in order
        ]
        for copy in copies:
            copy.start()
        writes = []
        for copy, (p, k) in zip(copies, order):
            copy.wait()
            out_ref[p, k] = in_ref[p, k].astype(F32)
            target = (one_hbm, two_hbm)[k].at[p * rows : (p + 1) * rows]
            writes.append(pltpu.make_async_copy(out_ref.at[p, k], target, sent.at[p, k]))
            writes[-1].start()
        for write in writes:
            write.wait()

    return call(
        kernel,
        (shape((planes * rows, width), F32),) * 2,
        (gathered,),
        [HBM],
        [
            pltpu.VMEM(gathered.shape, BF),
            pltpu.VMEM(gathered.shape, F32),
            pltpu.SemaphoreType.DMA((planes, 2)),
            pltpu.SemaphoreType.DMA((planes, 2)),
        ],
        out_specs=(HBM, HBM),
    )


def shards(
    inputs,
    cotangent,
    labels,
    scored,
    expand_weight,
    expand_bias,
    reduce_weight,
    reduce_bias,
    first_gain,
    first_shift,
    second_gain,
    second_shift,
):
    batches, feature_count, token_count = inputs.shape
    sections, halves, rests, sides, cores = (lax.axis_size(axis) for axis in AXES)
    mps = sides * cores
    group = sections * rests * mps
    width = feature_count * mps
    length = token_count * halves * rests
    units = expand_weight.shape[1]
    count = batches // halves
    part = token_count // sections // mps
    columns = count * halves * part
    rows = width // group
    factor = 1.0 / math.sqrt(length * width)
    section, half, rest, side, core = (lax.axis_index(axis) for axis in AXES)
    mp_index = side * cores + core
    is_first = section == 0

    packed, unpack = (jnp.asarray(t) for t in feature_tables(width, group))
    token_cos, token_sin = (jnp.asarray(t) for t in token_tables(sections, rests, mps, part))
    sorting = sorting_table(sections, token_count)
    unsorting, sorting = jnp.asarray(sorting.T), jnp.asarray(sorting)
    row_ids = jnp.arange(count * rows, dtype=jnp.int32) % rows
    corner = (section == 0) & (rest == 0) & (mp_index == 0)
    mask = (row_ids < rows // 2) | ((row_ids == rows // 2) & corner)
    mask = mask.astype(F32)[:, None]

    def swapped(array, axis, by=1):
        size = lax.axis_size(axis)
        return lax.ppermute(array, axis, [(i, (i + by) % size) for i in range(size)])

    own_one, own_two = expand_weight[0], reduce_weight[0]
    other_one, other_two = swapped(own_one, "section"), swapped(own_two, "section")

    def ordered(own, other):
        return [jnp.where(is_first, own, other), jnp.where(is_first, other, own)]

    small = [expand_bias, reduce_bias, first_gain, first_shift, second_gain, second_shift]
    small = jnp.concatenate([vector[0] for vector in small])
    small = jnp.stack(ordered(small, swapped(small, "section")))
    biases = jnp.pad(small[:, :units], ((0, 8 - sections), (0, 0)))
    vectors = small[:, units:].reshape(sections * 5, 1, feature_count)
    vectors = jnp.concatenate(ordered_by(core, vectors, swapped(vectors, "core")), axis=1)
    chips = [swapped(vectors, "side", -j) if j else vectors for j in range(sides)]
    chips = jnp.stack(chips, axis=1)
    order = [(i - side) % sides for i in range(sides)]
    table = jnp.stack(
        [lax.dynamic_index_in_dim(chips, i, 1, keepdims=False) for i in order], axis=1
    ).reshape(sections * 5, width)
    table = jnp.pad(table, ((0, -table.shape[0] % 16), (0, 0)))

    lanes = 2 * part

    def small_rows(layer, hits):
        high = hits.astype(BF)
        middle = (hits - high.astype(F32)).astype(BF)
        lowest = (hits - high.astype(F32) - middle.astype(F32)).astype(BF)
        counted = jnp.broadcast_to(jnp.stack([high, middle, lowest])[None], (mps, 3))
        of_features = smalls[layer][:5].reshape(5, mps, feature_count).transpose(1, 0, 2)
        mine = jnp.arange(mps, dtype=jnp.int32)[:, None] == mp_index
        bias = jnp.where(mine, bias_rows[layer][None], 0.0)
        extra = jnp.concatenate(
            [of_features.reshape(mps, -1).astype(BF), bias.astype(BF), counted], axis=1
        )
        extra = jnp.pad(extra, ((0, 0), (0, -extra.shape[1] % (8 * lanes))))
        extra = jnp.broadcast_to(extra[None], (halves,) + extra.shape)
        return extra.reshape(halves * mps, -1, lanes)

    def small_sums(got, extra):
        most = got.shape[1] - extra.shape[1]
        return jnp.sum(got[:, most:].astype(F32), axis=0).reshape(-1)

    def fourier(sent, *others):
        sent = sent.reshape(group, rows, columns)
        got = lax.all_to_all(sent, RING, 0, 0, tiled=True)
        mixed = token_transform(got, mask, token_cos, token_sin, count)
        if others:
            mixed, others = lax.optimization_barrier((mixed, others))
        mixed = lax.all_to_all(mixed, RING, 0, 0, tiled=True).reshape(width, columns)
        return (mixed, *others) if others else mixed

    def gathered(own):
        return [own] + [swapped(own, "side", j) for j in range(1, sides)]

    def reduced(parts):
        terms = [parts[0][0], swapped(parts[0][1], "core")]
        for j in range(1, sides):
            keep, give = parts[j]
            chip = keep.astype(F32) + swapped(give, "core").astype(F32)
            terms.append(swapped(chip.astype(BF), "side", -j))
        return terms

    def added(first, second):
        return (first.astype(F32) + second.astype(F32)).astype(BF)

    def scattered(array):
        return lax.psum_scatter(array, ("half", "rest"), scatter_dimension=0, tiled=True)

    def in_turn(step, firsts):
        done, pairs = [], []
        for i, first in enumerate(firsts):
            if done:
                first, done[-1] = lax.optimization_barrier((first, done[-1]))
            pairs.append((first, swapped(first, "core")))
            done.append(step(*pairs[-1], i))
        return done, pairs

    marks = 2 * labels + scored
    marks = jnp.stack(ordered_by(half, marks, swapped(marks, "half")))
    marks = lax.dynamic_slice_in_dim(marks, half * count, count, 1)
    marks = marks.reshape(halves, count, mps, part, sections)
    marks = lax.dynamic_index_in_dim(marks, section, 4, keepdims=False)
    marks = lax.dynamic_index_in_dim(marks, mp_index, 2, keepdims=False)
    marks = marks.transpose(1, 0, 2).reshape(1, columns)
    local_labels, local_scored = marks // 2, (marks % 2).astype(F32)

    got = send_pencils((inputs, cotangent), section, sections, halves, mps, sorting)
    got = lax.all_to_all(got, PLANE, 0, 0, tiled=True)
    got, other_one = lax.optimization_barrier((got, other_one))
    low, sent = take_pencils(got, 0, 2, halves, mps, count, packed)
    up, _ = lax.optimization_barrier((got, sent))
    flags = [is_first.astype(jnp.int32).reshape(1), (1 - is_first.astype(jnp.int32)).reshape(1)]
    saved, outs, hits = [], [], jnp.zeros((), F32)
    for layer in range(2):
        if layer == 0:
            mixed, other_two, table, biases = fourier(sent, other_two, table, biases)
        else:
            mixed = fourier(sent)
        unit1, inv1, normed = first_norm(mixed, low, unpack, factor, table, layer)
        runs, xs = in_turn(
            lambda a, b, i: ffn(
                flags[layer], a, b, (own_one, own_two), (other_one, other_two), biases, layer
            ),
            gathered(normed),
        )
        terms = reduced([run[:2] for run in runs])
        if layer == 0:
            up, _ = take_pencils(up, 1, 2, halves, mps, count)
            terms, up = lax.optimization_barrier((terms, up))
        result = second_norm(
            unit1,
            terms,
            table,
            layer,
            local_labels,
            local_scored,
            packed if layer == 0 else None,
        )
        unit2, inv2, low, hit = result[:4]
        sent = result[-1]
        outs.append(low)
        hits = hits + jnp.sum(hit)
        saved.append((unit1, inv1, xs, runs, unit2, inv2))
    nothing = jnp.zeros((sections * halves * mps, 16, lanes), BF)
    outputs = send_blocks(outs, nothing, halves, mps, count, part)
    outputs = lax.all_to_all(outputs, SQUARE, 0, 0, tiled=True)

    grads_in, weights_out, smalls, bias_rows = [None, None], [None, None], [None, None], [None, None]
    mix = None
    for layer in (1, 0):
        unit1, inv1, xs, runs, unit2, inv2 = saved[layer]
        result = second_back(up, unit2, inv2, table, layer, mix)
        grad_low, sums2 = result[:2]
        if mix is not None:
            grads_in[1] = result[2]
        backs, gs = in_turn(
            lambda a, b, i: ffn_back(
                flags[layer], a, b, (own_one, own_two), (other_one, other_two), runs[i][3]
            ),
            gathered(grad_low),
        )
        if layer == 0:
            late, _ = lax.optimization_barrier((late, backs[-1][0]))
            weights_out[1] = scattered(added(*late))
        terms = reduced([back[:2] for back in backs])
        keep, give = weight_grads(
            flags[0],
            [x for pair in xs for x in pair],
            [back[2] for back in backs],
            [g for pair in gs for g in pair],
            [run[2] for run in runs],
        )
        terms, keep, give = lax.optimization_barrier((terms, keep, give))
        if layer == 1:
            terms, outputs = lax.optimization_barrier((terms, outputs))
        up, sums1, sent = first_back(grad_low, terms, unit1, inv1, table, layer, packed)
        if layer == 1:
            mixed = fourier(sent)
            give, _ = lax.optimization_barrier((give, mixed))
            late = (keep, swapped(give, "section"))
        else:
            extra = small_rows(1, hits)
            got_late, _ = lax.optimization_barrier((grads_in[1], sent))
            got_late = send_blocks([got_late], extra, halves, mps, count, part)
            got_late = lax.all_to_all(got_late, PLANE, 0, 0, tiled=True)
            sent, taken, weights_out[1], got_late = lax.optimization_barrier(
                (sent, swapped(give, "section"), weights_out[1], got_late)
            )
            weights_out[0] = scattered(added(keep, taken))
            mixed = fourier(sent)
            rows_of = feature_count // 2
            outputs = take_blocks(
                (outputs, outputs), (0, 1), 0 * flags[0], rows_of, halves, mps, count, unsorting
            )
            mixed, outputs = lax.optimization_barrier((mixed, outputs))
        mix = (mixed, unpack, factor)
        smalls[layer] = sums1 + sums2
        bias_rows[layer] = sum(back[3][0] for back in backs)
    grads_in[0] = last_mix(mix[0], up, unpack, factor)

    extra = small_rows(0, hits)
    sent = send_blocks(grads_in[:1], extra, halves, mps, count, part)
    got = lax.all_to_all(sent, PLANE, 0, 0, tiled=True)
    mine, other = jnp.where(is_first, got, got_late), jnp.where(is_first, got_late, got)
    other = swapped(other, "section")
    rows_of = feature_count // 2
    input_grads = take_blocks(
        (mine, other), (0, 0), flags[1], rows_of, halves, mps, count, unsorting
    )
    small, step = (small_sums(mine, extra) + small_sums(other, extra)).reshape(-1, lanes), 1
    while step < rests:
        small = small + lax.ppermute(small, "rest", [(i, i ^ step) for i in range(rests)])
        step *= 2
    small, per = small.reshape(-1), 5 * feature_count
    features = small[:per].reshape(5, feature_count)
    bias_sum = small[per : per + units]
    accuracy = jnp.sum(small[per + units : per + units + 3])

    early, late = weights_out
    early, late, _ = lax.optimization_barrier((early, late, sent))
    mine, other = jnp.where(is_first, early, late), jnp.where(is_first, late, early)
    other = swapped(other, "section")
    pair = jnp.stack(ordered(mine, other))
    pair = lax.all_gather(pair, ("half", "rest"), axis=0, tiled=False)
    one, two = widened(pair.reshape((-1,) + pair.shape[-3:]))
    weight_sums = [one, two.reshape(width, units)]

    return (
        outputs,
        input_grads,
        weight_sums[0][None],
        bias_sum[None],
        weight_sums[1][None],
        features[0][None],
        features[1][None],
        features[2][None],
        features[3][None],
        features[4][None],
        accuracy,
    )


def ordered_by(index, own, other):
    return [jnp.where(index == 0, own, other), jnp.where(index == 0, other, own)]


def solution(mesh):
    sizes = mesh.shape
    dims = (sizes["section"], 2, sizes["seq"] // 2, sizes["mp"] // 2, 2)
    names = ("section", ("half", "rest"), ("side", "core"))
    section, seq, mp = names
    placed = (
        P(None, mp, seq),
        P(None, mp, seq),
        P(None, seq),
        P(None, seq),
        P(section, mp, None),
        P(section, mp),
        P(section, None, mp),
        P(section, mp),
        P(section, mp),
        P(section, mp),
        P(section, mp),
        P(section, mp),
    )
    return jax.shard_map(
        shards,
        mesh=Mesh(mesh.devices.reshape(dims), AXES),
        in_specs=placed,
        out_specs=(
            P(section, None, mp, seq),
            P(section, None, mp, seq),
            P(section, mp, None),
            P(section, mp),
            P(section, None, mp),
            P(section, mp),
            P(section, mp),
            P(section, mp),
            P(section, mp),
            P(section, mp),
            P(),
        ),
        check_vma=False,
    )
```

```python
import math

import jax
import jax.numpy as jnp
import ml_dtypes
import numpy as np
from jax import lax
from jax.experimental import pallas as pl
from jax.experimental.pallas import tpu as pltpu
from jax.sharding import Mesh
from jax.sharding import PartitionSpec as P

EPSILON = 1e-05
BF = jnp.bfloat16
F32 = jnp.float32
MIB = 1 << 20
AXES = ("section", "half", "rest", "side", "core")
RING = ("section", "rest", "side", "core")
PLANE = ("half", "side", "core")
SQUARE = ("section", "half", "side", "core")
VMEM = pl.BlockSpec(memory_space=pltpu.VMEM)
HBM = pl.BlockSpec(memory_space=pltpu.HBM)
SMEM = pl.BlockSpec(memory_space=pltpu.SMEM)


def trig(rows, columns, points):
    phases = (rows.astype(np.int64)[:, None] * columns.astype(np.int64)[None, :]) % points
    angles = phases.astype(np.float64) * (2.0 * math.pi / points)
    return np.cos(angles), np.sin(angles)


def low_table(table):
    return table.astype(np.float32).astype(ml_dtypes.bfloat16)


def feature_tables(width, group):
    pairs = width // group // 2
    ids = np.arange(width // 2)
    cos, sin = trig(ids, np.arange(width), width)
    sin[0] = trig(np.array([width // 2]), np.arange(width), width)[0][0]
    packed = np.stack([cos.reshape(group, pairs, width), sin.reshape(group, pairs, width)], 1)
    unpack = np.zeros((width, width), np.float32)
    for k in range(width // 2):
        place = (k // pairs) * 2 * pairs + k % pairs
        if k == 0:
            unpack[0, place] = 1.0
            unpack[width // 2, place + pairs] = 1.0
        else:
            unpack[k, place] = 1.0
            unpack[k, place + pairs] = -1.0
            unpack[width - k, place] = 1.0
            unpack[width - k, place + pairs] = 1.0
    return low_table(packed.reshape(width, width)), low_table(unpack)


def token_tables(sections, rests, mps, part):
    parity, rest, place, i = np.meshgrid(
        np.arange(sections), np.arange(rests), np.arange(mps), np.arange(part), indexing="ij"
    )
    first = rest * sections * mps * part + sections * (place * part + i) + parity
    length = 2 * first.size
    every = np.stack([first, first + length // 2], 3).reshape(-1)
    cos, sin = trig(every, first.reshape(-1), length)
    return low_table(cos), low_table(sin)


def sorting_table(sections, count):
    table = np.zeros((count, count), np.float32)
    order = np.arange(count).reshape(-1, sections).T.reshape(-1)
    table[order, np.arange(count)] = 1.0
    return low_table(table)


def mm(left, right):
    return jnp.dot(left, right, preferred_element_type=F32)


def mm_nt(left, right):
    return lax.dot_general(left, right, (((1,), (1,)), ((), ())), preferred_element_type=F32)


def blocks(size, step):
    step = step if size % step == 0 else size
    return [(i, i + step) for i in range(0, size, step)]


def shape(dims, dtype=BF):
    return jax.ShapeDtypeStruct(tuple(dims), dtype)


def call(kernel, outs, args, specs=None, scratch=(), limit=52, flops=0, **extra):
    return pl.pallas_call(
        kernel,
        out_shape=outs,
        in_specs=specs or [VMEM] * len(args),
        scratch_shapes=list(scratch),
        compiler_params=pltpu.CompilerParams(vmem_limit_bytes=limit * MIB),
        cost_estimate=pl.CostEstimate(flops=flops, bytes_accessed=6 << 20, transcendentals=0),
        **extra,
    )(*args)


def paired(first, second):
    left = lax.broadcasted_iota(jnp.int32, first.shape, 1) < 64
    return (
        jnp.where(left, first, pltpu.roll(second, 64, axis=1)),
        jnp.where(left, pltpu.roll(first, 64, axis=1), second),
    )


def send_pencils(locals_, section, sections, halves, mps, sorting):
    batches, features, tokens = locals_[0].shape
    count, part, rows = batches // halves, tokens // sections // mps, features // 2
    kinds = len(locals_)
    out = shape((halves * mps, kinds * count * rows, 2 * part))
    if part != 64 or mps % 2:
        own = jnp.stack(locals_).reshape(kinds, halves, count, 2, rows, mps, part, sections)
        own = lax.dynamic_index_in_dim(own, section, 7, keepdims=False)
        return own.transpose(1, 5, 0, 2, 4, 3, 6).reshape(out.shape)
    sorting = sorting.reshape(tokens, sections, tokens // sections).transpose(1, 0, 2)

    def kernel(section_ref, *refs):
        x_refs, sorting_ref, o_ref = refs[:kinds], refs[kinds], refs[kinds + 1]
        for kind in range(kinds):
            for seq in range(batches):
                half, m = seq // count, seq % count
                values = mm(x_refs[kind][seq], sorting_ref[0])
                for place in range(0, mps, 2):
                    a = place * part
                    pair = paired(values[:rows, a : a + 128], values[rows:, a : a + 128])
                    for k in range(2):
                        d, at = half * mps + place + k, (kind * count + m) * rows
                        o_ref[d, at : at + rows] = pair[k].astype(BF)

    return pl.pallas_call(
        kernel,
        grid_spec=pltpu.PrefetchScalarGridSpec(
            num_scalar_prefetch=1,
            grid=(1,),
            in_specs=[pl.BlockSpec(locals_[0].shape, lambda i, s: (0, 0, 0))] * kinds
            + [pl.BlockSpec((1,) + sorting.shape[1:], lambda i, s: (s[0], 0, 0))],
            out_specs=pl.BlockSpec(out.shape, lambda i, s: (0, 0, 0)),
        ),
        out_shape=out,
        compiler_params=pltpu.CompilerParams(vmem_limit_bytes=52 * MIB),
    )(section.reshape(1), *locals_, sorting)


def take_pencils(got, kind, kinds, halves, mps, count, packed=None):
    rows, part = got.shape[1] // count // kinds, got.shape[2] // 2
    width, columns = mps * 2 * rows, count * halves * part
    if part != 64:
        got = got.reshape(halves, mps, kinds, count, rows, 2, part)[:, :, kind]
        low = got.transpose(1, 4, 3, 2, 0, 5).reshape(width, columns)
        return low, None if packed is None else mm(packed, low).astype(BF)

    def kernel(*refs):
        x_ref, o_ref = refs[0], refs[1 if packed is None else 2]
        for mp in range(mps):
            for m in range(count):
                at = (kind * count + m) * rows
                pair = paired(*(x_ref[h * mps + mp, at : at + rows].astype(F32) for h in range(2)))
                for k in range(2):
                    a = (mp * 2 + k) * rows
                    o_ref[a : a + rows, m * 128 : (m + 1) * 128] = pair[k].astype(BF)
        if packed is not None:
            refs[3][...] = mm(refs[1][...], o_ref[...]).astype(BF)

    low = shape((width, columns))
    if packed is None:
        return call(kernel, low, (got,)), None
    return call(kernel, (low, low), (got, packed))


def send_blocks(layers, extra, halves, mps, count, part):
    width, columns = layers[0].shape
    rows, kinds = width // mps // 2, len(layers)
    more = extra.shape[1]
    out = shape((kinds * halves * mps, count * rows + more, 2 * part))
    if part != 64:
        sent = jnp.stack(layers).reshape(kinds, mps, 2, rows, count, halves, part)
        sent = sent.transpose(0, 5, 1, 4, 3, 2, 6).reshape(-1, count * rows, 2 * part)
        return jnp.concatenate([sent, extra], axis=1)

    def kernel(*refs):
        o_ref = refs[-1]
        o_ref[:, count * rows :] = refs[kinds][...]
        for layer in range(kinds):
            for mp in range(mps):
                for m in range(count):
                    a, b = mp * 2 * rows, m * 128
                    pair = paired(
                        refs[layer][a : a + rows, b : b + 128].astype(F32),
                        refs[layer][a + rows : a + 2 * rows, b : b + 128].astype(F32),
                    )
                    for k in range(2):
                        d = (layer * halves + k) * mps + mp
                        o_ref[d, m * rows : (m + 1) * rows] = pair[k].astype(BF)

    return call(kernel, out, (*layers, extra))


def take_blocks(got, places, flipped, rows, halves, mps, count, unsorting):
    part = got[0].shape[-1] // 2
    out = (1, halves * count, 2 * rows, 2 * mps * part)
    got = [array.reshape(-1, halves, mps, array.shape[-2], 2 * part) for array in got]
    if part != 64 or mps % 2:
        both = jnp.stack([array[place, :, :, : count * rows] for array, place in zip(got, places)])
        both = jnp.where(flipped == 1, both[::-1], both)
        both = both.reshape(2, halves, mps, count, rows, 2, part)
        return both.transpose(1, 3, 5, 4, 2, 6, 0).reshape(out).astype(F32)
    tables = unsorting.reshape(2, -1, out[3])
    tables = jnp.stack([unsorting, tables[::-1].reshape(unsorting.shape)])

    def kernel(flag_ref, a_ref, b_ref, table_ref, o_ref, s_ref):
        for x, x_ref in enumerate((a_ref, b_ref)):
            for place in range(0, mps, 2):
                a = x * mps * part + place * part
                for m in range(count):
                    pair = paired(
                        *(
                            x_ref[0, 0, place + k, m * rows : (m + 1) * rows].astype(F32)
                            for k in range(2)
                        )
                    )
                    for k in range(2):
                        s_ref[(2 * m + k) * rows : (2 * m + k + 1) * rows, a : a + 128] = pair[
                            k
                        ].astype(BF)
        for m in range(count):
            o_ref[0, m] = mm(s_ref[2 * m * rows : 2 * (m + 1) * rows], table_ref[0])

    def block(place):
        return pl.BlockSpec((1, 1) + got[0].shape[2:], lambda i, s: (place, i, 0, 0, 0))

    return pl.pallas_call(
        kernel,
        grid_spec=pltpu.PrefetchScalarGridSpec(
            num_scalar_prefetch=1,
            grid=(halves,),
            in_specs=[
                block(places[0]),
                block(places[1]),
                pl.BlockSpec((1,) + unsorting.shape, lambda i, s: (s[0], 0, 0)),
            ],
            out_specs=pl.BlockSpec((1, count) + out[2:], lambda i, s: (i, 0, 0, 0)),
            scratch_shapes=[pltpu.VMEM((count * 2 * rows, out[3]), BF)],
        ),
        out_shape=shape((halves, count) + out[2:], F32),
        compiler_params=pltpu.CompilerParams(vmem_limit_bytes=52 * MIB),
    )(flipped, *got, tables).reshape(out)


def token_transform(data, mask, cos, sin, count):
    group, rows, columns = data.shape
    length, spread = cos.shape
    tokens = columns // count
    part = tokens // 2
    if part != 64:
        x = data.reshape(group, rows, count, tokens).transpose(2, 1, 0, 3)
        x = x.reshape(count * rows, length)
        mixed = [
            jnp.where(mask > 0.0, mm(x[:, a:b], cos[a:b]), mm(x[:, a:b], sin[a:b]))
            for a, b in ((0, spread), (spread, length))
        ]
        both = jnp.stack([mixed[0] + mixed[1], mixed[0] - mixed[1]]).astype(BF)
        both = both.reshape(2, count, rows, group, part).transpose(3, 2, 1, 0, 4)
        return both.reshape(data.shape)
    step = 256

    def kernel(d_ref, m_ref, c_hbm, s_hbm, o_ref, x_ref, c_ref, s_ref, sems):
        copies = []
        for n in range(spread // step):
            window = slice(n * step, (n + 1) * step)
            copies.append(
                [
                    pltpu.make_async_copy(src.at[:, window], dst.at[n], sems.at[n, k])
                    for k, (src, dst) in enumerate(((c_hbm, c_ref), (s_hbm, s_ref)))
                ]
            )
            for copy in copies[-1]:
                copy.start()
        for m in range(count):
            for g in range(group):
                x_ref[m * rows : (m + 1) * rows, g * tokens : (g + 1) * tokens] = d_ref[
                    g, :, m * tokens : (m + 1) * tokens
                ]
        keep = m_ref[...] > 0.0
        for n in range(spread // step):
            for copy in copies[n]:
                copy.wait()
            even, odd = (
                jnp.where(
                    keep,
                    mm(x_ref[:, a : a + spread], c_ref[n, a : a + spread]),
                    mm(x_ref[:, a : a + spread], s_ref[n, a : a + spread]),
                )
                for a in (0, spread)
            )
            total, other = even + odd, even - odd
            for p in range(step // 128):
                pair = paired(total[:, p * 128 : (p + 1) * 128], other[:, p * 128 : (p + 1) * 128])
                for k in range(2):
                    g = n * (step // part) + 2 * p + k
                    low = pair[k].astype(BF)
                    for m in range(count):
                        o_ref[g, :, m * tokens : (m + 1) * tokens] = low[m * rows : (m + 1) * rows]

    return call(
        kernel,
        shape(data.shape),
        (data, mask, cos, sin),
        [VMEM, VMEM, HBM, HBM],
        [pltpu.VMEM((count * rows, length), BF)]
        + [pltpu.VMEM((spread // step, length, step), BF)] * 2
        + [pltpu.SemaphoreType.DMA((spread // step, 2))],
        limit=52,
        flops=4 * count * rows * length * spread,
    )


def standardize(values):
    average = jnp.mean(values, axis=0, keepdims=True)
    centered = values - average
    spread = jnp.mean(centered * centered, axis=0, keepdims=True)
    inverse = lax.rsqrt(spread + EPSILON)
    return centered * inverse, inverse


def norm_back(upstream, standard, inverse, scaling):
    weighted = upstream * scaling
    return inverse * (
        weighted
        - jnp.mean(weighted, axis=0, keepdims=True)
        - standard * jnp.mean(weighted * standard, axis=0, keepdims=True)
    )


def column(table, layer, i):
    k = layer * 5 + i
    return table[:, k : k + 1]


def first_norm(got, low, unpack, factor, table, layer):
    width, columns = low.shape

    def kernel(r_ref, x_ref, unpack_ref, table_ref, unit_ref, inverse_ref, low_ref):
        mixed = mm(unpack_ref[...], r_ref[...])
        table = table_ref[...].T
        gain, shift = column(table, layer, 1), column(table, layer, 2)
        for a, b in blocks(columns, 128):
            unit, inverse = standardize(x_ref[:, a:b].astype(F32) + mixed[:, a:b] * factor)
            unit_ref[:, a:b] = unit.astype(BF)
            inverse_ref[:, a:b] = inverse
            low_ref[:, a:b] = (unit * gain + shift).astype(BF)

    outs = (shape((width, columns)), shape((1, columns), F32), shape((width, columns)))
    return call(kernel, outs, (got, low, unpack, table), flops=2 * width * width * columns)


def second_norm(unit1, parts, table, layer, labels, scored, packed):
    width, columns = unit1.shape
    count = len(parts)

    def kernel(*refs):
        unit1_ref, part_refs = refs[0], refs[1 : 1 + count]
        table_ref, labels_ref, scored_ref = refs[1 + count : 4 + count]
        vectors = table_ref[...].T
        bias, gain1, shift1, gain2, shift2 = (column(vectors, layer, i) for i in range(5))
        bias = bias + shift1
        unit_ref, inverse_ref, low_ref, hits_ref = refs[len(refs) - outs_count :][:4]
        for a, b in blocks(columns, 128):
            values = unit1_ref[:, a:b].astype(F32) * gain1 + bias
            for part in part_refs:
                values = values + part[:, a:b].astype(F32)
            unit, inverse = standardize(values)
            unit_ref[:, a:b] = unit.astype(BF)
            inverse_ref[:, a:b] = inverse
            out = unit * gain2 + shift2
            low_ref[:, a:b] = out.astype(BF)
            exponent = jnp.exp(out)
            match = lax.broadcasted_iota(jnp.int32, out.shape, 0) == labels_ref[:, a:b]
            picked = jnp.sum(jnp.where(match, exponent, 0.0), axis=0, keepdims=True)
            total = jnp.sum(exponent, axis=0, keepdims=True)
            hits_ref[:, a:b] = picked / total * scored_ref[:, a:b]
        if packed is not None:
            refs[-1][...] = mm(refs[4 + count][...], low_ref[...]).astype(BF)

    row = shape((1, columns), F32)
    outs = [shape((width, columns)), row, shape((width, columns)), row]
    args = [unit1, *parts, table, labels, scored]
    if packed is not None:
        outs, args = outs + [shape((width, columns))], args + [packed]
    outs_count = len(outs)
    return call(kernel, tuple(outs), tuple(args), flops=2 * width * width * columns)


def row_sums(terms, width):
    total = jnp.zeros((8, width), F32)
    for row, term in terms:
        mark = (lax.broadcasted_iota(jnp.int32, (8, term.shape[1]), 0) == row).astype(BF)
        total = total + mm_nt(mark, term)
    return total


def second_back(up, unit, inverse, table, layer, mix=None):
    width, columns = unit.shape

    def kernel(*refs):
        up_ref, unit_ref, inverse_ref, table_ref = refs[:4]
        if mix is None:
            low_ref, sums_ref, product_ref = refs[4:]
            source_ref = up_ref
        else:
            got_ref, unpack_ref, low_ref, sums_ref, source_ref, product_ref = refs[4:]
            mixed = mm(unpack_ref[...], got_ref[...])
        gain = column(table_ref[...].T, layer, 3)
        for a, b in blocks(columns, 128):
            if mix is not None:
                values = up_ref[:, a:b].astype(F32) + mixed[:, a:b] * mix[2]
                source_ref[:, a:b] = values.astype(BF)
            values, unit = source_ref[:, a:b].astype(F32), unit_ref[:, a:b].astype(F32)
            low_ref[:, a:b] = norm_back(values, unit, inverse_ref[:, a:b], gain).astype(BF)
            product_ref[:, a:b] = (values * unit).astype(BF)
        sums_ref[...] = row_sums(
            ((0, low_ref[...]), (3, product_ref[...]), (4, source_ref[...])), width
        )

    outs = (shape(unit.shape), shape((8, width), F32))
    args = (up, unit, inverse, table)
    if mix is not None:
        outs, args = outs + (shape(unit.shape),), args + mix[:2]
    scratch = [pltpu.VMEM(unit.shape, BF)]
    return call(kernel, outs, args, None, scratch, flops=2 * width * width * columns)


def first_back(grad_second, parts, unit, inverse, table, layer, packed):
    width, columns = unit.shape
    count = len(parts)

    def kernel(second_ref, *refs):
        part_refs = refs[:count]
        unit_ref, inverse_ref, table_ref, packed_ref = refs[count : count + 4]
        low_ref, sums_ref, sent_ref, product_ref, normed_ref = refs[count + 4 :]
        gain = column(table_ref[...].T, layer, 1)
        for a, b in blocks(columns, 128):
            values, unit = second_ref[:, a:b].astype(F32), unit_ref[:, a:b].astype(F32)
            for part in part_refs:
                values = values + part[:, a:b].astype(F32)
            low_ref[:, a:b] = norm_back(values, unit, inverse_ref[:, a:b], gain).astype(BF)
            product_ref[:, a:b] = (values * unit).astype(BF)
            normed_ref[:, a:b] = values.astype(BF)
        sent_ref[...] = mm(packed_ref[...], low_ref[...]).astype(BF)
        sums_ref[...] = row_sums(((1, product_ref[...]), (2, normed_ref[...])), width)

    outs = (shape(unit.shape), shape((8, width), F32), shape(unit.shape))
    args = (grad_second, *parts, unit, inverse, table, packed)
    scratch = [pltpu.VMEM(unit.shape, BF)] * 2
    return call(kernel, outs, args, None, scratch, flops=2 * width * width * columns)


def last_mix(got, grad, unpack, factor):
    width, columns = grad.shape

    def kernel(got_ref, grad_ref, unpack_ref, o_ref):
        mixed = mm(unpack_ref[...], got_ref[...])
        o_ref[...] = (grad_ref[...].astype(F32) + mixed * factor).astype(BF)

    args = (got, grad, unpack)
    return call(kernel, shape(grad.shape), args, flops=2 * width * width * columns)


def gelu_parts(x):
    cdf = 0.5 + 0.5 * lax.erf(x * (1.0 / math.sqrt(2.0)))
    return cdf, jnp.exp(-0.5 * x * x) * (1.0 / math.sqrt(2.0 * math.pi))


def mm_tn(left, right):
    return lax.dot_general(left, right, (((0,), (0,)), ((), ())), preferred_element_type=F32)


def staged(pairs, sems):
    copies = [
        pltpu.make_async_copy(src, dst, sems.at[i]) for i, (src, dst) in enumerate(pairs)
    ]
    for copy in copies:
        copy.start()
    return copies


def chosen(flag, pairs, sems):
    copies = []
    for i, (sources, target) in enumerate(pairs):
        either = [pltpu.make_async_copy(src, target, sems.at[i]) for src in sources]

        @pl.when(flag == 1)
        def _():
            either[0].start()

        @pl.when(flag != 1)
        def _():
            either[1].start()

        copies.append(either[0])
    return copies


def ffn(flag, first, second, own, other, biases, layer):
    width, columns = first.shape
    units = own[0].shape[0]
    steps = blocks(units, 256)

    def kernel(flag_ref, a_ref, b_ref, own1, own2, other1, other2, bias_ref, *refs):
        oa_ref, ob_ref, act_hbm, slope_hbm, one_ref, two_ref, act_ref, slope_ref, sems, sent = refs
        copies = chosen(
            flag_ref[0],
            [((own1.at[a:b], other1.at[a:b]), one_ref.at[a:b]) for a, b in steps]
            + [((own2, other2), two_ref)],
            sems,
        )
        x = jnp.concatenate([a_ref[...], b_ref[...]], axis=1)
        bias = bias_ref[...].T
        writes = []
        for i, (a, b) in enumerate(steps):
            copies[i].wait()
            hidden = mm(one_ref[a:b], x) + bias[a:b, layer : layer + 1]
            cdf, density = gelu_parts(hidden)
            act_ref[a:b] = (hidden * cdf).astype(BF)
            slope_ref[a:b] = (cdf + hidden * density).astype(BF)
            for k, (src, dst) in enumerate(((act_ref, act_hbm), (slope_ref, slope_hbm))):
                writes.append(pltpu.make_async_copy(src.at[a:b], dst.at[a:b], sent.at[i, k]))
                writes[-1].start()
        copies[-1].wait()
        for a, b in blocks(width, 256):
            part = mm(two_ref[a:b], act_ref[...])
            oa_ref[a:b] = part[:, :columns].astype(BF)
            ob_ref[a:b] = part[:, columns:].astype(BF)
        for write in writes:
            write.wait()

    half, full = shape((width, columns)), shape((units, 2 * columns))
    return call(
        kernel,
        (half, half, full, full),
        (flag, first, second, *own, *other, biases),
        [SMEM] + [VMEM] * 2 + [HBM] * 4 + [VMEM],
        [
            pltpu.VMEM((units, width), BF),
            pltpu.VMEM((width, units), BF),
            pltpu.VMEM(full.shape, BF),
            pltpu.VMEM(full.shape, BF),
            pltpu.SemaphoreType.DMA((len(steps) + 1,)),
            pltpu.SemaphoreType.DMA((len(steps), 2)),
        ],
        limit=52,
        flops=8 * width * units * columns,
        out_specs=(VMEM, VMEM, HBM, HBM),
    )


def ffn_back(flag, first, second, own, other, slope):
    width, columns = first.shape
    units = own[0].shape[0]
    steps = blocks(units, 256)

    def kernel(flag_ref, a_ref, b_ref, own1, own2, other1, other2, slope_hbm, *refs):
        oa_ref, ob_ref, pre_hbm, sums_ref, one_ref, two_ref, pre_ref, slope_ref, sems, sent = refs
        copies = chosen(
            flag_ref[0],
            [((own2, other2), two_ref)]
            + [((slope_hbm.at[a:b],) * 2, slope_ref.at[a:b]) for a, b in steps]
            + [((own1, other1), one_ref)],
            sems,
        )
        g = jnp.concatenate([a_ref[...], b_ref[...]], axis=1)
        copies[0].wait()
        writes = []
        for i, (a, b) in enumerate(steps):
            grad = mm_tn(two_ref[:, a:b], g)
            copies[1 + i].wait()
            pre_ref[a:b] = (grad * slope_ref[a:b].astype(F32)).astype(BF)
            writes.append(pltpu.make_async_copy(pre_ref.at[a:b], pre_hbm.at[a:b], sent.at[i]))
            writes[-1].start()
        copies[-1].wait()
        for a, b in blocks(width, 256):
            part = mm_tn(one_ref[:, a:b], pre_ref[...])
            oa_ref[a:b] = part[:, :columns].astype(BF)
            ob_ref[a:b] = part[:, columns:].astype(BF)
        sums_ref[...] = row_sums(((0, pre_ref[...]),), units)
        for write in writes:
            write.wait()

    half, full = shape((width, columns)), shape((units, 2 * columns))
    return call(
        kernel,
        (half, half, full, shape((8, units), F32)),
        (flag, first, second, *own, *other, slope),
        [SMEM] + [VMEM] * 2 + [HBM] * 5,
        [
            pltpu.VMEM((units, width), BF),
            pltpu.VMEM((width, units), BF),
            pltpu.VMEM(full.shape, BF),
            pltpu.VMEM(full.shape, BF),
            pltpu.SemaphoreType.DMA((len(steps) + 2,)),
            pltpu.SemaphoreType.DMA((len(steps),)),
        ],
        limit=52,
        flops=8 * width * units * columns,
        out_specs=(VMEM, VMEM, HBM, VMEM),
    )


def weight_grad(flag, lefts, rights):
    rows, width = lefts[0][0].shape[0], rights[0][0].shape[0]
    sizes = [[array.shape[1] for array in either] for either in (lefts[1], rights[1])]
    tokens = sum(sizes[0])
    parts = [(side, either) for side in range(2) for either in range(2)]
    lists = {(side, either): (lefts, rights)[side][either] for side, either in parts}

    def kernel(flag_ref, *refs):
        inputs, (out_ref, left_ref, right_ref, sems) = refs[:-4], refs[-4:]
        at, groups = 0, {}
        for part in parts:
            groups[part] = inputs[at : at + len(lists[part])]
            at += len(lists[part])
        wholes = (left_ref, right_ref)

        def fill(either, act):
            k = 0
            for side in range(2):
                place = 0
                for src in groups[side, either]:
                    step = src.shape[1]
                    target = wholes[side].at[:, place : place + step]
                    act(pltpu.make_async_copy(src, target, sems.at[either, k]))
                    place, k = place + step, k + 1

        for act in (lambda copy: copy.start(), lambda copy: copy.wait()):
            for either in range(2):

                @pl.when((flag_ref[0] == 1) == (either == 0))
                def _():
                    fill(either, act)

        for a, b in blocks(rows, 256):
            out_ref[a:b] = mm_nt(left_ref[a:b], right_ref[...]).astype(BF)

    count = max(len(lists[0, e]) + len(lists[1, e]) for e in range(2))
    args = [array for part in parts for array in lists[part]]
    return call(
        kernel,
        shape((rows, width)),
        (flag, *args),
        [SMEM] + [HBM] * len(args),
        [
            pltpu.VMEM((rows, tokens), BF),
            pltpu.VMEM((width, tokens), BF),
            pltpu.SemaphoreType.DMA((2, count)),
        ],
        limit=52,
        flops=2 * width * rows * tokens,
    )


def weight_grads(flag, xs, pres, gs, acts):
    units, width = pres[0].shape[0], xs[0].shape[0]
    if units != width:
        pre, x, g, act = (jnp.concatenate(group, axis=1) for group in (pres, xs, gs, acts))
        one, two = mm_nt(pre, x).astype(BF), mm_nt(g, act).astype(BF).reshape(units, width)
        return jnp.where(flag == 1, one, two), jnp.where(flag == 1, two, one)
    give = weight_grad(flag, (gs, pres), (acts, xs))
    keep = weight_grad(flag, (pres, gs), (xs, acts))
    return keep, give


def widened(gathered):
    planes, _, rows, width = gathered.shape

    def kernel(x_hbm, one_hbm, two_hbm, in_ref, out_ref, sems, sent):
        order = [(p, k) for k in range(2) for p in range(planes)]
        copies = [
            pltpu.make_async_copy(x_hbm.at[p, k], in_ref.at[p, k], sems.at[p, k]) for p, k in order
        ]
        for copy in copies:
            copy.start()
        writes = []
        for copy, (p, k) in zip(copies, order):
            copy.wait()
            out_ref[p, k] = in_ref[p, k].astype(F32)
            target = (one_hbm, two_hbm)[k].at[p * rows : (p + 1) * rows]
            writes.append(pltpu.make_async_copy(out_ref.at[p, k], target, sent.at[p, k]))
            writes[-1].start()
        for write in writes:
            write.wait()

    return call(
        kernel,
        (shape((planes * rows, width), F32),) * 2,
        (gathered,),
        [HBM],
        [
            pltpu.VMEM(gathered.shape, BF),
            pltpu.VMEM(gathered.shape, F32),
            pltpu.SemaphoreType.DMA((planes, 2)),
            pltpu.SemaphoreType.DMA((planes, 2)),
        ],
        out_specs=(HBM, HBM),
    )


def shards(
    inputs,
    cotangent,
    labels,
    scored,
    expand_weight,
    expand_bias,
    reduce_weight,
    reduce_bias,
    first_gain,
    first_shift,
    second_gain,
    second_shift,
):
    batches, feature_count, token_count = inputs.shape
    sections, halves, rests, sides, cores = (lax.axis_size(axis) for axis in AXES)
    mps = sides * cores
    group = sections * rests * mps
    width = feature_count * mps
    length = token_count * halves * rests
    units = expand_weight.shape[1]
    count = batches // halves
    part = token_count // sections // mps
    columns = count * halves * part
    rows = width // group
    factor = 1.0 / math.sqrt(length * width)
    section, half, rest, side, core = (lax.axis_index(axis) for axis in AXES)
    mp_index = side * cores + core
    is_first = section == 0

    packed, unpack = (jnp.asarray(t) for t in feature_tables(width, group))
    token_cos, token_sin = (jnp.asarray(t) for t in token_tables(sections, rests, mps, part))
    sorting = sorting_table(sections, token_count)
    unsorting, sorting = jnp.asarray(sorting.T), jnp.asarray(sorting)
    row_ids = jnp.arange(count * rows, dtype=jnp.int32) % rows
    corner = (section == 0) & (rest == 0) & (mp_index == 0)
    mask = (row_ids < rows // 2) | ((row_ids == rows // 2) & corner)
    mask = mask.astype(F32)[:, None]

    def swapped(array, axis, by=1):
        size = lax.axis_size(axis)
        return lax.ppermute(array, axis, [(i, (i + by) % size) for i in range(size)])

    own_one, own_two = expand_weight[0], reduce_weight[0]
    other_one, other_two = swapped(own_one, "section"), swapped(own_two, "section")

    def ordered(own, other):
        return [jnp.where(is_first, own, other), jnp.where(is_first, other, own)]

    small = [expand_bias, reduce_bias, first_gain, first_shift, second_gain, second_shift]
    small = jnp.concatenate([vector[0] for vector in small])
    small = jnp.stack(ordered(small, swapped(small, "section")))
    biases = jnp.pad(small[:, :units], ((0, 8 - sections), (0, 0)))
    vectors = small[:, units:].reshape(sections * 5, 1, feature_count)
    vectors = jnp.concatenate(ordered_by(core, vectors, swapped(vectors, "core")), axis=1)
    chips = [swapped(vectors, "side", -j) if j else vectors for j in range(sides)]
    chips = jnp.stack(chips, axis=1)
    order = [(i - side) % sides for i in range(sides)]
    table = jnp.stack(
        [lax.dynamic_index_in_dim(chips, i, 1, keepdims=False) for i in order], axis=1
    ).reshape(sections * 5, width)
    table = jnp.pad(table, ((0, -table.shape[0] % 16), (0, 0)))

    lanes = 2 * part

    def small_rows(layer, hits):
        high = hits.astype(BF)
        middle = (hits - high.astype(F32)).astype(BF)
        lowest = (hits - high.astype(F32) - middle.astype(F32)).astype(BF)
        counted = jnp.broadcast_to(jnp.stack([high, middle, lowest])[None], (mps, 3))
        of_features = smalls[layer][:5].reshape(5, mps, feature_count).transpose(1, 0, 2)
        mine = jnp.arange(mps, dtype=jnp.int32)[:, None] == mp_index
        bias = jnp.where(mine, bias_rows[layer][None], 0.0)
        extra = jnp.concatenate(
            [of_features.reshape(mps, -1).astype(BF), bias.astype(BF), counted], axis=1
        )
        extra = jnp.pad(extra, ((0, 0), (0, -extra.shape[1] % (8 * lanes))))
        extra = jnp.broadcast_to(extra[None], (halves,) + extra.shape)
        return extra.reshape(halves * mps, -1, lanes)

    def small_sums(got, extra):
        most = got.shape[1] - extra.shape[1]
        return jnp.sum(got[:, most:].astype(F32), axis=0).reshape(-1)

    def fourier(sent, *others):
        sent = sent.reshape(group, rows, columns)
        got = lax.all_to_all(sent, RING, 0, 0, tiled=True)
        mixed = token_transform(got, mask, token_cos, token_sin, count)
        if others:
            mixed, others = lax.optimization_barrier((mixed, others))
        mixed = lax.all_to_all(mixed, RING, 0, 0, tiled=True).reshape(width, columns)
        return (mixed, *others) if others else mixed

    def gathered(own):
        return [own] + [swapped(own, "side", j) for j in range(1, sides)]

    def reduced(parts):
        terms = [parts[0][0], swapped(parts[0][1], "core")]
        for j in range(1, sides):
            keep, give = parts[j]
            chip = keep.astype(F32) + swapped(give, "core").astype(F32)
            terms.append(swapped(chip.astype(BF), "side", -j))
        return terms

    def added(first, second):
        return (first.astype(F32) + second.astype(F32)).astype(BF)

    def scattered(array):
        return lax.psum_scatter(array, ("half", "rest"), scatter_dimension=0, tiled=True)

    def in_turn(step, firsts):
        done, pairs = [], []
        for i, first in enumerate(firsts):
            if done:
                first, done[-1] = lax.optimization_barrier((first, done[-1]))
            pairs.append((first, swapped(first, "core")))
            done.append(step(*pairs[-1], i))
        return done, pairs

    marks = 2 * labels + scored
    marks = jnp.stack(ordered_by(half, marks, swapped(marks, "half")))
    marks = lax.dynamic_slice_in_dim(marks, half * count, count, 1)
    marks = marks.reshape(halves, count, mps, part, sections)
    marks = lax.dynamic_index_in_dim(marks, section, 4, keepdims=False)
    marks = lax.dynamic_index_in_dim(marks, mp_index, 2, keepdims=False)
    marks = marks.transpose(1, 0, 2).reshape(1, columns)
    local_labels, local_scored = marks // 2, (marks % 2).astype(F32)

    got = send_pencils((inputs, cotangent), section, sections, halves, mps, sorting)
    got = lax.all_to_all(got, PLANE, 0, 0, tiled=True)
    got, other_one = lax.optimization_barrier((got, other_one))
    low, sent = take_pencils(got, 0, 2, halves, mps, count, packed)
    up, _ = lax.optimization_barrier((got, sent))
    flags = [is_first.astype(jnp.int32).reshape(1), (1 - is_first.astype(jnp.int32)).reshape(1)]
    saved, outs, hits = [], [], jnp.zeros((), F32)
    for layer in range(2):
        if layer == 0:
            mixed, other_two, table, biases = fourier(sent, other_two, table, biases)
        else:
            mixed = fourier(sent)
        unit1, inv1, normed = first_norm(mixed, low, unpack, factor, table, layer)
        runs, xs = in_turn(
            lambda a, b, i: ffn(
                flags[layer], a, b, (own_one, own_two), (other_one, other_two), biases, layer
            ),
            gathered(normed),
        )
        terms = reduced([run[:2] for run in runs])
        if layer == 0:
            up, _ = take_pencils(up, 1, 2, halves, mps, count)
            terms, up = lax.optimization_barrier((terms, up))
        result = second_norm(
            unit1,
            terms,
            table,
            layer,
            local_labels,
            local_scored,
            packed if layer == 0 else None,
        )
        unit2, inv2, low, hit = result[:4]
        sent = result[-1]
        outs.append(low)
        hits = hits + jnp.sum(hit)
        saved.append((unit1, inv1, xs, runs, unit2, inv2))
    nothing = jnp.zeros((sections * halves * mps, 16, lanes), BF)
    outputs = send_blocks(outs, nothing, halves, mps, count, part)
    outputs = lax.all_to_all(outputs, SQUARE, 0, 0, tiled=True)

    grads_in, weights_out, smalls, bias_rows = [None, None], [None, None], [None, None], [None, None]
    mix = None
    for layer in (1, 0):
        unit1, inv1, xs, runs, unit2, inv2 = saved[layer]
        result = second_back(up, unit2, inv2, table, layer, mix)
        grad_low, sums2 = result[:2]
        if mix is not None:
            grads_in[1] = result[2]
        backs, gs = in_turn(
            lambda a, b, i: ffn_back(
                flags[layer], a, b, (own_one, own_two), (other_one, other_two), runs[i][3]
            ),
            gathered(grad_low),
        )
        if layer == 0:
            late, _ = lax.optimization_barrier((late, backs[-1][0]))
            weights_out[1] = scattered(added(*late))
        terms = reduced([back[:2] for back in backs])
        keep, give = weight_grads(
            flags[0],
            [x for pair in xs for x in pair],
            [back[2] for back in backs],
            [g for pair in gs for g in pair],
            [run[2] for run in runs],
        )
        terms, keep, give = lax.optimization_barrier((terms, keep, give))
        if layer == 1:
            terms, outputs = lax.optimization_barrier((terms, outputs))
        up, sums1, sent = first_back(grad_low, terms, unit1, inv1, table, layer, packed)
        if layer == 1:
            mixed = fourier(sent)
            give, _ = lax.optimization_barrier((give, mixed))
            late = (keep, swapped(give, "section"))
        else:
            extra = small_rows(1, hits)
            got_late, _ = lax.optimization_barrier((grads_in[1], sent))
            got_late = send_blocks([got_late], extra, halves, mps, count, part)
            got_late = lax.all_to_all(got_late, PLANE, 0, 0, tiled=True)
            both, weights_out[1] = lax.optimization_barrier(
                (added(keep, swapped(give, "section")), weights_out[1])
            )
            weights_out[0] = scattered(both)
            sent, got_late, _ = lax.optimization_barrier((sent, got_late, both))
            mixed = fourier(sent)
            rows_of = feature_count // 2
            outputs = take_blocks(
                (outputs, outputs), (0, 1), 0 * flags[0], rows_of, halves, mps, count, unsorting
            )
            mixed, outputs = lax.optimization_barrier((mixed, outputs))
        mix = (mixed, unpack, factor)
        smalls[layer] = sums1 + sums2
        bias_rows[layer] = sum(back[3][0] for back in backs)
    grads_in[0] = last_mix(mix[0], up, unpack, factor)

    extra = small_rows(0, hits)
    sent = send_blocks(grads_in[:1], extra, halves, mps, count, part)
    got = lax.all_to_all(sent, PLANE, 0, 0, tiled=True)
    mine, other = jnp.where(is_first, got, got_late), jnp.where(is_first, got_late, got)
    other = swapped(other, "section")
    rows_of = feature_count // 2
    input_grads = take_blocks(
        (mine, other), (0, 0), flags[1], rows_of, halves, mps, count, unsorting
    )
    small, step = (small_sums(mine, extra) + small_sums(other, extra)).reshape(-1, lanes), 1
    while step < rests:
        small = small + lax.ppermute(small, "rest", [(i, i ^ step) for i in range(rests)])
        step *= 2
    small, per = small.reshape(-1), 5 * feature_count
    features = small[:per].reshape(5, feature_count)
    bias_sum = small[per : per + units]
    accuracy = jnp.sum(small[per + units : per + units + 3])

    early, late = weights_out
    early, late, _ = lax.optimization_barrier((early, late, sent))
    mine, other = jnp.where(is_first, early, late), jnp.where(is_first, late, early)
    other = swapped(other, "section")
    pair = jnp.stack(ordered(mine, other))
    pair = lax.all_gather(pair, ("half", "rest"), axis=0, tiled=False)
    one, two = widened(pair.reshape((-1,) + pair.shape[-3:]))
    weight_sums = [one, two.reshape(width, units)]

    return (
        outputs,
        input_grads,
        weight_sums[0][None],
        bias_sum[None],
        weight_sums[1][None],
        features[0][None],
        features[1][None],
        features[2][None],
        features[3][None],
        features[4][None],
        accuracy,
    )


def ordered_by(index, own, other):
    return [jnp.where(index == 0, own, other), jnp.where(index == 0, other, own)]


def solution(mesh):
    sizes = mesh.shape
    dims = (sizes["section"], 2, sizes["seq"] // 2, sizes["mp"] // 2, 2)
    names = ("section", ("half", "rest"), ("side", "core"))
    section, seq, mp = names
    placed = (
        P(None, mp, seq),
        P(None, mp, seq),
        P(None, seq),
        P(None, seq),
        P(section, mp, None),
        P(section, mp),
        P(section, None, mp),
        P(section, mp),
        P(section, mp),
        P(section, mp),
        P(section, mp),
        P(section, mp),
    )
    return jax.shard_map(
        shards,
        mesh=Mesh(mesh.devices.reshape(dims), AXES),
        in_specs=placed,
        out_specs=(
            P(section, None, mp, seq),
            P(section, None, mp, seq),
            P(section, mp, None),
            P(section, mp),
            P(section, None, mp),
            P(section, mp),
            P(section, mp),
            P(section, mp),
            P(section, mp),
            P(section, mp),
            P(),
        ),
        check_vma=False,
    )
```

```python
import math

import jax
import jax.numpy as jnp
import ml_dtypes
import numpy as np
from jax import lax
from jax.experimental import pallas as pl
from jax.experimental.pallas import tpu as pltpu
from jax.sharding import Mesh
from jax.sharding import PartitionSpec as P

EPSILON = 1e-05
BF = jnp.bfloat16
F32 = jnp.float32
MIB = 1 << 20
AXES = ("section", "half", "rest", "side", "core")
RING = ("section", "rest", "side", "core")
PLANE = ("half", "side", "core")
SQUARE = ("section", "half", "side", "core")
VMEM = pl.BlockSpec(memory_space=pltpu.VMEM)
HBM = pl.BlockSpec(memory_space=pltpu.HBM)
SMEM = pl.BlockSpec(memory_space=pltpu.SMEM)


def trig(rows, columns, points):
    phases = (rows.astype(np.int64)[:, None] * columns.astype(np.int64)[None, :]) % points
    angles = phases.astype(np.float64) * (2.0 * math.pi / points)
    return np.cos(angles), np.sin(angles)


def low_table(table):
    return table.astype(np.float32).astype(ml_dtypes.bfloat16)


def feature_tables(width, group):
    pairs = width // group // 2
    ids = np.arange(width // 2)
    cos, sin = trig(ids, np.arange(width), width)
    sin[0] = trig(np.array([width // 2]), np.arange(width), width)[0][0]
    packed = np.stack([cos.reshape(group, pairs, width), sin.reshape(group, pairs, width)], 1)
    unpack = np.zeros((width, width), np.float32)
    for k in range(width // 2):
        place = (k // pairs) * 2 * pairs + k % pairs
        if k == 0:
            unpack[0, place] = 1.0
            unpack[width // 2, place + pairs] = 1.0
        else:
            unpack[k, place] = 1.0
            unpack[k, place + pairs] = -1.0
            unpack[width - k, place] = 1.0
            unpack[width - k, place + pairs] = 1.0
    return low_table(packed.reshape(width, width)), low_table(unpack)


def token_tables(sections, rests, mps, part):
    parity, rest, place, i = np.meshgrid(
        np.arange(sections), np.arange(rests), np.arange(mps), np.arange(part), indexing="ij"
    )
    first = rest * sections * mps * part + sections * (place * part + i) + parity
    length = 2 * first.size
    every = np.stack([first, first + length // 2], 3).reshape(-1)
    cos, sin = trig(every, first.reshape(-1), length)
    return low_table(cos), low_table(sin)


def sorting_table(sections, count):
    table = np.zeros((count, count), np.float32)
    order = np.arange(count).reshape(-1, sections).T.reshape(-1)
    table[order, np.arange(count)] = 1.0
    return low_table(table)


def mm(left, right):
    return jnp.dot(left, right, preferred_element_type=F32)


def mm_nt(left, right):
    return lax.dot_general(left, right, (((1,), (1,)), ((), ())), preferred_element_type=F32)


def blocks(size, step):
    step = step if size % step == 0 else size
    return [(i, i + step) for i in range(0, size, step)]


def shape(dims, dtype=BF):
    return jax.ShapeDtypeStruct(tuple(dims), dtype)


def call(kernel, outs, args, specs=None, scratch=(), limit=52, flops=0, **extra):
    return pl.pallas_call(
        kernel,
        out_shape=outs,
        in_specs=specs or [VMEM] * len(args),
        scratch_shapes=list(scratch),
        compiler_params=pltpu.CompilerParams(vmem_limit_bytes=limit * MIB),
        cost_estimate=pl.CostEstimate(flops=flops, bytes_accessed=6 << 20, transcendentals=0),
        **extra,
    )(*args)


def paired(first, second):
    left = lax.broadcasted_iota(jnp.int32, first.shape, 1) < 64
    return (
        jnp.where(left, first, pltpu.roll(second, 64, axis=1)),
        jnp.where(left, pltpu.roll(first, 64, axis=1), second),
    )


def send_pencils(locals_, section, sections, halves, mps, sorting):
    batches, features, tokens = locals_[0].shape
    count, part, rows = batches // halves, tokens // sections // mps, features // 2
    kinds = len(locals_)
    out = shape((halves * mps, kinds * count * rows, 2 * part))
    if part != 64 or mps % 2:
        own = jnp.stack(locals_).reshape(kinds, halves, count, 2, rows, mps, part, sections)
        own = lax.dynamic_index_in_dim(own, section, 7, keepdims=False)
        return own.transpose(1, 5, 0, 2, 4, 3, 6).reshape(out.shape)
    sorting = sorting.reshape(tokens, sections, tokens // sections).transpose(1, 0, 2)

    def kernel(section_ref, *refs):
        x_refs, sorting_ref, o_ref = refs[:kinds], refs[kinds], refs[kinds + 1]
        for kind in range(kinds):
            for seq in range(batches):
                half, m = seq // count, seq % count
                values = mm(x_refs[kind][seq], sorting_ref[0])
                for place in range(0, mps, 2):
                    a = place * part
                    pair = paired(values[:rows, a : a + 128], values[rows:, a : a + 128])
                    for k in range(2):
                        d, at = half * mps + place + k, (kind * count + m) * rows
                        o_ref[d, at : at + rows] = pair[k].astype(BF)

    return pl.pallas_call(
        kernel,
        grid_spec=pltpu.PrefetchScalarGridSpec(
            num_scalar_prefetch=1,
            grid=(1,),
            in_specs=[pl.BlockSpec(locals_[0].shape, lambda i, s: (0, 0, 0))] * kinds
            + [pl.BlockSpec((1,) + sorting.shape[1:], lambda i, s: (s[0], 0, 0))],
            out_specs=pl.BlockSpec(out.shape, lambda i, s: (0, 0, 0)),
        ),
        out_shape=out,
        compiler_params=pltpu.CompilerParams(vmem_limit_bytes=52 * MIB),
    )(section.reshape(1), *locals_, sorting)


def take_pencils(got, kind, kinds, halves, mps, count, packed=None):
    rows, part = got.shape[1] // count // kinds, got.shape[2] // 2
    width, columns = mps * 2 * rows, count * halves * part
    if part != 64:
        got = got.reshape(halves, mps, kinds, count, rows, 2, part)[:, :, kind]
        low = got.transpose(1, 4, 3, 2, 0, 5).reshape(width, columns)
        return low, None if packed is None else mm(packed, low).astype(BF)

    def kernel(*refs):
        x_ref, o_ref = refs[0], refs[1 if packed is None else 2]
        for mp in range(mps):
            for m in range(count):
                at = (kind * count + m) * rows
                pair = paired(*(x_ref[h * mps + mp, at : at + rows].astype(F32) for h in range(2)))
                for k in range(2):
                    a = (mp * 2 + k) * rows
                    o_ref[a : a + rows, m * 128 : (m + 1) * 128] = pair[k].astype(BF)
        if packed is not None:
            refs[3][...] = mm(refs[1][...], o_ref[...]).astype(BF)

    low = shape((width, columns))
    if packed is None:
        return call(kernel, low, (got,)), None
    return call(kernel, (low, low), (got, packed))


def send_blocks(layers, extra, halves, mps, count, part):
    width, columns = layers[0].shape
    rows, kinds = width // mps // 2, len(layers)
    more = extra.shape[1]
    out = shape((kinds * halves * mps, count * rows + more, 2 * part))
    if part != 64:
        sent = jnp.stack(layers).reshape(kinds, mps, 2, rows, count, halves, part)
        sent = sent.transpose(0, 5, 1, 4, 3, 2, 6).reshape(-1, count * rows, 2 * part)
        return jnp.concatenate([sent, extra], axis=1)

    def kernel(*refs):
        o_ref = refs[-1]
        o_ref[:, count * rows :] = refs[kinds][...]
        for layer in range(kinds):
            for mp in range(mps):
                for m in range(count):
                    a, b = mp * 2 * rows, m * 128
                    pair = paired(
                        refs[layer][a : a + rows, b : b + 128].astype(F32),
                        refs[layer][a + rows : a + 2 * rows, b : b + 128].astype(F32),
                    )
                    for k in range(2):
                        d = (layer * halves + k) * mps + mp
                        o_ref[d, m * rows : (m + 1) * rows] = pair[k].astype(BF)

    return call(kernel, out, (*layers, extra))


def take_blocks(got, places, flipped, rows, halves, mps, count, unsorting):
    part = got[0].shape[-1] // 2
    out = (1, halves * count, 2 * rows, 2 * mps * part)
    got = [array.reshape(-1, halves, mps, array.shape[-2], 2 * part) for array in got]
    if part != 64 or mps % 2:
        both = jnp.stack([array[place, :, :, : count * rows] for array, place in zip(got, places)])
        both = jnp.where(flipped == 1, both[::-1], both)
        both = both.reshape(2, halves, mps, count, rows, 2, part)
        return both.transpose(1, 3, 5, 4, 2, 6, 0).reshape(out).astype(F32)
    tables = unsorting.reshape(2, -1, out[3])
    tables = jnp.stack([unsorting, tables[::-1].reshape(unsorting.shape)])

    def kernel(flag_ref, a_ref, b_ref, table_ref, o_ref, s_ref):
        for x, x_ref in enumerate((a_ref, b_ref)):
            for place in range(0, mps, 2):
                a = x * mps * part + place * part
                for m in range(count):
                    pair = paired(
                        *(
                            x_ref[0, 0, place + k, m * rows : (m + 1) * rows].astype(F32)
                            for k in range(2)
                        )
                    )
                    for k in range(2):
                        s_ref[(2 * m + k) * rows : (2 * m + k + 1) * rows, a : a + 128] = pair[
                            k
                        ].astype(BF)
        for m in range(count):
            o_ref[0, m] = mm(s_ref[2 * m * rows : 2 * (m + 1) * rows], table_ref[0])

    def block(place):
        return pl.BlockSpec((1, 1) + got[0].shape[2:], lambda i, s: (place, i, 0, 0, 0))

    return pl.pallas_call(
        kernel,
        grid_spec=pltpu.PrefetchScalarGridSpec(
            num_scalar_prefetch=1,
            grid=(halves,),
            in_specs=[
                block(places[0]),
                block(places[1]),
                pl.BlockSpec((1,) + unsorting.shape, lambda i, s: (s[0], 0, 0)),
            ],
            out_specs=pl.BlockSpec((1, count) + out[2:], lambda i, s: (i, 0, 0, 0)),
            scratch_shapes=[pltpu.VMEM((count * 2 * rows, out[3]), BF)],
        ),
        out_shape=shape((halves, count) + out[2:], F32),
        compiler_params=pltpu.CompilerParams(vmem_limit_bytes=52 * MIB),
    )(flipped, *got, tables).reshape(out)


def token_transform(data, mask, cos, sin, count):
    group, rows, columns = data.shape
    length, spread = cos.shape
    tokens = columns // count
    part = tokens // 2
    if part != 64:
        x = data.reshape(group, rows, count, tokens).transpose(2, 1, 0, 3)
        x = x.reshape(count * rows, length)
        mixed = [
            jnp.where(mask > 0.0, mm(x[:, a:b], cos[a:b]), mm(x[:, a:b], sin[a:b]))
            for a, b in ((0, spread), (spread, length))
        ]
        both = jnp.stack([mixed[0] + mixed[1], mixed[0] - mixed[1]]).astype(BF)
        both = both.reshape(2, count, rows, group, part).transpose(3, 2, 1, 0, 4)
        return both.reshape(data.shape)
    step = 256

    def kernel(d_ref, m_ref, c_hbm, s_hbm, o_ref, x_ref, c_ref, s_ref, sems):
        copies = []
        for n in range(spread // step):
            window = slice(n * step, (n + 1) * step)
            copies.append(
                [
                    pltpu.make_async_copy(src.at[:, window], dst.at[n], sems.at[n, k])
                    for k, (src, dst) in enumerate(((c_hbm, c_ref), (s_hbm, s_ref)))
                ]
            )
            for copy in copies[-1]:
                copy.start()
        for m in range(count):
            for g in range(group):
                x_ref[m * rows : (m + 1) * rows, g * tokens : (g + 1) * tokens] = d_ref[
                    g, :, m * tokens : (m + 1) * tokens
                ]
        keep = m_ref[...] > 0.0
        for n in range(spread // step):
            for copy in copies[n]:
                copy.wait()
            even, odd = (
                jnp.where(
                    keep,
                    mm(x_ref[:, a : a + spread], c_ref[n, a : a + spread]),
                    mm(x_ref[:, a : a + spread], s_ref[n, a : a + spread]),
                )
                for a in (0, spread)
            )
            total, other = even + odd, even - odd
            for p in range(step // 128):
                pair = paired(total[:, p * 128 : (p + 1) * 128], other[:, p * 128 : (p + 1) * 128])
                for k in range(2):
                    g = n * (step // part) + 2 * p + k
                    low = pair[k].astype(BF)
                    for m in range(count):
                        o_ref[g, :, m * tokens : (m + 1) * tokens] = low[m * rows : (m + 1) * rows]

    return call(
        kernel,
        shape(data.shape),
        (data, mask, cos, sin),
        [VMEM, VMEM, HBM, HBM],
        [pltpu.VMEM((count * rows, length), BF)]
        + [pltpu.VMEM((spread // step, length, step), BF)] * 2
        + [pltpu.SemaphoreType.DMA((spread // step, 2))],
        limit=52,
        flops=4 * count * rows * length * spread,
    )


def standardize(values):
    average = jnp.mean(values, axis=0, keepdims=True)
    centered = values - average
    spread = jnp.mean(centered * centered, axis=0, keepdims=True)
    inverse = lax.rsqrt(spread + EPSILON)
    return centered * inverse, inverse


def norm_back(upstream, standard, inverse, scaling):
    weighted = upstream * scaling
    return inverse * (
        weighted
        - jnp.mean(weighted, axis=0, keepdims=True)
        - standard * jnp.mean(weighted * standard, axis=0, keepdims=True)
    )


def column(table, layer, i):
    k = layer * 5 + i
    return table[:, k : k + 1]


def first_norm(got, low, unpack, factor, table, layer):
    width, columns = low.shape

    def kernel(r_ref, x_ref, unpack_ref, table_ref, unit_ref, inverse_ref, low_ref):
        mixed = mm(unpack_ref[...], r_ref[...])
        table = table_ref[...].T
        gain, shift = column(table, layer, 1), column(table, layer, 2)
        for a, b in blocks(columns, 128):
            unit, inverse = standardize(x_ref[:, a:b].astype(F32) + mixed[:, a:b] * factor)
            unit_ref[:, a:b] = unit.astype(BF)
            inverse_ref[:, a:b] = inverse
            low_ref[:, a:b] = (unit * gain + shift).astype(BF)

    outs = (shape((width, columns)), shape((1, columns), F32), shape((width, columns)))
    return call(kernel, outs, (got, low, unpack, table), flops=2 * width * width * columns)


def second_norm(unit1, parts, table, layer, labels, scored, packed):
    width, columns = unit1.shape
    count = len(parts)

    def kernel(*refs):
        unit1_ref, part_refs = refs[0], refs[1 : 1 + count]
        table_ref, labels_ref, scored_ref = refs[1 + count : 4 + count]
        vectors = table_ref[...].T
        bias, gain1, shift1, gain2, shift2 = (column(vectors, layer, i) for i in range(5))
        bias = bias + shift1
        unit_ref, inverse_ref, low_ref, hits_ref = refs[len(refs) - outs_count :][:4]
        for a, b in blocks(columns, 128):
            values = unit1_ref[:, a:b].astype(F32) * gain1 + bias
            for part in part_refs:
                values = values + part[:, a:b].astype(F32)
            unit, inverse = standardize(values)
            unit_ref[:, a:b] = unit.astype(BF)
            inverse_ref[:, a:b] = inverse
            out = unit * gain2 + shift2
            low_ref[:, a:b] = out.astype(BF)
            exponent = jnp.exp(out)
            match = lax.broadcasted_iota(jnp.int32, out.shape, 0) == labels_ref[:, a:b]
            picked = jnp.sum(jnp.where(match, exponent, 0.0), axis=0, keepdims=True)
            total = jnp.sum(exponent, axis=0, keepdims=True)
            hits_ref[:, a:b] = picked / total * scored_ref[:, a:b]
        if packed is not None:
            refs[-1][...] = mm(refs[4 + count][...], low_ref[...]).astype(BF)

    row = shape((1, columns), F32)
    outs = [shape((width, columns)), row, shape((width, columns)), row]
    args = [unit1, *parts, table, labels, scored]
    if packed is not None:
        outs, args = outs + [shape((width, columns))], args + [packed]
    outs_count = len(outs)
    return call(kernel, tuple(outs), tuple(args), flops=2 * width * width * columns)


def row_sums(terms, width):
    total = jnp.zeros((8, width), F32)
    for row, term in terms:
        mark = (lax.broadcasted_iota(jnp.int32, (8, term.shape[1]), 0) == row).astype(BF)
        total = total + mm_nt(mark, term)
    return total


def second_back(up, unit, inverse, table, layer, mix=None):
    width, columns = unit.shape

    def kernel(*refs):
        up_ref, unit_ref, inverse_ref, table_ref = refs[:4]
        if mix is None:
            low_ref, sums_ref, product_ref = refs[4:]
            source_ref = up_ref
        else:
            got_ref, unpack_ref, low_ref, sums_ref, source_ref, product_ref = refs[4:]
            mixed = mm(unpack_ref[...], got_ref[...])
        gain = column(table_ref[...].T, layer, 3)
        for a, b in blocks(columns, 128):
            if mix is not None:
                values = up_ref[:, a:b].astype(F32) + mixed[:, a:b] * mix[2]
                source_ref[:, a:b] = values.astype(BF)
            values, unit = source_ref[:, a:b].astype(F32), unit_ref[:, a:b].astype(F32)
            low_ref[:, a:b] = norm_back(values, unit, inverse_ref[:, a:b], gain).astype(BF)
            product_ref[:, a:b] = (values * unit).astype(BF)
        sums_ref[...] = row_sums(
            ((0, low_ref[...]), (3, product_ref[...]), (4, source_ref[...])), width
        )

    outs = (shape(unit.shape), shape((8, width), F32))
    args = (up, unit, inverse, table)
    if mix is not None:
        outs, args = outs + (shape(unit.shape),), args + mix[:2]
    scratch = [pltpu.VMEM(unit.shape, BF)]
    return call(kernel, outs, args, None, scratch, flops=2 * width * width * columns)


def first_back(grad_second, parts, unit, inverse, table, layer, packed):
    width, columns = unit.shape
    count = len(parts)

    def kernel(second_ref, *refs):
        part_refs = refs[:count]
        unit_ref, inverse_ref, table_ref, packed_ref = refs[count : count + 4]
        low_ref, sums_ref, sent_ref, product_ref, normed_ref = refs[count + 4 :]
        gain = column(table_ref[...].T, layer, 1)
        for a, b in blocks(columns, 128):
            values, unit = second_ref[:, a:b].astype(F32), unit_ref[:, a:b].astype(F32)
            for part in part_refs:
                values = values + part[:, a:b].astype(F32)
            low_ref[:, a:b] = norm_back(values, unit, inverse_ref[:, a:b], gain).astype(BF)
            product_ref[:, a:b] = (values * unit).astype(BF)
            normed_ref[:, a:b] = values.astype(BF)
        sent_ref[...] = mm(packed_ref[...], low_ref[...]).astype(BF)
        sums_ref[...] = row_sums(((1, product_ref[...]), (2, normed_ref[...])), width)

    outs = (shape(unit.shape), shape((8, width), F32), shape(unit.shape))
    args = (grad_second, *parts, unit, inverse, table, packed)
    scratch = [pltpu.VMEM(unit.shape, BF)] * 2
    return call(kernel, outs, args, None, scratch, flops=2 * width * width * columns)


def last_mix(got, grad, unpack, factor):
    width, columns = grad.shape

    def kernel(got_ref, grad_ref, unpack_ref, o_ref):
        mixed = mm(unpack_ref[...], got_ref[...])
        o_ref[...] = (grad_ref[...].astype(F32) + mixed * factor).astype(BF)

    args = (got, grad, unpack)
    return call(kernel, shape(grad.shape), args, flops=2 * width * width * columns)


def gelu_parts(x):
    cdf = 0.5 + 0.5 * lax.erf(x * (1.0 / math.sqrt(2.0)))
    return cdf, jnp.exp(-0.5 * x * x) * (1.0 / math.sqrt(2.0 * math.pi))


def mm_tn(left, right):
    return lax.dot_general(left, right, (((0,), (0,)), ((), ())), preferred_element_type=F32)


def staged(pairs, sems):
    copies = [
        pltpu.make_async_copy(src, dst, sems.at[i]) for i, (src, dst) in enumerate(pairs)
    ]
    for copy in copies:
        copy.start()
    return copies


def chosen(flag, pairs, sems):
    copies = []
    for i, (sources, target) in enumerate(pairs):
        either = [pltpu.make_async_copy(src, target, sems.at[i]) for src in sources]

        @pl.when(flag == 1)
        def _():
            either[0].start()

        @pl.when(flag != 1)
        def _():
            either[1].start()

        copies.append(either[0])
    return copies


def ffn(flag, first, second, own, other, biases, layer):
    width, columns = first.shape
    units = own[0].shape[0]
    steps = blocks(units, 256)

    def kernel(flag_ref, a_ref, b_ref, own1, own2, other1, other2, bias_ref, *refs):
        oa_ref, ob_ref, act_hbm, slope_hbm, one_ref, two_ref, act_ref, slope_ref, sems, sent = refs
        copies = chosen(
            flag_ref[0],
            [((own1.at[a:b], other1.at[a:b]), one_ref.at[a:b]) for a, b in steps]
            + [((own2, other2), two_ref)],
            sems,
        )
        x = jnp.concatenate([a_ref[...], b_ref[...]], axis=1)
        bias = bias_ref[...].T
        writes = []
        for i, (a, b) in enumerate(steps):
            copies[i].wait()
            hidden = mm(one_ref[a:b], x) + bias[a:b, layer : layer + 1]
            cdf, density = gelu_parts(hidden)
            act_ref[a:b] = (hidden * cdf).astype(BF)
            slope_ref[a:b] = (cdf + hidden * density).astype(BF)
            for k, (src, dst) in enumerate(((act_ref, act_hbm), (slope_ref, slope_hbm))):
                writes.append(pltpu.make_async_copy(src.at[a:b], dst.at[a:b], sent.at[i, k]))
                writes[-1].start()
        copies[-1].wait()
        for a, b in blocks(width, 256):
            part = mm(two_ref[a:b], act_ref[...])
            oa_ref[a:b] = part[:, :columns].astype(BF)
            ob_ref[a:b] = part[:, columns:].astype(BF)
        for write in writes:
            write.wait()

    half, full = shape((width, columns)), shape((units, 2 * columns))
    return call(
        kernel,
        (half, half, full, full),
        (flag, first, second, *own, *other, biases),
        [SMEM] + [VMEM] * 2 + [HBM] * 4 + [VMEM],
        [
            pltpu.VMEM((units, width), BF),
            pltpu.VMEM((width, units), BF),
            pltpu.VMEM(full.shape, BF),
            pltpu.VMEM(full.shape, BF),
            pltpu.SemaphoreType.DMA((len(steps) + 1,)),
            pltpu.SemaphoreType.DMA((len(steps), 2)),
        ],
        limit=52,
        flops=8 * width * units * columns,
        out_specs=(VMEM, VMEM, HBM, HBM),
    )


def ffn_back(flag, first, second, own, other, slope):
    width, columns = first.shape
    units = own[0].shape[0]
    steps = blocks(units, 256)

    def kernel(flag_ref, a_ref, b_ref, own1, own2, other1, other2, slope_hbm, *refs):
        oa_ref, ob_ref, pre_hbm, sums_ref, one_ref, two_ref, pre_ref, slope_ref, sems, sent = refs
        copies = chosen(
            flag_ref[0],
            [((own2, other2), two_ref)]
            + [((slope_hbm.at[a:b],) * 2, slope_ref.at[a:b]) for a, b in steps]
            + [((own1, other1), one_ref)],
            sems,
        )
        g = jnp.concatenate([a_ref[...], b_ref[...]], axis=1)
        copies[0].wait()
        writes = []
        for i, (a, b) in enumerate(steps):
            grad = mm_tn(two_ref[:, a:b], g)
            copies[1 + i].wait()
            pre_ref[a:b] = (grad * slope_ref[a:b].astype(F32)).astype(BF)
            writes.append(pltpu.make_async_copy(pre_ref.at[a:b], pre_hbm.at[a:b], sent.at[i]))
            writes[-1].start()
        copies[-1].wait()
        for a, b in blocks(width, 256):
            part = mm_tn(one_ref[:, a:b], pre_ref[...])
            oa_ref[a:b] = part[:, :columns].astype(BF)
            ob_ref[a:b] = part[:, columns:].astype(BF)
        sums_ref[...] = row_sums(((0, pre_ref[...]),), units)
        for write in writes:
            write.wait()

    half, full = shape((width, columns)), shape((units, 2 * columns))
    return call(
        kernel,
        (half, half, full, shape((8, units), F32)),
        (flag, first, second, *own, *other, slope),
        [SMEM] + [VMEM] * 2 + [HBM] * 5,
        [
            pltpu.VMEM((units, width), BF),
            pltpu.VMEM((width, units), BF),
            pltpu.VMEM(full.shape, BF),
            pltpu.VMEM(full.shape, BF),
            pltpu.SemaphoreType.DMA((len(steps) + 2,)),
            pltpu.SemaphoreType.DMA((len(steps),)),
        ],
        limit=52,
        flops=8 * width * units * columns,
        out_specs=(VMEM, VMEM, HBM, VMEM),
    )


def weight_grad(flag, lefts, rights):
    rows, width = lefts[0][0].shape[0], rights[0][0].shape[0]
    sizes = [[array.shape[1] for array in either] for either in (lefts[1], rights[1])]
    tokens = sum(sizes[0])
    parts = [(side, either) for side in range(2) for either in range(2)]
    lists = {(side, either): (lefts, rights)[side][either] for side, either in parts}

    def kernel(flag_ref, *refs):
        inputs, (out_ref, left_ref, right_ref, sems) = refs[:-4], refs[-4:]
        at, groups = 0, {}
        for part in parts:
            groups[part] = inputs[at : at + len(lists[part])]
            at += len(lists[part])
        wholes = (left_ref, right_ref)

        def fill(either, act):
            k = 0
            for side in range(2):
                place = 0
                for src in groups[side, either]:
                    step = src.shape[1]
                    target = wholes[side].at[:, place : place + step]
                    act(pltpu.make_async_copy(src, target, sems.at[either, k]))
                    place, k = place + step, k + 1

        for act in (lambda copy: copy.start(), lambda copy: copy.wait()):
            for either in range(2):

                @pl.when((flag_ref[0] == 1) == (either == 0))
                def _():
                    fill(either, act)

        for a, b in blocks(rows, 256):
            out_ref[a:b] = mm_nt(left_ref[a:b], right_ref[...]).astype(BF)

    count = max(len(lists[0, e]) + len(lists[1, e]) for e in range(2))
    args = [array for part in parts for array in lists[part]]
    return call(
        kernel,
        shape((rows, width)),
        (flag, *args),
        [SMEM] + [HBM] * len(args),
        [
            pltpu.VMEM((rows, tokens), BF),
            pltpu.VMEM((width, tokens), BF),
            pltpu.SemaphoreType.DMA((2, count)),
        ],
        limit=52,
        flops=2 * width * rows * tokens,
    )


def weight_grads(flag, xs, pres, gs, acts):
    units, width = pres[0].shape[0], xs[0].shape[0]
    if units != width:
        pre, x, g, act = (jnp.concatenate(group, axis=1) for group in (pres, xs, gs, acts))
        one, two = mm_nt(pre, x).astype(BF), mm_nt(g, act).astype(BF).reshape(units, width)
        return jnp.where(flag == 1, one, two), jnp.where(flag == 1, two, one)
    give = weight_grad(flag, (gs, pres), (acts, xs))
    keep = weight_grad(flag, (pres, gs), (xs, acts))
    return keep, give


def widened(flag, mine, other):
    units, width = mine.shape
    steps = blocks(units, 256)

    def kernel(flag_ref, mine_hbm, other_hbm, one_hbm, two_hbm, in_ref, out_ref, sems, sent):
        sources = ((mine_hbm, other_hbm), (other_hbm, mine_hbm))
        copies = chosen(
            flag_ref[0],
            [
                (tuple(src.at[a:b] for src in pair), in_ref.at[k, a:b])
                for k, pair in enumerate(sources)
                for a, b in steps
            ],
            sems,
        )
        writes = []
        for k, target in enumerate((one_hbm, two_hbm)):
            for i, (a, b) in enumerate(steps):
                copies[k * len(steps) + i].wait()
                out_ref[k, a:b] = in_ref[k, a:b].astype(F32)
                writes.append(
                    pltpu.make_async_copy(out_ref.at[k, a:b], target.at[a:b], sent.at[k, i])
                )
                writes[-1].start()
        for write in writes:
            write.wait()

    return call(
        kernel,
        (shape((units, width), F32),) * 2,
        (flag, mine, other),
        [SMEM] + [HBM] * 2,
        [
            pltpu.VMEM((2, units, width), BF),
            pltpu.VMEM((2, units, width), F32),
            pltpu.SemaphoreType.DMA((2 * len(steps),)),
            pltpu.SemaphoreType.DMA((2, len(steps))),
        ],
        out_specs=(HBM, HBM),
    )


def shards(
    inputs,
    cotangent,
    labels,
    scored,
    expand_weight,
    expand_bias,
    reduce_weight,
    reduce_bias,
    first_gain,
    first_shift,
    second_gain,
    second_shift,
):
    batches, feature_count, token_count = inputs.shape
    sections, halves, rests, sides, cores = (lax.axis_size(axis) for axis in AXES)
    mps = sides * cores
    group = sections * rests * mps
    width = feature_count * mps
    length = token_count * halves * rests
    units = expand_weight.shape[1]
    count = batches // halves
    part = token_count // sections // mps
    columns = count * halves * part
    rows = width // group
    factor = 1.0 / math.sqrt(length * width)
    section, half, rest, side, core = (lax.axis_index(axis) for axis in AXES)
    mp_index = side * cores + core
    is_first = section == 0

    packed, unpack = (jnp.asarray(t) for t in feature_tables(width, group))
    token_cos, token_sin = (jnp.asarray(t) for t in token_tables(sections, rests, mps, part))
    sorting = sorting_table(sections, token_count)
    unsorting, sorting = jnp.asarray(sorting.T), jnp.asarray(sorting)
    row_ids = jnp.arange(count * rows, dtype=jnp.int32) % rows
    corner = (section == 0) & (rest == 0) & (mp_index == 0)
    mask = (row_ids < rows // 2) | ((row_ids == rows // 2) & corner)
    mask = mask.astype(F32)[:, None]

    def swapped(array, axis, by=1):
        size = lax.axis_size(axis)
        return lax.ppermute(array, axis, [(i, (i + by) % size) for i in range(size)])

    own_one, own_two = expand_weight[0], reduce_weight[0]
    other_one, other_two = swapped(own_one, "section"), swapped(own_two, "section")

    def ordered(own, other):
        return [jnp.where(is_first, own, other), jnp.where(is_first, other, own)]

    small = [expand_bias, reduce_bias, first_gain, first_shift, second_gain, second_shift]
    small = jnp.concatenate([vector[0] for vector in small])
    small = jnp.stack(ordered(small, swapped(small, "section")))
    biases = jnp.pad(small[:, :units], ((0, 8 - sections), (0, 0)))
    vectors = small[:, units:].reshape(sections * 5, 1, feature_count)
    vectors = jnp.concatenate(ordered_by(core, vectors, swapped(vectors, "core")), axis=1)
    chips = [swapped(vectors, "side", -j) if j else vectors for j in range(sides)]
    chips = jnp.stack(chips, axis=1)
    order = [(i - side) % sides for i in range(sides)]
    table = jnp.stack(
        [lax.dynamic_index_in_dim(chips, i, 1, keepdims=False) for i in order], axis=1
    ).reshape(sections * 5, width)
    table = jnp.pad(table, ((0, -table.shape[0] % 16), (0, 0)))

    lanes = 2 * part

    def small_rows(layer, hits):
        high = hits.astype(BF)
        middle = (hits - high.astype(F32)).astype(BF)
        lowest = (hits - high.astype(F32) - middle.astype(F32)).astype(BF)
        counted = jnp.broadcast_to(jnp.stack([high, middle, lowest])[None], (mps, 3))
        of_features = smalls[layer][:5].reshape(5, mps, feature_count).transpose(1, 0, 2)
        mine = jnp.arange(mps, dtype=jnp.int32)[:, None] == mp_index
        bias = jnp.where(mine, bias_rows[layer][None], 0.0)
        extra = jnp.concatenate(
            [of_features.reshape(mps, -1).astype(BF), bias.astype(BF), counted], axis=1
        )
        extra = jnp.pad(extra, ((0, 0), (0, -extra.shape[1] % (8 * lanes))))
        extra = jnp.broadcast_to(extra[None], (halves,) + extra.shape)
        return extra.reshape(halves * mps, -1, lanes)

    def small_sums(got, extra):
        most = got.shape[1] - extra.shape[1]
        return jnp.sum(got[:, most:].astype(F32), axis=0).reshape(-1)

    def fourier(sent, *others):
        sent = sent.reshape(group, rows, columns)
        got = lax.all_to_all(sent, RING, 0, 0, tiled=True)
        mixed = token_transform(got, mask, token_cos, token_sin, count)
        if others:
            mixed, others = lax.optimization_barrier((mixed, others))
        mixed = lax.all_to_all(mixed, RING, 0, 0, tiled=True).reshape(width, columns)
        return (mixed, *others) if others else mixed

    def gathered(own):
        return [own] + [swapped(own, "side", j) for j in range(1, sides)]

    def reduced(parts):
        terms = [parts[0][0], swapped(parts[0][1], "core")]
        for j in range(1, sides):
            keep, give = parts[j]
            chip = keep.astype(F32) + swapped(give, "core").astype(F32)
            terms.append(swapped(chip.astype(BF), "side", -j))
        return terms

    def added(first, second):
        return (first.astype(F32) + second.astype(F32)).astype(BF)

    def scattered(array):
        return lax.psum_scatter(array, ("half", "rest"), scatter_dimension=0, tiled=True)

    def in_turn(step, firsts):
        done, pairs = [], []
        for i, first in enumerate(firsts):
            if done:
                first, done[-1] = lax.optimization_barrier((first, done[-1]))
            pairs.append((first, swapped(first, "core")))
            done.append(step(*pairs[-1], i))
        return done, pairs

    marks = 2 * labels + scored
    marks = jnp.stack(ordered_by(half, marks, swapped(marks, "half")))
    marks = lax.dynamic_slice_in_dim(marks, half * count, count, 1)
    marks = marks.reshape(halves, count, mps, part, sections)
    marks = lax.dynamic_index_in_dim(marks, section, 4, keepdims=False)
    marks = lax.dynamic_index_in_dim(marks, mp_index, 2, keepdims=False)
    marks = marks.transpose(1, 0, 2).reshape(1, columns)
    local_labels, local_scored = marks // 2, (marks % 2).astype(F32)

    got = send_pencils((inputs, cotangent), section, sections, halves, mps, sorting)
    got = lax.all_to_all(got, PLANE, 0, 0, tiled=True)
    got, other_one = lax.optimization_barrier((got, other_one))
    low, sent = take_pencils(got, 0, 2, halves, mps, count, packed)
    up, _ = lax.optimization_barrier((got, sent))
    flags = [is_first.astype(jnp.int32).reshape(1), (1 - is_first.astype(jnp.int32)).reshape(1)]
    saved, outs, hits = [], [], jnp.zeros((), F32)
    for layer in range(2):
        if layer == 0:
            mixed, other_two, table, biases = fourier(sent, other_two, table, biases)
        else:
            mixed = fourier(sent)
        unit1, inv1, normed = first_norm(mixed, low, unpack, factor, table, layer)
        runs, xs = in_turn(
            lambda a, b, i: ffn(
                flags[layer], a, b, (own_one, own_two), (other_one, other_two), biases, layer
            ),
            gathered(normed),
        )
        terms = reduced([run[:2] for run in runs])
        if layer == 0:
            up, _ = take_pencils(up, 1, 2, halves, mps, count)
            terms, up = lax.optimization_barrier((terms, up))
        result = second_norm(
            unit1,
            terms,
            table,
            layer,
            local_labels,
            local_scored,
            packed if layer == 0 else None,
        )
        unit2, inv2, low, hit = result[:4]
        sent = result[-1]
        outs.append(low)
        hits = hits + jnp.sum(hit)
        saved.append((unit1, inv1, xs, runs, unit2, inv2))
    nothing = jnp.zeros((sections * halves * mps, 16, lanes), BF)
    outputs = send_blocks(outs, nothing, halves, mps, count, part)
    outputs = lax.all_to_all(outputs, SQUARE, 0, 0, tiled=True)

    grads_in, weights_out, smalls, bias_rows = [None, None], [None, None], [None, None], [None, None]
    mix = None
    for layer in (1, 0):
        unit1, inv1, xs, runs, unit2, inv2 = saved[layer]
        result = second_back(up, unit2, inv2, table, layer, mix)
        grad_low, sums2 = result[:2]
        if mix is not None:
            grads_in[1] = result[2]
        backs, gs = in_turn(
            lambda a, b, i: ffn_back(
                flags[layer], a, b, (own_one, own_two), (other_one, other_two), runs[i][3]
            ),
            gathered(grad_low),
        )
        if layer == 0:
            late, _ = lax.optimization_barrier((late, backs[-1][0]))
            weights_out[1] = scattered(added(*late))
        terms = reduced([back[:2] for back in backs])
        keep, give = weight_grads(
            flags[0],
            [x for pair in xs for x in pair],
            [back[2] for back in backs],
            [g for pair in gs for g in pair],
            [run[2] for run in runs],
        )
        terms, keep, give = lax.optimization_barrier((terms, keep, give))
        if layer == 1:
            terms, outputs = lax.optimization_barrier((terms, outputs))
        up, sums1, sent = first_back(grad_low, terms, unit1, inv1, table, layer, packed)
        if layer == 1:
            mixed = fourier(sent)
            give, _ = lax.optimization_barrier((give, mixed))
            late = (keep, swapped(give, "section"))
        else:
            extra = small_rows(1, hits)
            got_late, _ = lax.optimization_barrier((grads_in[1], sent))
            got_late = send_blocks([got_late], extra, halves, mps, count, part)
            got_late = lax.all_to_all(got_late, PLANE, 0, 0, tiled=True)
            both, weights_out[1] = lax.optimization_barrier(
                (added(keep, swapped(give, "section")), weights_out[1])
            )
            weights_out[0] = scattered(both)
            sent, got_late, _ = lax.optimization_barrier((sent, got_late, both))
            mixed = fourier(sent)
            rows_of = feature_count // 2
            outputs = take_blocks(
                (outputs, outputs), (0, 1), 0 * flags[0], rows_of, halves, mps, count, unsorting
            )
            mixed, outputs = lax.optimization_barrier((mixed, outputs))
        mix = (mixed, unpack, factor)
        smalls[layer] = sums1 + sums2
        bias_rows[layer] = sum(back[3][0] for back in backs)
    grads_in[0] = last_mix(mix[0], up, unpack, factor)

    extra = small_rows(0, hits)
    sent = send_blocks(grads_in[:1], extra, halves, mps, count, part)
    got = lax.all_to_all(sent, PLANE, 0, 0, tiled=True)
    mine, other = jnp.where(is_first, got, got_late), jnp.where(is_first, got_late, got)
    other = swapped(other, "section")
    rows_of = feature_count // 2
    input_grads = take_blocks(
        (mine, other), (0, 0), flags[1], rows_of, halves, mps, count, unsorting
    )
    small, step = (small_sums(mine, extra) + small_sums(other, extra)).reshape(-1, lanes), 1
    while step < rests:
        small = small + lax.ppermute(small, "rest", [(i, i ^ step) for i in range(rests)])
        step *= 2
    small, per = small.reshape(-1), 5 * feature_count
    features = small[:per].reshape(5, feature_count)
    bias_sum = small[per : per + units]
    accuracy = jnp.sum(small[per + units : per + units + 3])

    early, late = weights_out
    early, late, _ = lax.optimization_barrier((early, late, sent))
    mine, other = jnp.where(is_first, early, late), jnp.where(is_first, late, early)
    other = swapped(other, "section")
    mine, other = (
        lax.all_gather(shard, ("half", "rest"), axis=0, tiled=True) for shard in (mine, other)
    )
    one, two = widened(flags[0], mine, other)
    weight_sums = [one, two.reshape(width, units)]

    return (
        outputs,
        input_grads,
        weight_sums[0][None],
        bias_sum[None],
        weight_sums[1][None],
        features[0][None],
        features[1][None],
        features[2][None],
        features[3][None],
        features[4][None],
        accuracy,
    )


def ordered_by(index, own, other):
    return [jnp.where(index == 0, own, other), jnp.where(index == 0, other, own)]


def solution(mesh):
    sizes = mesh.shape
    dims = (sizes["section"], 2, sizes["seq"] // 2, sizes["mp"] // 2, 2)
    names = ("section", ("half", "rest"), ("side", "core"))
    section, seq, mp = names
    placed = (
        P(None, mp, seq),
        P(None, mp, seq),
        P(None, seq),
        P(None, seq),
        P(section, mp, None),
        P(section, mp),
        P(section, None, mp),
        P(section, mp),
        P(section, mp),
        P(section, mp),
        P(section, mp),
        P(section, mp),
    )
    return jax.shard_map(
        shards,
        mesh=Mesh(mesh.devices.reshape(dims), AXES),
        in_specs=placed,
        out_specs=(
            P(section, None, mp, seq),
            P(section, None, mp, seq),
            P(section, mp, None),
            P(section, mp),
            P(section, None, mp),
            P(section, mp),
            P(section, mp),
            P(section, mp),
            P(section, mp),
            P(section, mp),
            P(),
        ),
        check_vma=False,
    )
```

```python
import math

import jax
import jax.numpy as jnp
import ml_dtypes
import numpy as np
from jax import lax
from jax.experimental import pallas as pl
from jax.experimental.pallas import tpu as pltpu
from jax.sharding import Mesh
from jax.sharding import PartitionSpec as P

EPSILON = 1e-05
BF = jnp.bfloat16
F32 = jnp.float32
MIB = 1 << 20
AXES = ("section", "half", "rest", "side", "core")
RING = ("section", "rest", "side", "core")
PLANE = ("half", "side", "core")
SQUARE = ("section", "half", "side", "core")
VMEM = pl.BlockSpec(memory_space=pltpu.VMEM)
HBM = pl.BlockSpec(memory_space=pltpu.HBM)
SMEM = pl.BlockSpec(memory_space=pltpu.SMEM)


def trig(rows, columns, points):
    phases = (rows.astype(np.int64)[:, None] * columns.astype(np.int64)[None, :]) % points
    angles = phases.astype(np.float64) * (2.0 * math.pi / points)
    return np.cos(angles), np.sin(angles)


def low_table(table):
    return table.astype(np.float32).astype(ml_dtypes.bfloat16)


def feature_tables(width, group):
    pairs = width // group // 2
    ids = np.arange(width // 2)
    cos, sin = trig(ids, np.arange(width), width)
    sin[0] = trig(np.array([width // 2]), np.arange(width), width)[0][0]
    packed = np.stack([cos.reshape(group, pairs, width), sin.reshape(group, pairs, width)], 1)
    unpack = np.zeros((width, width), np.float32)
    for k in range(width // 2):
        place = (k // pairs) * 2 * pairs + k % pairs
        if k == 0:
            unpack[0, place] = 1.0
            unpack[width // 2, place + pairs] = 1.0
        else:
            unpack[k, place] = 1.0
            unpack[k, place + pairs] = -1.0
            unpack[width - k, place] = 1.0
            unpack[width - k, place + pairs] = 1.0
    return low_table(packed.reshape(width, width)), low_table(unpack)


def token_tables(sections, rests, mps, part):
    parity, rest, place, i = np.meshgrid(
        np.arange(sections), np.arange(rests), np.arange(mps), np.arange(part), indexing="ij"
    )
    first = rest * sections * mps * part + sections * (place * part + i) + parity
    length = 2 * first.size
    every = np.stack([first, first + length // 2], 3).reshape(-1)
    cos, sin = trig(every, first.reshape(-1), length)
    return low_table(cos), low_table(sin)


def sorting_table(sections, count):
    table = np.zeros((count, count), np.float32)
    order = np.arange(count).reshape(-1, sections).T.reshape(-1)
    table[order, np.arange(count)] = 1.0
    return low_table(table)


def mm(left, right):
    return jnp.dot(left, right, preferred_element_type=F32)


def mm_nt(left, right):
    return lax.dot_general(left, right, (((1,), (1,)), ((), ())), preferred_element_type=F32)


def blocks(size, step):
    step = step if size % step == 0 else size
    return [(i, i + step) for i in range(0, size, step)]


def shape(dims, dtype=BF):
    return jax.ShapeDtypeStruct(tuple(dims), dtype)


def call(kernel, outs, args, specs=None, scratch=(), limit=52, flops=0, **extra):
    return pl.pallas_call(
        kernel,
        out_shape=outs,
        in_specs=specs or [VMEM] * len(args),
        scratch_shapes=list(scratch),
        compiler_params=pltpu.CompilerParams(vmem_limit_bytes=limit * MIB),
        cost_estimate=pl.CostEstimate(flops=flops, bytes_accessed=6 << 20, transcendentals=0),
        **extra,
    )(*args)


def paired(first, second):
    left = lax.broadcasted_iota(jnp.int32, first.shape, 1) < 64
    return (
        jnp.where(left, first, pltpu.roll(second, 64, axis=1)),
        jnp.where(left, pltpu.roll(first, 64, axis=1), second),
    )


def send_pencils(locals_, section, sections, halves, mps, sorting):
    batches, features, tokens = locals_[0].shape
    count, part, rows = batches // halves, tokens // sections // mps, features // 2
    kinds = len(locals_)
    out = shape((halves * mps, kinds * count * rows, 2 * part))
    if part != 64 or mps % 2:
        own = jnp.stack(locals_).reshape(kinds, halves, count, 2, rows, mps, part, sections)
        own = lax.dynamic_index_in_dim(own, section, 7, keepdims=False)
        return own.transpose(1, 5, 0, 2, 4, 3, 6).reshape(out.shape)
    sorting = sorting.reshape(tokens, sections, tokens // sections).transpose(1, 0, 2)

    def kernel(section_ref, *refs):
        x_refs, sorting_ref, o_ref = refs[:kinds], refs[kinds], refs[kinds + 1]
        for kind in range(kinds):
            for seq in range(batches):
                half, m = seq // count, seq % count
                values = mm(x_refs[kind][seq], sorting_ref[0])
                for place in range(0, mps, 2):
                    a = place * part
                    pair = paired(values[:rows, a : a + 128], values[rows:, a : a + 128])
                    for k in range(2):
                        d, at = half * mps + place + k, (kind * count + m) * rows
                        o_ref[d, at : at + rows] = pair[k].astype(BF)

    return pl.pallas_call(
        kernel,
        grid_spec=pltpu.PrefetchScalarGridSpec(
            num_scalar_prefetch=1,
            grid=(1,),
            in_specs=[pl.BlockSpec(locals_[0].shape, lambda i, s: (0, 0, 0))] * kinds
            + [pl.BlockSpec((1,) + sorting.shape[1:], lambda i, s: (s[0], 0, 0))],
            out_specs=pl.BlockSpec(out.shape, lambda i, s: (0, 0, 0)),
        ),
        out_shape=out,
        compiler_params=pltpu.CompilerParams(vmem_limit_bytes=52 * MIB),
    )(section.reshape(1), *locals_, sorting)


def take_pencils(got, kind, kinds, halves, mps, count, packed=None):
    rows, part = got.shape[1] // count // kinds, got.shape[2] // 2
    width, columns = mps * 2 * rows, count * halves * part
    if part != 64:
        got = got.reshape(halves, mps, kinds, count, rows, 2, part)[:, :, kind]
        low = got.transpose(1, 4, 3, 2, 0, 5).reshape(width, columns)
        return low, None if packed is None else mm(packed, low).astype(BF)

    def kernel(*refs):
        x_ref, o_ref = refs[0], refs[1 if packed is None else 2]
        for mp in range(mps):
            for m in range(count):
                at = (kind * count + m) * rows
                pair = paired(*(x_ref[h * mps + mp, at : at + rows].astype(F32) for h in range(2)))
                for k in range(2):
                    a = (mp * 2 + k) * rows
                    o_ref[a : a + rows, m * 128 : (m + 1) * 128] = pair[k].astype(BF)
        if packed is not None:
            refs[3][...] = mm(refs[1][...], o_ref[...]).astype(BF)

    low = shape((width, columns))
    if packed is None:
        return call(kernel, low, (got,)), None
    return call(kernel, (low, low), (got, packed))


def send_blocks(layers, extra, halves, mps, count, part):
    width, columns = layers[0].shape
    rows, kinds = width // mps // 2, len(layers)
    more = extra.shape[1]
    out = shape((kinds * halves * mps, count * rows + more, 2 * part))
    if part != 64:
        sent = jnp.stack(layers).reshape(kinds, mps, 2, rows, count, halves, part)
        sent = sent.transpose(0, 5, 1, 4, 3, 2, 6).reshape(-1, count * rows, 2 * part)
        return jnp.concatenate([sent, extra], axis=1)

    def kernel(*refs):
        o_ref = refs[-1]
        o_ref[:, count * rows :] = refs[kinds][...]
        for layer in range(kinds):
            for mp in range(mps):
                for m in range(count):
                    a, b = mp * 2 * rows, m * 128
                    pair = paired(
                        refs[layer][a : a + rows, b : b + 128].astype(F32),
                        refs[layer][a + rows : a + 2 * rows, b : b + 128].astype(F32),
                    )
                    for k in range(2):
                        d = (layer * halves + k) * mps + mp
                        o_ref[d, m * rows : (m + 1) * rows] = pair[k].astype(BF)

    return call(kernel, out, (*layers, extra))


def take_blocks(got, places, flipped, rows, halves, mps, count, unsorting):
    part = got[0].shape[-1] // 2
    out = (1, halves * count, 2 * rows, 2 * mps * part)
    got = [array.reshape(-1, halves, mps, array.shape[-2], 2 * part) for array in got]
    if part != 64 or mps % 2:
        both = jnp.stack([array[place, :, :, : count * rows] for array, place in zip(got, places)])
        both = jnp.where(flipped == 1, both[::-1], both)
        both = both.reshape(2, halves, mps, count, rows, 2, part)
        return both.transpose(1, 3, 5, 4, 2, 6, 0).reshape(out).astype(F32)
    tables = unsorting.reshape(2, -1, out[3])
    tables = jnp.stack([unsorting, tables[::-1].reshape(unsorting.shape)])

    def kernel(flag_ref, a_ref, b_ref, table_ref, o_ref, s_ref):
        for x, x_ref in enumerate((a_ref, b_ref)):
            for place in range(0, mps, 2):
                a = x * mps * part + place * part
                for m in range(count):
                    pair = paired(
                        *(
                            x_ref[0, 0, place + k, m * rows : (m + 1) * rows].astype(F32)
                            for k in range(2)
                        )
                    )
                    for k in range(2):
                        s_ref[(2 * m + k) * rows : (2 * m + k + 1) * rows, a : a + 128] = pair[
                            k
                        ].astype(BF)
        for m in range(count):
            o_ref[0, m] = mm(s_ref[2 * m * rows : 2 * (m + 1) * rows], table_ref[0])

    def block(place):
        return pl.BlockSpec((1, 1) + got[0].shape[2:], lambda i, s: (place, i, 0, 0, 0))

    return pl.pallas_call(
        kernel,
        grid_spec=pltpu.PrefetchScalarGridSpec(
            num_scalar_prefetch=1,
            grid=(halves,),
            in_specs=[
                block(places[0]),
                block(places[1]),
                pl.BlockSpec((1,) + unsorting.shape, lambda i, s: (s[0], 0, 0)),
            ],
            out_specs=pl.BlockSpec((1, count) + out[2:], lambda i, s: (i, 0, 0, 0)),
            scratch_shapes=[pltpu.VMEM((count * 2 * rows, out[3]), BF)],
        ),
        out_shape=shape((halves, count) + out[2:], F32),
        compiler_params=pltpu.CompilerParams(vmem_limit_bytes=52 * MIB),
    )(flipped, *got, tables).reshape(out)


def token_transform(data, mask, cos, sin, count):
    group, rows, columns = data.shape
    length, spread = cos.shape
    tokens = columns // count
    part = tokens // 2
    if part != 64:
        x = data.reshape(group, rows, count, tokens).transpose(2, 1, 0, 3)
        x = x.reshape(count * rows, length)
        mixed = [
            jnp.where(mask > 0.0, mm(x[:, a:b], cos[a:b]), mm(x[:, a:b], sin[a:b]))
            for a, b in ((0, spread), (spread, length))
        ]
        both = jnp.stack([mixed[0] + mixed[1], mixed[0] - mixed[1]]).astype(BF)
        both = both.reshape(2, count, rows, group, part).transpose(3, 2, 1, 0, 4)
        return both.reshape(data.shape)
    step = 256

    def kernel(d_ref, m_ref, c_hbm, s_hbm, o_ref, x_ref, c_ref, s_ref, sems):
        copies = []
        for n in range(spread // step):
            window = slice(n * step, (n + 1) * step)
            copies.append(
                [
                    pltpu.make_async_copy(src.at[:, window], dst.at[n], sems.at[n, k])
                    for k, (src, dst) in enumerate(((c_hbm, c_ref), (s_hbm, s_ref)))
                ]
            )
            for copy in copies[-1]:
                copy.start()
        for m in range(count):
            for g in range(group):
                x_ref[m * rows : (m + 1) * rows, g * tokens : (g + 1) * tokens] = d_ref[
                    g, :, m * tokens : (m + 1) * tokens
                ]
        keep = m_ref[...] > 0.0
        for n in range(spread // step):
            for copy in copies[n]:
                copy.wait()
            even, odd = (
                jnp.where(
                    keep,
                    mm(x_ref[:, a : a + spread], c_ref[n, a : a + spread]),
                    mm(x_ref[:, a : a + spread], s_ref[n, a : a + spread]),
                )
                for a in (0, spread)
            )
            total, other = even + odd, even - odd
            for p in range(step // 128):
                pair = paired(total[:, p * 128 : (p + 1) * 128], other[:, p * 128 : (p + 1) * 128])
                for k in range(2):
                    g = n * (step // part) + 2 * p + k
                    low = pair[k].astype(BF)
                    for m in range(count):
                        o_ref[g, :, m * tokens : (m + 1) * tokens] = low[m * rows : (m + 1) * rows]

    return call(
        kernel,
        shape(data.shape),
        (data, mask, cos, sin),
        [VMEM, VMEM, HBM, HBM],
        [pltpu.VMEM((count * rows, length), BF)]
        + [pltpu.VMEM((spread // step, length, step), BF)] * 2
        + [pltpu.SemaphoreType.DMA((spread // step, 2))],
        limit=52,
        flops=4 * count * rows * length * spread,
    )


def standardize(values):
    average = jnp.mean(values, axis=0, keepdims=True)
    centered = values - average
    spread = jnp.mean(centered * centered, axis=0, keepdims=True)
    inverse = lax.rsqrt(spread + EPSILON)
    return centered * inverse, inverse


def norm_back(upstream, standard, inverse, scaling):
    weighted = upstream * scaling
    return inverse * (
        weighted
        - jnp.mean(weighted, axis=0, keepdims=True)
        - standard * jnp.mean(weighted * standard, axis=0, keepdims=True)
    )


def column(table, layer, i):
    k = layer * 5 + i
    return table[:, k : k + 1]


def first_norm(got, low, unpack, factor, table, layer):
    width, columns = low.shape

    def kernel(r_ref, x_ref, unpack_ref, table_ref, unit_ref, inverse_ref, low_ref):
        mixed = mm(unpack_ref[...], r_ref[...])
        table = table_ref[...].T
        gain, shift = column(table, layer, 1), column(table, layer, 2)
        for a, b in blocks(columns, 128):
            unit, inverse = standardize(x_ref[:, a:b].astype(F32) + mixed[:, a:b] * factor)
            unit_ref[:, a:b] = unit.astype(BF)
            inverse_ref[:, a:b] = inverse
            low_ref[:, a:b] = (unit * gain + shift).astype(BF)

    outs = (shape((width, columns)), shape((1, columns), F32), shape((width, columns)))
    return call(kernel, outs, (got, low, unpack, table), flops=2 * width * width * columns)


def second_norm(unit1, parts, table, layer, labels, scored, packed):
    width, columns = unit1.shape
    count = len(parts)

    def kernel(*refs):
        unit1_ref, part_refs = refs[0], refs[1 : 1 + count]
        table_ref, labels_ref, scored_ref = refs[1 + count : 4 + count]
        vectors = table_ref[...].T
        bias, gain1, shift1, gain2, shift2 = (column(vectors, layer, i) for i in range(5))
        bias = bias + shift1
        unit_ref, inverse_ref, low_ref, hits_ref = refs[len(refs) - outs_count :][:4]
        for a, b in blocks(columns, 128):
            values = unit1_ref[:, a:b].astype(F32) * gain1 + bias
            for part in part_refs:
                values = values + part[:, a:b].astype(F32)
            unit, inverse = standardize(values)
            unit_ref[:, a:b] = unit.astype(BF)
            inverse_ref[:, a:b] = inverse
            out = unit * gain2 + shift2
            low_ref[:, a:b] = out.astype(BF)
            exponent = jnp.exp(out)
            match = lax.broadcasted_iota(jnp.int32, out.shape, 0) == labels_ref[:, a:b]
            picked = jnp.sum(jnp.where(match, exponent, 0.0), axis=0, keepdims=True)
            total = jnp.sum(exponent, axis=0, keepdims=True)
            hits_ref[:, a:b] = picked / total * scored_ref[:, a:b]
        if packed is not None:
            refs[-1][...] = mm(refs[4 + count][...], low_ref[...]).astype(BF)

    row = shape((1, columns), F32)
    outs = [shape((width, columns)), row, shape((width, columns)), row]
    args = [unit1, *parts, table, labels, scored]
    if packed is not None:
        outs, args = outs + [shape((width, columns))], args + [packed]
    outs_count = len(outs)
    return call(kernel, tuple(outs), tuple(args), flops=2 * width * width * columns)


def row_sums(terms, width):
    total = jnp.zeros((8, width), F32)
    for row, term in terms:
        mark = (lax.broadcasted_iota(jnp.int32, (8, term.shape[1]), 0) == row).astype(BF)
        total = total + mm_nt(mark, term)
    return total


def second_back(up, unit, inverse, table, layer, mix=None):
    width, columns = unit.shape

    def kernel(*refs):
        up_ref, unit_ref, inverse_ref, table_ref = refs[:4]
        if mix is None:
            low_ref, sums_ref, product_ref = refs[4:]
            source_ref = up_ref
        else:
            got_ref, unpack_ref, low_ref, sums_ref, source_ref, product_ref = refs[4:]
            mixed = mm(unpack_ref[...], got_ref[...])
        gain = column(table_ref[...].T, layer, 3)
        for a, b in blocks(columns, 128):
            if mix is not None:
                values = up_ref[:, a:b].astype(F32) + mixed[:, a:b] * mix[2]
                source_ref[:, a:b] = values.astype(BF)
            values, unit = source_ref[:, a:b].astype(F32), unit_ref[:, a:b].astype(F32)
            low_ref[:, a:b] = norm_back(values, unit, inverse_ref[:, a:b], gain).astype(BF)
            product_ref[:, a:b] = (values * unit).astype(BF)
        sums_ref[...] = row_sums(
            ((0, low_ref[...]), (3, product_ref[...]), (4, source_ref[...])), width
        )

    outs = (shape(unit.shape), shape((8, width), F32))
    args = (up, unit, inverse, table)
    if mix is not None:
        outs, args = outs + (shape(unit.shape),), args + mix[:2]
    scratch = [pltpu.VMEM(unit.shape, BF)]
    return call(kernel, outs, args, None, scratch, flops=2 * width * width * columns)


def first_back(grad_second, parts, unit, inverse, table, layer, packed):
    width, columns = unit.shape
    count = len(parts)

    def kernel(second_ref, *refs):
        part_refs = refs[:count]
        unit_ref, inverse_ref, table_ref, packed_ref = refs[count : count + 4]
        low_ref, sums_ref, sent_ref, product_ref, normed_ref = refs[count + 4 :]
        gain = column(table_ref[...].T, layer, 1)
        for a, b in blocks(columns, 128):
            values, unit = second_ref[:, a:b].astype(F32), unit_ref[:, a:b].astype(F32)
            for part in part_refs:
                values = values + part[:, a:b].astype(F32)
            low_ref[:, a:b] = norm_back(values, unit, inverse_ref[:, a:b], gain).astype(BF)
            product_ref[:, a:b] = (values * unit).astype(BF)
            normed_ref[:, a:b] = values.astype(BF)
        sent_ref[...] = mm(packed_ref[...], low_ref[...]).astype(BF)
        sums_ref[...] = row_sums(((1, product_ref[...]), (2, normed_ref[...])), width)

    outs = (shape(unit.shape), shape((8, width), F32), shape(unit.shape))
    args = (grad_second, *parts, unit, inverse, table, packed)
    scratch = [pltpu.VMEM(unit.shape, BF)] * 2
    return call(kernel, outs, args, None, scratch, flops=2 * width * width * columns)


def last_mix(got, grad, unpack, factor):
    width, columns = grad.shape

    def kernel(got_ref, grad_ref, unpack_ref, o_ref):
        mixed = mm(unpack_ref[...], got_ref[...])
        o_ref[...] = (grad_ref[...].astype(F32) + mixed * factor).astype(BF)

    args = (got, grad, unpack)
    return call(kernel, shape(grad.shape), args, flops=2 * width * width * columns)


def gelu_parts(x):
    cdf = 0.5 + 0.5 * lax.erf(x * (1.0 / math.sqrt(2.0)))
    return cdf, jnp.exp(-0.5 * x * x) * (1.0 / math.sqrt(2.0 * math.pi))


def mm_tn(left, right):
    return lax.dot_general(left, right, (((0,), (0,)), ((), ())), preferred_element_type=F32)


def staged(pairs, sems):
    copies = [
        pltpu.make_async_copy(src, dst, sems.at[i]) for i, (src, dst) in enumerate(pairs)
    ]
    for copy in copies:
        copy.start()
    return copies


def chosen(flag, pairs, sems):
    copies = []
    for i, (sources, target) in enumerate(pairs):
        either = [pltpu.make_async_copy(src, target, sems.at[i]) for src in sources]

        @pl.when(flag == 1)
        def _():
            either[0].start()

        @pl.when(flag != 1)
        def _():
            either[1].start()

        copies.append(either[0])
    return copies


def ffn(flag, first, second, own, other, biases, layer):
    width, columns = first.shape
    units = own[0].shape[0]
    steps = blocks(units, 256)

    def kernel(flag_ref, a_ref, b_ref, own1, own2, other1, other2, bias_ref, *refs):
        oa_ref, ob_ref, act_hbm, slope_hbm, one_ref, two_ref, act_ref, slope_ref, sems, sent = refs
        copies = chosen(
            flag_ref[0],
            [((own1.at[a:b], other1.at[a:b]), one_ref.at[a:b]) for a, b in steps]
            + [((own2, other2), two_ref)],
            sems,
        )
        x = jnp.concatenate([a_ref[...], b_ref[...]], axis=1)
        bias = bias_ref[...].T
        writes = []
        for i, (a, b) in enumerate(steps):
            copies[i].wait()
            hidden = mm(one_ref[a:b], x) + bias[a:b, layer : layer + 1]
            cdf, density = gelu_parts(hidden)
            act_ref[a:b] = (hidden * cdf).astype(BF)
            slope_ref[a:b] = (cdf + hidden * density).astype(BF)
            for k, (src, dst) in enumerate(((act_ref, act_hbm), (slope_ref, slope_hbm))):
                writes.append(pltpu.make_async_copy(src.at[a:b], dst.at[a:b], sent.at[i, k]))
                writes[-1].start()
        copies[-1].wait()
        for a, b in blocks(width, 256):
            part = mm(two_ref[a:b], act_ref[...])
            oa_ref[a:b] = part[:, :columns].astype(BF)
            ob_ref[a:b] = part[:, columns:].astype(BF)
        for write in writes:
            write.wait()

    half, full = shape((width, columns)), shape((units, 2 * columns))
    return call(
        kernel,
        (half, half, full, full),
        (flag, first, second, *own, *other, biases),
        [SMEM] + [VMEM] * 2 + [HBM] * 4 + [VMEM],
        [
            pltpu.VMEM((units, width), BF),
            pltpu.VMEM((width, units), BF),
            pltpu.VMEM(full.shape, BF),
            pltpu.VMEM(full.shape, BF),
            pltpu.SemaphoreType.DMA((len(steps) + 1,)),
            pltpu.SemaphoreType.DMA((len(steps), 2)),
        ],
        limit=52,
        flops=8 * width * units * columns,
        out_specs=(VMEM, VMEM, HBM, HBM),
    )


def ffn_back(flag, first, second, own, other, slope):
    width, columns = first.shape
    units = own[0].shape[0]
    steps = blocks(units, 256)

    def kernel(flag_ref, a_ref, b_ref, own1, own2, other1, other2, slope_hbm, *refs):
        oa_ref, ob_ref, pre_hbm, sums_ref, one_ref, two_ref, pre_ref, slope_ref, sems, sent = refs
        copies = chosen(
            flag_ref[0],
            [((own2, other2), two_ref)]
            + [((slope_hbm.at[a:b],) * 2, slope_ref.at[a:b]) for a, b in steps]
            + [((own1, other1), one_ref)],
            sems,
        )
        g = jnp.concatenate([a_ref[...], b_ref[...]], axis=1)
        copies[0].wait()
        writes = []
        for i, (a, b) in enumerate(steps):
            grad = mm_tn(two_ref[:, a:b], g)
            copies[1 + i].wait()
            pre_ref[a:b] = (grad * slope_ref[a:b].astype(F32)).astype(BF)
            writes.append(pltpu.make_async_copy(pre_ref.at[a:b], pre_hbm.at[a:b], sent.at[i]))
            writes[-1].start()
        copies[-1].wait()
        for a, b in blocks(width, 256):
            part = mm_tn(one_ref[:, a:b], pre_ref[...])
            oa_ref[a:b] = part[:, :columns].astype(BF)
            ob_ref[a:b] = part[:, columns:].astype(BF)
        sums_ref[...] = row_sums(((0, pre_ref[...]),), units)
        for write in writes:
            write.wait()

    half, full = shape((width, columns)), shape((units, 2 * columns))
    return call(
        kernel,
        (half, half, full, shape((8, units), F32)),
        (flag, first, second, *own, *other, slope),
        [SMEM] + [VMEM] * 2 + [HBM] * 5,
        [
            pltpu.VMEM((units, width), BF),
            pltpu.VMEM((width, units), BF),
            pltpu.VMEM(full.shape, BF),
            pltpu.VMEM(full.shape, BF),
            pltpu.SemaphoreType.DMA((len(steps) + 2,)),
            pltpu.SemaphoreType.DMA((len(steps),)),
        ],
        limit=52,
        flops=8 * width * units * columns,
        out_specs=(VMEM, VMEM, HBM, VMEM),
    )


def weight_grad(flag, lefts, rights):
    rows, width = lefts[0][0].shape[0], rights[0][0].shape[0]
    sizes = [[array.shape[1] for array in either] for either in (lefts[1], rights[1])]
    tokens = sum(sizes[0])
    parts = [(side, either) for side in range(2) for either in range(2)]
    lists = {(side, either): (lefts, rights)[side][either] for side, either in parts}

    def kernel(flag_ref, *refs):
        inputs, (out_ref, left_ref, right_ref, sems) = refs[:-4], refs[-4:]
        at, groups = 0, {}
        for part in parts:
            groups[part] = inputs[at : at + len(lists[part])]
            at += len(lists[part])
        wholes = (left_ref, right_ref)

        def fill(either, act):
            k = 0
            for side in range(2):
                place = 0
                for src in groups[side, either]:
                    step = src.shape[1]
                    target = wholes[side].at[:, place : place + step]
                    act(pltpu.make_async_copy(src, target, sems.at[either, k]))
                    place, k = place + step, k + 1

        for act in (lambda copy: copy.start(), lambda copy: copy.wait()):
            for either in range(2):

                @pl.when((flag_ref[0] == 1) == (either == 0))
                def _():
                    fill(either, act)

        for a, b in blocks(rows, 256):
            out_ref[a:b] = mm_nt(left_ref[a:b], right_ref[...]).astype(BF)

    count = max(len(lists[0, e]) + len(lists[1, e]) for e in range(2))
    args = [array for part in parts for array in lists[part]]
    return call(
        kernel,
        shape((rows, width)),
        (flag, *args),
        [SMEM] + [HBM] * len(args),
        [
            pltpu.VMEM((rows, tokens), BF),
            pltpu.VMEM((width, tokens), BF),
            pltpu.SemaphoreType.DMA((2, count)),
        ],
        limit=52,
        flops=2 * width * rows * tokens,
    )


def weight_grads(flag, xs, pres, gs, acts):
    units, width = pres[0].shape[0], xs[0].shape[0]
    if units != width:
        pre, x, g, act = (jnp.concatenate(group, axis=1) for group in (pres, xs, gs, acts))
        one, two = mm_nt(pre, x).astype(BF), mm_nt(g, act).astype(BF).reshape(units, width)
        return jnp.where(flag == 1, one, two), jnp.where(flag == 1, two, one)
    give = weight_grad(flag, (gs, pres), (acts, xs))
    keep = weight_grad(flag, (pres, gs), (xs, acts))
    return keep, give


def widened(gathered):
    planes, _, rows, width = gathered.shape

    def kernel(x_hbm, one_hbm, two_hbm, in_ref, out_ref, sems, sent):
        order = [(p, k) for k in range(2) for p in range(planes)]
        copies = [
            pltpu.make_async_copy(x_hbm.at[p, k], in_ref.at[p, k], sems.at[p, k]) for p, k in order
        ]
        for copy in copies:
            copy.start()
        writes = []
        for copy, (p, k) in zip(copies, order):
            copy.wait()
            out_ref[p, k] = in_ref[p, k].astype(F32)
            target = (one_hbm, two_hbm)[k].at[p * rows : (p + 1) * rows]
            writes.append(pltpu.make_async_copy(out_ref.at[p, k], target, sent.at[p, k]))
            writes[-1].start()
        for write in writes:
            write.wait()

    return call(
        kernel,
        (shape((planes * rows, width), F32),) * 2,
        (gathered,),
        [HBM],
        [
            pltpu.VMEM(gathered.shape, BF),
            pltpu.VMEM(gathered.shape, F32),
            pltpu.SemaphoreType.DMA((planes, 2)),
            pltpu.SemaphoreType.DMA((planes, 2)),
        ],
        out_specs=(HBM, HBM),
    )


def shards(
    inputs,
    cotangent,
    labels,
    scored,
    expand_weight,
    expand_bias,
    reduce_weight,
    reduce_bias,
    first_gain,
    first_shift,
    second_gain,
    second_shift,
):
    batches, feature_count, token_count = inputs.shape
    sections, halves, rests, sides, cores = (lax.axis_size(axis) for axis in AXES)
    mps = sides * cores
    group = sections * rests * mps
    width = feature_count * mps
    length = token_count * halves * rests
    units = expand_weight.shape[1]
    count = batches // halves
    part = token_count // sections // mps
    columns = count * halves * part
    rows = width // group
    factor = 1.0 / math.sqrt(length * width)
    section, half, rest, side, core = (lax.axis_index(axis) for axis in AXES)
    mp_index = side * cores + core
    is_first = section == 0

    packed, unpack = (jnp.asarray(t) for t in feature_tables(width, group))
    token_cos, token_sin = (jnp.asarray(t) for t in token_tables(sections, rests, mps, part))
    sorting = sorting_table(sections, token_count)
    unsorting, sorting = jnp.asarray(sorting.T), jnp.asarray(sorting)
    row_ids = jnp.arange(count * rows, dtype=jnp.int32) % rows
    corner = (section == 0) & (rest == 0) & (mp_index == 0)
    mask = (row_ids < rows // 2) | ((row_ids == rows // 2) & corner)
    mask = mask.astype(F32)[:, None]

    def swapped(array, axis, by=1):
        size = lax.axis_size(axis)
        return lax.ppermute(array, axis, [(i, (i + by) % size) for i in range(size)])

    own_one, own_two = expand_weight[0], reduce_weight[0]
    other_one, other_two = swapped(own_one, "section"), swapped(own_two, "section")

    def ordered(own, other):
        return [jnp.where(is_first, own, other), jnp.where(is_first, other, own)]

    small = [expand_bias, reduce_bias, first_gain, first_shift, second_gain, second_shift]
    small = jnp.concatenate([vector[0] for vector in small])
    small = jnp.stack(ordered(small, swapped(small, "section")))
    biases = jnp.pad(small[:, :units], ((0, 8 - sections), (0, 0)))
    vectors = small[:, units:].reshape(sections * 5, 1, feature_count)
    vectors = jnp.concatenate(ordered_by(core, vectors, swapped(vectors, "core")), axis=1)
    chips = [swapped(vectors, "side", -j) if j else vectors for j in range(sides)]
    chips = jnp.stack(chips, axis=1)
    order = [(i - side) % sides for i in range(sides)]
    table = jnp.stack(
        [lax.dynamic_index_in_dim(chips, i, 1, keepdims=False) for i in order], axis=1
    ).reshape(sections * 5, width)
    table = jnp.pad(table, ((0, -table.shape[0] % 16), (0, 0)))

    lanes = 2 * part

    def small_rows(layer, hits):
        high = hits.astype(BF)
        middle = (hits - high.astype(F32)).astype(BF)
        lowest = (hits - high.astype(F32) - middle.astype(F32)).astype(BF)
        counted = jnp.broadcast_to(jnp.stack([high, middle, lowest])[None], (mps, 3))
        of_features = smalls[layer][:5].reshape(5, mps, feature_count).transpose(1, 0, 2)
        mine = jnp.arange(mps, dtype=jnp.int32)[:, None] == mp_index
        bias = jnp.where(mine, bias_rows[layer][None], 0.0)
        extra = jnp.concatenate(
            [of_features.reshape(mps, -1).astype(BF), bias.astype(BF), counted], axis=1
        )
        extra = jnp.pad(extra, ((0, 0), (0, -extra.shape[1] % (8 * lanes))))
        extra = jnp.broadcast_to(extra[None], (halves,) + extra.shape)
        return extra.reshape(halves * mps, -1, lanes)

    def small_sums(got, extra):
        most = got.shape[1] - extra.shape[1]
        return jnp.sum(got[:, most:].astype(F32), axis=0).reshape(-1)

    def fourier(sent, *others):
        sent = sent.reshape(group, rows, columns)
        got = lax.all_to_all(sent, RING, 0, 0, tiled=True)
        mixed = token_transform(got, mask, token_cos, token_sin, count)
        if others:
            mixed, others = lax.optimization_barrier((mixed, others))
        mixed = lax.all_to_all(mixed, RING, 0, 0, tiled=True).reshape(width, columns)
        return (mixed, *others) if others else mixed

    def gathered(own):
        return [own] + [swapped(own, "side", j) for j in range(1, sides)]

    def reduced(parts):
        terms = [parts[0][0], swapped(parts[0][1], "core")]
        for j in range(1, sides):
            keep, give = parts[j]
            chip = keep.astype(F32) + swapped(give, "core").astype(F32)
            terms.append(swapped(chip.astype(BF), "side", -j))
        return terms

    def added(first, second):
        return (first.astype(F32) + second.astype(F32)).astype(BF)

    def scattered(array):
        return lax.psum_scatter(array, ("half", "rest"), scatter_dimension=0, tiled=True)

    def in_turn(step, firsts):
        done, pairs = [], []
        for i, first in enumerate(firsts):
            if done:
                first, done[-1] = lax.optimization_barrier((first, done[-1]))
            pairs.append((first, swapped(first, "core")))
            done.append(step(*pairs[-1], i))
        return done, pairs

    marks = 2 * labels + scored
    marks = jnp.stack(ordered_by(half, marks, swapped(marks, "half")))
    marks = lax.dynamic_slice_in_dim(marks, half * count, count, 1)
    marks = marks.reshape(halves, count, mps, part, sections)
    marks = lax.dynamic_index_in_dim(marks, section, 4, keepdims=False)
    marks = lax.dynamic_index_in_dim(marks, mp_index, 2, keepdims=False)
    marks = marks.transpose(1, 0, 2).reshape(1, columns)
    local_labels, local_scored = marks // 2, (marks % 2).astype(F32)

    got = send_pencils((inputs, cotangent), section, sections, halves, mps, sorting)
    got = lax.all_to_all(got, PLANE, 0, 0, tiled=True)
    low, sent = take_pencils(got, 0, 2, halves, mps, count, packed)
    up, _ = lax.optimization_barrier((got, sent))
    flags = [is_first.astype(jnp.int32).reshape(1), (1 - is_first.astype(jnp.int32)).reshape(1)]
    saved, outs, hits = [], [], jnp.zeros((), F32)
    for layer in range(2):
        if layer == 0:
            mixed, other_one, other_two, table, biases = fourier(
                sent, other_one, other_two, table, biases
            )
        else:
            mixed = fourier(sent)
        unit1, inv1, normed = first_norm(mixed, low, unpack, factor, table, layer)
        runs, xs = in_turn(
            lambda a, b, i: ffn(
                flags[layer], a, b, (own_one, own_two), (other_one, other_two), biases, layer
            ),
            gathered(normed),
        )
        terms = reduced([run[:2] for run in runs])
        if layer == 0:
            up, _ = take_pencils(up, 1, 2, halves, mps, count)
            terms, up = lax.optimization_barrier((terms, up))
        result = second_norm(
            unit1,
            terms,
            table,
            layer,
            local_labels,
            local_scored,
            packed if layer == 0 else None,
        )
        unit2, inv2, low, hit = result[:4]
        sent = result[-1]
        outs.append(low)
        hits = hits + jnp.sum(hit)
        saved.append((unit1, inv1, xs, runs, unit2, inv2))
    nothing = jnp.zeros((sections * halves * mps, 16, lanes), BF)
    outputs = send_blocks(outs, nothing, halves, mps, count, part)
    outputs = lax.all_to_all(outputs, SQUARE, 0, 0, tiled=True)

    grads_in, weights_out, smalls, bias_rows = [None, None], [None, None], [None, None], [None, None]
    mix = None
    for layer in (1, 0):
        unit1, inv1, xs, runs, unit2, inv2 = saved[layer]
        result = second_back(up, unit2, inv2, table, layer, mix)
        grad_low, sums2 = result[:2]
        if mix is not None:
            grads_in[1] = result[2]
        backs, gs = in_turn(
            lambda a, b, i: ffn_back(
                flags[layer], a, b, (own_one, own_two), (other_one, other_two), runs[i][3]
            ),
            gathered(grad_low),
        )
        if layer == 0:
            late, _ = lax.optimization_barrier((late, backs[-1][0]))
            weights_out[1] = scattered(added(*late))
        terms = reduced([back[:2] for back in backs])
        keep, give = weight_grads(
            flags[0],
            [x for pair in xs for x in pair],
            [back[2] for back in backs],
            [g for pair in gs for g in pair],
            [run[2] for run in runs],
        )
        terms, keep, give = lax.optimization_barrier((terms, keep, give))
        if layer == 1:
            terms, outputs = lax.optimization_barrier((terms, outputs))
        up, sums1, sent = first_back(grad_low, terms, unit1, inv1, table, layer, packed)
        if layer == 1:
            mixed = fourier(sent)
            give, _ = lax.optimization_barrier((give, mixed))
            late = (keep, swapped(give, "section"))
        else:
            extra = small_rows(1, hits)
            got_late, _ = lax.optimization_barrier((grads_in[1], sent))
            got_late = send_blocks([got_late], extra, halves, mps, count, part)
            got_late = lax.all_to_all(got_late, PLANE, 0, 0, tiled=True)
            both, weights_out[1] = lax.optimization_barrier(
                (added(keep, swapped(give, "section")), weights_out[1])
            )
            weights_out[0] = scattered(both)
            sent, got_late, _ = lax.optimization_barrier((sent, got_late, both))
            mixed = fourier(sent)
            rows_of = feature_count // 2
            outputs = take_blocks(
                (outputs, outputs), (0, 1), 0 * flags[0], rows_of, halves, mps, count, unsorting
            )
            mixed, outputs = lax.optimization_barrier((mixed, outputs))
        mix = (mixed, unpack, factor)
        smalls[layer] = sums1 + sums2
        bias_rows[layer] = sum(back[3][0] for back in backs)
    grads_in[0] = last_mix(mix[0], up, unpack, factor)

    extra = small_rows(0, hits)
    sent = send_blocks(grads_in[:1], extra, halves, mps, count, part)
    got = lax.all_to_all(sent, PLANE, 0, 0, tiled=True)
    mine, other = jnp.where(is_first, got, got_late), jnp.where(is_first, got_late, got)
    other = swapped(other, "section")
    rows_of = feature_count // 2
    input_grads = take_blocks(
        (mine, other), (0, 0), flags[1], rows_of, halves, mps, count, unsorting
    )
    small, step = (small_sums(mine, extra) + small_sums(other, extra)).reshape(-1, lanes), 1
    while step < rests:
        small = small + lax.ppermute(small, "rest", [(i, i ^ step) for i in range(rests)])
        step *= 2
    small, per = small.reshape(-1), 5 * feature_count
    features = small[:per].reshape(5, feature_count)
    bias_sum = small[per : per + units]
    accuracy = jnp.sum(small[per + units : per + units + 3])

    early, late = weights_out
    early, late, _ = lax.optimization_barrier((early, late, sent))
    mine, other = jnp.where(is_first, early, late), jnp.where(is_first, late, early)
    other = swapped(other, "section")
    pair = jnp.stack(ordered(mine, other))
    pair = lax.all_gather(pair, ("half", "rest"), axis=0, tiled=False)
    one, two = widened(pair.reshape((-1,) + pair.shape[-3:]))
    weight_sums = [one, two.reshape(width, units)]

    return (
        outputs,
        input_grads,
        weight_sums[0][None],
        bias_sum[None],
        weight_sums[1][None],
        features[0][None],
        features[1][None],
        features[2][None],
        features[3][None],
        features[4][None],
        accuracy,
    )


def ordered_by(index, own, other):
    return [jnp.where(index == 0, own, other), jnp.where(index == 0, other, own)]


def solution(mesh):
    sizes = mesh.shape
    dims = (sizes["section"], 2, sizes["seq"] // 2, sizes["mp"] // 2, 2)
    names = ("section", ("half", "rest"), ("side", "core"))
    section, seq, mp = names
    placed = (
        P(None, mp, seq),
        P(None, mp, seq),
        P(None, seq),
        P(None, seq),
        P(section, mp, None),
        P(section, mp),
        P(section, None, mp),
        P(section, mp),
        P(section, mp),
        P(section, mp),
        P(section, mp),
        P(section, mp),
    )
    return jax.shard_map(
        shards,
        mesh=Mesh(mesh.devices.reshape(dims), AXES),
        in_specs=placed,
        out_specs=(
            P(section, None, mp, seq),
            P(section, None, mp, seq),
            P(section, mp, None),
            P(section, mp),
            P(section, None, mp),
            P(section, mp),
            P(section, mp),
            P(section, mp),
            P(section, mp),
            P(section, mp),
            P(),
        ),
        check_vma=False,
    )
```
